32 devices in a mesh: dp: 4 (over z), label: 8 (over y, x, core).
Axes of the slice: x: 2, y: 2, z: 4, core: 2. Of those that a mesh axis runs over, the one named last changes fastest.
Arguments:
- enc: bfloat16 [32768, 768], P(('dp', 'label')), may hold values from -6 to 6
- proj: bfloat16 [768, 768], replicated, may hold values from -0.21875 to 0.21875
- head_weight: bfloat16 [1024, 768], P('label'), may hold values from -0.21875 to 0.21875
- shortlist: int32 [256, 4], P(('dp', 'label')), may hold values from 0 to 7, all different within a row; in each aligned block of 8 rows (0 to 7, 8 to 15, ...) at most 8 rows name the same one
- positives: int32 [32768, 8], P(('dp', 'label')), may hold values from 0 to 511
- weight_num: int32 [1024], P('label'), may hold values from 1 to 16
- weight_den: int32 [1024], P('label'), may hold values from 1 to 16
Outputs:
- grad_enc: float32 [32768, 768], P(('dp', 'label'))
- grad_proj: float32 [768, 768], replicated
- grad_head: float32 [1024, 768], P('label', 'dp')
The draws below stay inside these ranges and needn't reach their ends.
Inputs may be any that keep to these rules, and one draw needn't show every extreme that they name: `shortlist`: each row names 4 different clusters; among the rows of one device no cluster is named by more than 8 rows, and in every draw some cluster is named by exactly 8 rows of some device; every cluster is named somewhere.
All inputs are finite; a program needn't handle non-finite values.
Results may differ from the reference program's by a relative error of at most 0.005.
Values may be sent and summed in bfloat16 or wider, within the bound.
No kernel may reach another device: no remote copies, remote signals or barrier semaphores. Data moves between devices by JAX's collectives and lax.ppermute only.
A program may use at most 128 MiB of HBM per device.

```python
import math
import jax
import jax.numpy as jnp
import numpy as np
from jax import lax

D = 768
LB = 128
SB = 128
BEAM = 4
POS = 8
BLK_DEV = 8
CAP = 8
CLUSTERS = 8
LABELS = 1024
BLOCKS = 256
SAMPLES = 32768


def touch_ends(values, key, low, high):
    spot = [jax.random.randint(jax.random.fold_in(key, axis), (), 0, length) for axis, length in enumerate(values.shape)]
    main_axis = values.shape.index(max(values.shape))
    neighbour = spot[:main_axis] + [(spot[main_axis] + 1) % values.shape[main_axis]] + spot[main_axis + 1:]
    return values.at[tuple(spot)].set(low).at[tuple(neighbour)].set(high)


def steps_of(stream_key, shape, shards, low, top_value):
    level, own = 1.0, jax.random.fold_in(stream_key, 6)
    for axis_at, blocks in shards:
        heights = jnp.exp(jax.random.uniform(jax.random.fold_in(own, axis_at), (blocks,), jnp.float32, low / len(shards), top_value / len(shards)))
        level = level * jnp.repeat(heights, shape[axis_at] // blocks).reshape([-1 if axis == axis_at else 1 for axis in range(len(shape))])
    return level


def shared_out(stream_key, own, number, rows, count, top, bound, lean):
    ranking = jax.random.permutation(stream_key, count)
    heavy_load, usual = shares(count, rows * top, bound, lean, True), shares(count, rows * top, bound, lean, False)
    places = jnp.arange(count)

    def named(tallies, rotation):
        used = int((tallies > 0).sum())
        fixed = max(1, used // 4)
        moved = fixed + (places - fixed + rotation * (used - fixed)) % max(1, count - fixed)
        return jnp.zeros((count,), jnp.int32).at[ranking[jnp.where(places < fixed, places, moved)]].set(jnp.asarray(tallies, jnp.int32))

    tallies = jnp.where(number % 4 == 0, named(heavy_load, number // 4), named(usual, number - number // 4 - 1))
    mixed = jax.random.permutation(jax.random.fold_in(own, 3), count)
    giver, taker = mixed[0:count // 2 * 2:2], mixed[1:count // 2 * 2:2]
    slack = jnp.minimum(tallies[giver] - 1, bound - tallies[taker]) // 2
    slack = jnp.where((giver == ranking[0]) | (taker == ranking[0]) | (tallies[taker] == 0), 0, jnp.maximum(slack, 0))
    moved = jax.random.randint(jax.random.fold_in(own, 4), (count // 2,), 0, 1 << 20) % (slack + 1)
    tallies = tallies.at[giver].add(-moved).at[taker].add(moved)
    items = jnp.searchsorted(jnp.cumsum(tallies), jnp.arange(rows * top), side="right").astype(jnp.int32)
    table = items.reshape(top, rows).T
    table = table[jax.random.permutation(jax.random.fold_in(own, 1), rows)]
    rotation = jax.random.randint(jax.random.fold_in(own, 2), (rows, 1), 0, top)
    return jnp.take_along_axis(table, (jnp.arange(top)[None, :] + rotation) % top, axis=1)


def shares(number_of, total, most, skew, full):
    weights = [(1 << 20) // math.isqrt(rank ** skew) + 1 for rank in range(1, number_of + 1)]
    largest = most if full else min(most, max(-(-total // number_of), total * weights[0] // sum(weights)))
    least = 1 if total - largest >= number_of - 1 else 0
    given, surplus = [largest] + [least] * (number_of - 1), total - largest - least * (number_of - 1)
    while surplus > 0:
        movable = [i for i in range(1, number_of) if given[i] < largest] or [i for i in range(1, number_of) if given[i] < most]
        pool, budget = sum([weights[i] for i in movable]), surplus
        for i in movable:
            more = min(most - given[i], max(1, budget * weights[i] // pool), surplus)
            given[i] = given[i] + more
            surplus = surplus - more
    return np.array(given)


def scatter_about(rng, shape, deviation, most, cuts=(), kind=jnp.bfloat16):
    values = jax.random.normal(rng, shape, jnp.float32) * deviation
    if len(cuts) > 0:
        values = steps_of(rng, shape, cuts, -0.22, 0.18) * values
    return jnp.clip(values, min=-most, max=most).astype(kind)


def setup_inputs(seed: int = 0) -> dict:
    key_of = jax.random.split(jax.random.key(seed), 8)
    enc = scatter_about(key_of[0], (SAMPLES, D), 1.0, 6.0, ((0, 32),))
    proj = scatter_about(key_of[1], (D, D), D ** -0.5, 0.21875)
    head_weight = scatter_about(key_of[2], (LABELS, D), D ** -0.5, 0.21875, ((0, 8),))
    shortlist_keys = jax.random.split(jax.random.fold_in(key_of[3], 1), BLOCKS // BLK_DEV)
    shortlist_turns = jax.random.permutation(jax.random.fold_in(key_of[3], 3), BLOCKS // BLK_DEV)
    shortlist = jax.vmap(lambda own, number: shared_out(jax.random.fold_in(key_of[3], 2), own, number, BLK_DEV, CLUSTERS, BEAM, CAP, 2))(shortlist_keys, shortlist_turns).reshape((BLOCKS, BEAM))
    positives = touch_ends(jax.random.randint(key_of[4], (SAMPLES, POS), 0, BEAM * LB), jax.random.fold_in(key_of[4], 1), 0, (BEAM * LB) - 1).astype(jnp.int32)
    weight_num = touch_ends(jax.random.randint(key_of[5], (LABELS,), 1, 17), jax.random.fold_in(key_of[5], 1), 1, 16).astype(jnp.int32)
    weight_den = touch_ends(jax.random.randint(key_of[6], (LABELS,), 1, 17), jax.random.fold_in(key_of[6], 1), 1, 16).astype(jnp.int32)
    return dict(enc=enc, proj=proj, head_weight=head_weight, shortlist=shortlist, positives=positives, weight_num=weight_num, weight_den=weight_den)


def contract(left, right, left_dim, right_dim):
    return lax.dot_general(left, right, (((left_dim,), (right_dim,)), ((), ())), preferred_element_type=jnp.float32)


def reference(enc, proj, head_weight, shortlist, positives, weight_num, weight_den):
    label_weight = weight_num.astype(jnp.float32) / weight_den.astype(jnp.float32)
    label_iota = jnp.arange(LB, dtype=jnp.int32)
    enc_blocks = enc.reshape(BLOCKS, SB, D)
    pos_blocks = positives.reshape(BLOCKS, SB, POS)

    def one_block(carried, inputs):
        grad_head, grad_proj = carried
        block_rows, picked, wanted = inputs
        hidden = jnp.dot(block_rows, proj, preferred_element_type=jnp.float32).astype(jnp.bfloat16)
        grad_hidden = jnp.zeros((SB, D), jnp.float32)
        for beam_slot in range(BEAM):
            row_start = (picked[beam_slot] * LB).astype(jnp.int32)
            cluster_rows = lax.dynamic_slice_in_dim(head_weight, row_start, LB, 0)
            cluster_scale = lax.dynamic_slice_in_dim(label_weight, row_start, LB, 0)
            logits = contract(hidden, cluster_rows, 1, 1)
            shifted = wanted - beam_slot * LB
            target = jnp.zeros((SB, LB), jnp.bool_)
            for column in range(POS):
                target = target | (shifted[:, column, None] == label_iota[None, :])
            grad_logits = (cluster_scale[None, :] * (jax.nn.sigmoid(logits) - target.astype(jnp.float32)) / SB).astype(jnp.bfloat16)
            grad_part = jnp.dot(grad_logits, cluster_rows, preferred_element_type=jnp.float32).astype(jnp.bfloat16)
            grad_part = lax.optimization_barrier(grad_part)
            grad_hidden = grad_hidden + grad_part.astype(jnp.float32)
            update = contract(grad_logits, hidden, 0, 0)
            current = lax.dynamic_slice_in_dim(grad_head, row_start, LB, 0)
            grad_head = lax.dynamic_update_slice_in_dim(grad_head, current + update, row_start, 0)
        grad_hidden = grad_hidden.astype(jnp.bfloat16)
        grad_rows = contract(grad_hidden, proj, 1, 1)
        grad_proj = grad_proj + contract(block_rows, grad_hidden, 0, 0)
        return (grad_head, grad_proj), grad_rows

    start_carry = (jnp.zeros((LABELS, D), jnp.float32), jnp.zeros((D, D), jnp.float32))
    (grad_head, grad_proj), grad_rows = lax.scan(one_block, start_carry, (enc_blocks, shortlist, pos_blocks))
    return grad_rows.reshape(SAMPLES, D), grad_proj, grad_head
```

```python
import functools

import jax
import jax.numpy as jnp
from jax import lax
from jax.experimental import pallas as pl
from jax.experimental.pallas import tpu as pltpu
from jax.sharding import PartitionSpec as P

BF16 = jnp.bfloat16
F32 = jnp.float32
VMEM = pl.BlockSpec(memory_space=pltpu.VMEM)
SMEM = pl.BlockSpec(memory_space=pltpu.SMEM)
TAIL = 16
NN = (((1,), (0,)), ((), ()))
NT = (((1,), (1,)), ((), ()))
TN = (((0,), (0,)), ((), ()))


def dot(left, right, dims):
    return lax.dot_general(left, right, dims, preferred_element_type=F32)


def swap(value, axis, distance):
    size = lax.axis_size(axis)
    return lax.ppermute(value, axis, [(i, i ^ distance) for i in range(size)])


def call(kernel, outs, args, scalars=(), scratch=(), flops=0, nbytes=0):
    return pl.pallas_call(
        kernel,
        out_shape=outs,
        in_specs=[SMEM] * len(scalars) + [VMEM] * len(args),
        out_specs=[VMEM] * len(outs),
        scratch_shapes=list(scratch),
        compiler_params=pltpu.CompilerParams(vmem_limit_bytes=40 * 1024 * 1024),
        cost_estimate=pl.CostEstimate(flops=flops, bytes_accessed=nbytes, transcendentals=0),
    )(*scalars, *args)


def slot_of(relative, owners):
    return (relative >> 1) + (relative & 1) * (owners // 2)


def score_kernel(owners, beam, block, size, slots_ref, hidden_ref, wanted_ref, enc_t_ref, *refs):
    payloads, refs = refs[:owners], refs[owners:]
    grads_ref, weights_ref, refs = refs[0], refs[1], refs[2:]
    sent = refs[: owners // 2]
    scale_ref, logits_ref = refs[owners // 2 :]
    samples = hidden_ref.shape[0]
    for relative in range(owners):
        slot = slot_of(relative, owners)
        rows = pl.ds(slot * size, size)
        weights_ref[rows, :] = payloads[relative][:size, :]
        tail = payloads[relative][size : size + TAIL, :size].astype(F32)
        ratio = tail[0:1, :] / tail[1:2, :]
        scale_ref[rows, :] = jnp.broadcast_to(ratio, (block, size)).T / block
    grads_ref[...] = jnp.zeros_like(grads_ref)
    label_iota = lax.broadcasted_iota(jnp.int32, (size, block), 0)
    tile = min(2 * block, samples)
    for start in range(0, samples, tile):
        logits_ref[...] = dot(weights_ref[...], hidden_ref[start : start + tile, :], NT)
        for low in range(start, start + tile, block):
            for beam_slot in range(beam):
                slot = slots_ref[(low // block) * beam + beam_slot]
                rows = pl.ds(pl.multiple_of(slot * size, size), size)
                logits = logits_ref[rows, low - start : low - start + block]
                labels = label_iota + beam_slot * size
                target = labels == wanted_ref[0:1, low : low + block]
                for column in range(1, wanted_ref.shape[0]):
                    target = target | (labels == wanted_ref[column : column + 1, low : low + block])
                share = jax.nn.sigmoid(logits) - jnp.where(target, 1.0, 0.0)
                grads_ref[rows, low : low + block] = (scale_ref[rows, :] * share).astype(BF16)
    half = owners // 2 * size
    outer = dot(enc_t_ref[...], grads_ref[half:, :], NT)
    for j in range(owners // 2):
        sent[j][...] = outer[:, j * size : (j + 1) * size].astype(BF16)


def keep_kernel(owners, size, enc_t_ref, grads_ref, *kept):
    outer = dot(enc_t_ref[...], grads_ref[: owners // 2 * size, :], NT)
    for j in range(owners // 2):
        kept[j][...] = outer[:, j * size : (j + 1) * size]


def enc_kernel(grads_ref, weights_ref, proj_ref, out_ref):
    grad_hidden = dot(grads_ref[...], weights_ref[...], TN).astype(BF16)
    out_ref[...] = dot(grad_hidden, proj_ref[...], NT)


def plane_kernel(planes, z_ref, own_ref, *refs):
    recv, refs = refs[: len(refs) - planes - 1], refs[len(refs) - planes - 1 :]
    kept, sent, total_ref = refs[0], refs[1:planes], refs[planes]
    total = own_ref[...]
    for ref in recv:
        total = total + ref[...].astype(F32)
    total_ref[...] = total
    depth = kept.shape[0]
    z = z_ref[0]
    kept[...] = total_ref[pl.ds(pl.multiple_of(z * depth, depth), depth), :]
    for q in range(1, planes):
        start = pl.multiple_of((z ^ q) * depth, depth)
        sent[q - 1][...] = total_ref[pl.ds(start, depth), :].astype(BF16)


def head_kernel(planes, z_ref, *refs):
    parts, refs = refs[:planes], refs[planes:]
    proj_ref, whole_ref, out_ref = refs
    depth = parts[0].shape[0]
    z = z_ref[0]
    for q in range(planes):
        start = pl.multiple_of((z ^ q) * depth, depth)
        whole_ref[pl.ds(start, depth), :] = parts[q][...]
    out_ref[...] = dot(whole_ref[...], proj_ref[...], TN)


def proj_kernel(owners, size, me_ref, *refs):
    parts, refs = refs[:owners], refs[owners:]
    weights_ref, out_ref, outer_ref, rows_ref = refs
    me = me_ref[0]
    for relative in range(owners):
        start = pl.multiple_of((me ^ relative) * size, size)
        slot = slot_of(relative, owners)
        outer_ref[:, pl.ds(start, size)] = parts[relative][...]
        rows_ref[pl.ds(start, size), :] = weights_ref[slot * size : (slot + 1) * size, :]
    out_ref[...] = dot(outer_ref[...], rows_ref[...], NN)


def shards(enc, proj, head_weight, shortlist, positives, weight_num, weight_den):
    owners, planes = lax.axis_size("label"), lax.axis_size("dp")
    me, z = lax.axis_index("label"), lax.axis_index("dp")
    me_s = jnp.reshape(me, (1,)).astype(jnp.int32)
    z_s = jnp.reshape(z, (1,)).astype(jnp.int32)
    blocks, beam = shortlist.shape
    samples, width = enc.shape
    block = samples // blocks
    size = head_weight.shape[0]
    labels = owners * size
    chips = range(2, owners, 2)

    tail = jnp.zeros((TAIL, width), BF16)
    tail = tail.at[0, :size].set(weight_num.astype(BF16)).at[1, :size].set(weight_den.astype(BF16))
    payload = jnp.concatenate([head_weight, tail], axis=0)
    got = {0: payload, 1: swap(payload, "label", 1)}
    for relative in chips:
        got[relative] = swap(payload, "label", relative)
    for relative in chips:
        got[relative + 1] = swap(got[relative], "label", 1)

    hidden = dot(enc, proj, NN).astype(BF16)
    enc_t = enc.T
    wanted = positives.T
    slots = slot_of(jnp.bitwise_xor(shortlist, me), owners).astype(jnp.int32).reshape(-1)

    piece = jax.ShapeDtypeStruct((width, size), BF16)
    piece_f32 = jax.ShapeDtypeStruct((width, size), F32)
    grads, weights, *sent = call(
        functools.partial(score_kernel, owners, beam, block, size),
        [jax.ShapeDtypeStruct((labels, samples), BF16), jax.ShapeDtypeStruct((labels, width), BF16)]
        + [piece] * (owners // 2),
        [hidden, wanted, enc_t] + [got[relative] for relative in range(owners)],
        scalars=[slots],
        scratch=[pltpu.VMEM((labels, block), F32), pltpu.VMEM((labels, min(2 * block, samples)), F32)],
        flops=4 * samples * labels * width,
        nbytes=12_000_000,
    )
    from_core = [swap(value, "label", 1) for value in sent]
    kept = call(
        functools.partial(keep_kernel, owners, size),
        [piece_f32] * (owners // 2),
        [enc_t, grads],
        flops=samples * labels * width,
        nbytes=4_000_000,
    )
    grad_enc = pl.pallas_call(
        enc_kernel,
        grid=(max(1, samples // 256),),
        out_shape=jax.ShapeDtypeStruct((samples, width), F32),
        in_specs=[
            pl.BlockSpec((labels, min(256, samples)), lambda i: (0, i)),
            pl.BlockSpec((labels, width), lambda i: (0, 0)),
            pl.BlockSpec((width, width), lambda i: (0, 0)),
        ],
        out_specs=pl.BlockSpec((min(256, samples), width), lambda i: (i, 0)),
        compiler_params=pltpu.CompilerParams(vmem_limit_bytes=40 * 1024 * 1024),
        cost_estimate=pl.CostEstimate(
            flops=2 * samples * width * (labels + width), bytes_accessed=9_000_000, transcendentals=0
        ),
    )(grads, weights, proj)

    pairs = [a + b.astype(F32) for a, b in zip(kept, from_core)]
    from_chips = [swap(pairs[p // 2].astype(BF16), "label", p) for p in chips]
    depth = width // planes
    part = jax.ShapeDtypeStruct((depth, size), BF16)
    own, *sent = call(
        functools.partial(plane_kernel, planes),
        [jax.ShapeDtypeStruct((depth, size), F32)] + [part] * (planes - 1),
        [pairs[0]] + from_chips,
        scalars=[z_s],
        scratch=[pltpu.VMEM((width, size), F32)],
        nbytes=2_000_000,
    )
    total = own
    for q in range(1, planes):
        total = total + swap(sent[q - 1], "dp", q).astype(F32)
    total = total.astype(BF16)
    parts = [total] + [swap(total, "dp", q) for q in range(1, planes)]
    proj_slice = lax.dynamic_slice_in_dim(proj, z * depth, depth, 1)
    whole, grad_head = call(
        functools.partial(head_kernel, planes),
        [piece, jax.ShapeDtypeStruct((size, depth), F32)],
        parts + [proj_slice],
        scalars=[z_s],
        flops=2 * size * width * depth,
        nbytes=1_000_000,
    )
    have = {0: whole, 1: swap(whole, "label", 1)}
    for relative in chips:
        have[relative] = swap(whole, "label", relative)
    for relative in chips:
        have[relative + 1] = swap(have[relative], "label", 1)
    (grad_proj,) = call(
        functools.partial(proj_kernel, owners, size),
        [jax.ShapeDtypeStruct((width, width), F32)],
        [have[relative] for relative in range(owners)] + [weights],
        scalars=[me_s],
        scratch=[pltpu.VMEM((width, labels), BF16), pltpu.VMEM((labels, width), BF16)],
        flops=2 * labels * width * width,
        nbytes=6_000_000,
    )
    return (grad_enc, grad_proj, grad_head)


def solution(mesh):
    placed = (
        P(("dp", "label"), None),
        P(),
        P("label", None),
        P(("dp", "label"), None),
        P(("dp", "label"), None),
        P("label"),
        P("label"),
    )
    return jax.shard_map(
        shards,
        mesh=mesh,
        in_specs=placed,
        out_specs=(P(("dp", "label"), None), P(), P("label", "dp")),
        check_vma=False,
    )
```

```python
import functools

import jax
import jax.numpy as jnp
from jax import lax
from jax.experimental import pallas as pl
from jax.experimental.pallas import tpu as pltpu
from jax.sharding import PartitionSpec as P

BF16 = jnp.bfloat16
F32 = jnp.float32
VMEM = pl.BlockSpec(memory_space=pltpu.VMEM)
SMEM = pl.BlockSpec(memory_space=pltpu.SMEM)
TAIL = 16
MIB = 1024 * 1024
NN = (((1,), (0,)), ((), ()))
NT = (((1,), (1,)), ((), ()))
TN = (((0,), (0,)), ((), ()))


def dot(left, right, dims):
    return lax.dot_general(left, right, dims, preferred_element_type=F32)


def shape(dims, dtype):
    return jax.ShapeDtypeStruct(dims, dtype)


def call(kernel, outs, args, scalars=(), scratch=(), vmem=8, flops=0, nbytes=0):
    return pl.pallas_call(
        kernel,
        out_shape=outs,
        in_specs=[SMEM] * len(scalars) + [VMEM] * len(args),
        out_specs=[VMEM] * len(outs),
        scratch_shapes=list(scratch),
        compiler_params=pltpu.CompilerParams(vmem_limit_bytes=vmem * MIB),
        cost_estimate=pl.CostEstimate(flops=flops, bytes_accessed=nbytes, transcendentals=0),
    )(*scalars, *args)


def stage_distance(owner, stage, stages):
    forward, backward = 2 << stage, 2 << (stages - 1 - stage)
    return forward + (owner & 1) * (backward - forward)


def chip_swap(value, stage, stages):
    owners = lax.axis_size("label")
    return lax.ppermute(
        value, "label", [(i, i ^ stage_distance(i, stage, stages)) for i in range(owners)]
    )


def core_swap(value):
    owners = lax.axis_size("label")
    return lax.ppermute(value, "label", [(i, i ^ 1) for i in range(owners)])


def plane_swap(value, distance):
    planes = lax.axis_size("dp")
    return lax.ppermute(value, "dp", [(i, i ^ distance) for i in range(planes)])


def slot_of_cluster(cluster, me, stages):
    offset = cluster ^ me
    side = me ^ (offset & 1)
    chips = sum(
        (jnp.where((offset & stage_distance(side, stage, stages)) != 0, 1, 0) << stage)
        for stage in range(stages)
    )
    return chips + (offset & 1) * (1 << stages)


def cluster_of_slot(slot, me, stages):
    side = me ^ (slot >> stages)
    return side ^ sum(
        ((slot >> stage) & 1) * stage_distance(side, stage, stages) for stage in range(stages)
    )


def payload_kernel(num_ref, den_ref, rows_ref, out_ref):
    size, width = rows_ref.shape
    out_ref[:size, :] = rows_ref[...]
    row = lax.broadcasted_iota(jnp.int32, (TAIL, size), 0)
    both = jnp.where(row == 0, num_ref[...], den_ref[...])
    out_ref[size:, :size] = both.astype(F32).astype(BF16)
    out_ref[size:, size:] = jnp.zeros((TAIL, width - size), BF16)


def score_kernel(owners, beam, block, size, slots_ref, hidden_ref, wanted_ref, enc_t_ref, *refs):
    payloads, refs = refs[:owners], refs[owners:]
    grads_ref, weights_ref, first_ref, second_ref, scale_ref, logits_ref = refs
    samples = hidden_ref.shape[0]
    for slot in range(owners):
        rows = pl.ds(slot * size, size)
        weights_ref[rows, :] = payloads[slot][:size, :]
        tail = payloads[slot][size : size + TAIL, :size].astype(F32)
        ratio = tail[0:1, :] / tail[1:2, :]
        scale_ref[rows, :] = jnp.broadcast_to(ratio, (block, size)).T / block
    grads_ref[...] = jnp.zeros_like(grads_ref)
    label_iota = lax.broadcasted_iota(jnp.int32, (size, block), 0)
    tile = min(2 * block, samples)
    for start in range(0, samples, tile):
        logits_ref[...] = dot(weights_ref[...], hidden_ref[start : start + tile, :], NT)
        for low in range(start, start + tile, block):
            for beam_slot in range(beam):
                slot = slots_ref[(low // block) * beam + beam_slot]
                rows = pl.ds(pl.multiple_of(slot * size, size), size)
                logits = logits_ref[rows, low - start : low - start + block]
                labels = label_iota + beam_slot * size
                target = labels == wanted_ref[0:1, low : low + block]
                for column in range(1, wanted_ref.shape[0]):
                    target = target | (labels == wanted_ref[column : column + 1, low : low + block])
                share = jax.nn.sigmoid(logits) - jnp.where(target, 1.0, 0.0)
                grads_ref[rows, low : low + block] = (scale_ref[rows, :] * share).astype(BF16)
    half = owners // 2
    outer = dot(enc_t_ref[...], grads_ref[half * size :, :], NT)
    for slot in range(half):
        part = outer[:, slot * size : (slot + 1) * size].astype(BF16)
        if slot % 2:
            first_ref[slot // 2] = part
        else:
            second_ref[slot // 2] = part


def keep_kernel(owners, size, enc_t_ref, grads_ref, *kept):
    outer = dot(enc_t_ref[...], grads_ref[: owners // 2 * size, :], NT)
    for slot in range(owners // 2):
        kept[slot][...] = outer[:, slot * size : (slot + 1) * size]


def hidden_kernel(grads_ref, weights_ref, out_ref):
    out_ref[...] = dot(grads_ref[...], weights_ref[...], TN).astype(BF16)


def enc_kernel(grad_hidden_ref, proj_ref, out_ref):
    out_ref[...] = dot(grad_hidden_ref[...], proj_ref[...], NT)


def head_kernel(count, z_ref, *refs):
    parts, (proj_ref, out_ref) = refs[:count], refs[count:]
    depth = parts[0].shape[0]
    total = jnp.zeros(out_ref.shape, F32)
    for r in range(count):
        start = pl.multiple_of((z_ref[0] ^ r) * depth, depth)
        total = total + dot(proj_ref[pl.ds(start, depth), :], parts[r][...], TN)
    out_ref[...] = total


def proj_kernel(owners, size, count, me_ref, z_ref, *refs):
    parts, refs = refs[: owners * count], refs[owners * count :]
    weights_ref, out_ref, outer_ref, rows_ref = refs
    stages = owners.bit_length() - 2
    depth = parts[0].shape[0]
    for slot in range(owners):
        cluster = cluster_of_slot(slot, me_ref[0], stages)
        start = pl.multiple_of(cluster * size, size)
        rows_ref[pl.ds(start, size), :] = weights_ref[slot * size : (slot + 1) * size, :]
        for r in range(count):
            outer_ref[r * depth : (r + 1) * depth, pl.ds(start, size)] = parts[slot * count + r][...]
    for r in range(count):
        start = pl.multiple_of((z_ref[0] ^ r) * depth, depth)
        rows = outer_ref[r * depth : (r + 1) * depth, :]
        out_ref[pl.ds(start, depth), :] = dot(rows, rows_ref[...], NN)


def shards(enc, proj, head_weight, shortlist, positives, weight_num, weight_den):
    owners, planes = lax.axis_size("label"), lax.axis_size("dp")
    stages = owners.bit_length() - 2
    chips = 1 << stages
    row_blocks = max(1, planes // 2)
    me = lax.axis_index("label").astype(jnp.int32)
    z = lax.axis_index("dp").astype(jnp.int32)
    z_low = z & (row_blocks - 1)
    blocks, beam = shortlist.shape
    samples, width = enc.shape
    block = samples // blocks
    size = head_weight.shape[0]
    labels = owners * size
    depth = width // row_blocks
    me_s, z_s = me.reshape(1), z_low.reshape(1)

    (payload,) = call(
        payload_kernel,
        [shape((size + TAIL, width), BF16)],
        [weight_num.reshape(1, size), weight_den.reshape(1, size), head_weight],
        nbytes=400_000,
    )
    got = {0: payload}
    for stage in reversed(range(stages)):
        for slot in list(got):
            got[slot | (1 << stage)] = chip_swap(got[slot], stage, stages)
    hidden = dot(enc, proj, NN).astype(BF16)
    enc_blocks = enc.T.reshape(row_blocks, depth, samples)
    enc_t = jnp.concatenate(
        [lax.dynamic_index_in_dim(enc_blocks, z_low ^ r, 0, False) for r in range(row_blocks)], axis=0
    )
    for slot in range(chips):
        got[slot + chips] = core_swap(got[slot])
    slots = slot_of_cluster(shortlist, me, stages).astype(jnp.int32).reshape(-1)

    group = shape((chips // 2, width, size), BF16)
    grads, weights, send_first, send_second = call(
        functools.partial(score_kernel, owners, beam, block, size),
        [shape((labels, samples), BF16), shape((labels, width), BF16), group, group],
        [hidden, positives.T, enc_t] + [got[slot] for slot in range(owners)],
        scalars=[slots],
        scratch=[pltpu.VMEM((labels, block), F32), pltpu.VMEM((labels, min(2 * block, samples)), F32)],
        vmem=16,
        flops=4 * samples * labels * width,
        nbytes=12_000_000,
    )
    from_core = [core_swap(send_first), core_swap(send_second)]
    kept = call(
        functools.partial(keep_kernel, owners, size),
        [shape((width, size), F32)] * chips,
        [enc_t, grads],
        flops=samples * labels * width,
        nbytes=4_000_000,
    )
    sums = {}
    for slot in sorted(range(chips), key=lambda s: -(s & 1)):
        sums[slot] = kept[slot] + from_core[1 - slot % 2][slot // 2].astype(F32)
    for stage in range(stages):
        bit = 1 << stage
        moving = sorted((s for s in sums if s & bit), key=lambda s: -s)
        for slot in moving:
            if len(moving) > 1 or row_blocks == 1:
                recv = chip_swap(sums[slot].astype(BF16), stage, stages).astype(F32)
            else:
                cut = width // 2
                upper = chip_swap(sums[slot][cut:].astype(BF16), stage, stages)
                lower = chip_swap(sums[slot][:cut].astype(BF16), stage, stages)
                recv = jnp.concatenate([lower, upper], axis=0).astype(F32)
            sums[slot ^ bit] = sums[slot ^ bit] + recv
            del sums[slot]
    total = sums[0]
    (grad_hidden,) = call(
        hidden_kernel,
        [shape((samples, width), BF16)],
        [grads, weights],
        vmem=16,
        flops=2 * samples * width * labels,
        nbytes=5_000_000,
    )
    tile = min(256, samples)
    grad_enc = pl.pallas_call(
        enc_kernel,
        grid=(samples // tile,),
        out_shape=shape((samples, width), F32),
        in_specs=[
            pl.BlockSpec((tile, width), lambda i: (i, 0)),
            pl.BlockSpec((width, width), lambda i: (0, 0)),
        ],
        out_specs=pl.BlockSpec((tile, width), lambda i: (i, 0)),
        compiler_params=pltpu.CompilerParams(vmem_limit_bytes=12 * MIB),
        cost_estimate=pl.CostEstimate(
            flops=2 * samples * width * width, bytes_accessed=6_000_000, transcendentals=0
        ),
    )(grad_hidden, proj)

    span = row_blocks
    while span > 1:
        cut = span // 2 * depth
        total = total[:cut] + plane_swap(total[cut:].astype(BF16), span // 2).astype(F32)
        span //= 2
    total = total.astype(BF16)
    if planes > 1:
        other = plane_swap(total, planes // 2)
        total = (total.astype(F32) + other.astype(F32)).astype(BF16)
    parts = {0: total}
    span = 1
    while span < row_blocks:
        for r in range(span):
            parts[r + span] = plane_swap(parts[r], span)
        span *= 2

    proj_slice = lax.dynamic_slice_in_dim(proj, z * (width // planes), width // planes, 1)
    (grad_head,) = call(
        functools.partial(head_kernel, row_blocks),
        [shape((width // planes, size), F32)],
        [parts[r] for r in range(row_blocks)] + [proj_slice],
        scalars=[z_s],
        flops=2 * size * width * width // planes,
        nbytes=1_000_000,
    )
    have = {(0, r): parts[r] for r in range(row_blocks)}
    for r in range(row_blocks):
        for stage in reversed(range(stages)):
            for slot in [s for s, at in list(have) if at == r]:
                have[slot | (1 << stage), r] = chip_swap(have[slot, r], stage, stages)
        for slot in range(chips):
            have[slot + chips, r] = core_swap(have[slot, r])
    (grad_proj,) = call(
        functools.partial(proj_kernel, owners, size, row_blocks),
        [shape((width, width), F32)],
        [have[slot, r] for slot in range(owners) for r in range(row_blocks)] + [weights],
        scalars=[me_s, z_s],
        scratch=[pltpu.VMEM((width, labels), BF16), pltpu.VMEM((labels, width), BF16)],
        vmem=20,
        flops=2 * labels * width * width,
        nbytes=6_000_000,
    )
    return (grad_enc, grad_proj, grad_head.T)


def solution(mesh):
    placed = (
        P(("dp", "label"), None),
        P(),
        P("label", None),
        P(("dp", "label"), None),
        P(("dp", "label"), None),
        P("label"),
        P("label"),
    )
    return jax.shard_map(
        shards,
        mesh=mesh,
        in_specs=placed,
        out_specs=(P(("dp", "label"), None), P(), P("label", "dp")),
        check_vma=False,
    )
```

```python
import functools

import jax
import jax.numpy as jnp
from jax import lax
from jax.experimental import pallas as pl
from jax.experimental.pallas import tpu as pltpu
from jax.sharding import PartitionSpec as P

BF16 = jnp.bfloat16
F32 = jnp.float32
VMEM = pl.BlockSpec(memory_space=pltpu.VMEM)
SMEM = pl.BlockSpec(memory_space=pltpu.SMEM)
ANY = pl.BlockSpec(memory_space=pl.ANY)
MIB = 1024 * 1024
NN = (((1,), (0,)), ((), ()))
NT = (((1,), (1,)), ((), ()))
TN = (((0,), (0,)), ((), ()))


def dot(left, right, dims):
    return lax.dot_general(left, right, dims, preferred_element_type=F32)


def shape(dims, dtype):
    return jax.ShapeDtypeStruct(dims, dtype)


def call(kernel, outs, args, scalars=(), after=(), scratch=(), vmem=8, flops=0, nbytes=0):
    return pl.pallas_call(
        kernel,
        out_shape=outs,
        in_specs=[SMEM] * len(scalars) + [VMEM] * len(args) + [ANY] * len(after),
        out_specs=[VMEM] * len(outs),
        scratch_shapes=list(scratch),
        compiler_params=pltpu.CompilerParams(vmem_limit_bytes=vmem * MIB),
        cost_estimate=pl.CostEstimate(flops=flops, bytes_accessed=nbytes, transcendentals=0),
    )(*scalars, *args, *after)


def gate(value, after):
    return pl.pallas_call(
        lambda value_ref, after_ref, out_ref: None,
        out_shape=shape(value.shape, value.dtype),
        in_specs=[ANY, ANY],
        out_specs=ANY,
        input_output_aliases={0: 0},
    )(value, after)


def distance_of(slot, chips):
    return 2 * (slot % chips) + slot // chips


def slot_of(cluster, me, chips):
    distance = cluster ^ me
    return (distance >> 1) + (distance & 1) * chips


def swap(value, axis, distance):
    size = lax.axis_size(axis)
    return lax.ppermute(value, axis, [(i, i ^ distance) for i in range(size)])


def inputs_kernel(enc_ref, proj_ref, hidden_ref, enc_t_ref):
    samples = enc_ref.shape[0]
    tile = min(256, samples)
    for start in range(0, samples, tile):
        rows = enc_ref[start : start + tile, :]
        enc_t_ref[:, start : start + tile] = rows.T
        hidden_ref[start : start + tile, :] = dot(rows, proj_ref[...], NN).astype(BF16)


def outer_rows(enc_t_ref, grads, z, count):
    depth = enc_t_ref.shape[0] // count
    for r in range(count):
        start = pl.multiple_of((z ^ r) * depth, depth)
        yield r * depth, depth, dot(enc_t_ref[pl.ds(start, depth), :], grads, NT)


def score_kernel(owners, beam, block, count, slots_ref, me_ref, z_ref, hidden_ref, wanted_ref, enc_t_ref, ratio_ref, *refs):
    pieces, refs = refs[:owners], refs[owners:]
    grads_ref, weights_ref, first_ref, second_ref, scale_ref, logits_ref = refs
    samples = hidden_ref.shape[0]
    size = pieces[0].shape[0]
    chips = owners // 2
    for slot in range(owners):
        rows = pl.ds(slot * size, size)
        weights_ref[rows, :] = pieces[slot][...]
        ratio = ratio_ref[pl.ds(me_ref[0] ^ distance_of(slot, chips), 1), :]
        scale_ref[rows, :] = jnp.broadcast_to(ratio, (block, size)).T / block
    grads_ref[...] = jnp.zeros_like(grads_ref)
    label_iota = lax.broadcasted_iota(jnp.int32, (size, block), 0)
    tile = min(2 * block, samples)
    for start in range(0, samples, tile):
        logits_ref[...] = dot(weights_ref[...], hidden_ref[start : start + tile, :], NT)
        for low in range(start, start + tile, block):
            for beam_slot in range(beam):
                slot = slots_ref[(low // block) * beam + beam_slot]
                rows = pl.ds(pl.multiple_of(slot * size, size), size)
                logits = logits_ref[rows, low - start : low - start + block]
                labels = label_iota + beam_slot * size
                target = labels == wanted_ref[0:1, low : low + block]
                for column in range(1, wanted_ref.shape[0]):
                    target = target | (labels == wanted_ref[column : column + 1, low : low + block])
                share = jax.nn.sigmoid(logits) - jnp.where(target, 1.0, 0.0)
                grads_ref[rows, low : low + block] = (scale_ref[rows, :] * share).astype(BF16)
    for low, depth, outer in outer_rows(enc_t_ref, grads_ref[chips * size :, :], z_ref[0], count):
        for slot in range(chips):
            part = outer[:, slot * size : (slot + 1) * size].astype(BF16)
            out_ref = first_ref if slot % 2 else second_ref
            out_ref[slot // 2, low : low + depth, :] = part


def keep_kernel(count, z_ref, enc_t_ref, grads_ref, *kept):
    size = kept[0].shape[1]
    for low, depth, outer in outer_rows(enc_t_ref, grads_ref[: len(kept) * size, :], z_ref[0], count):
        for slot, ref in enumerate(kept):
            ref[low : low + depth, :] = outer[:, slot * size : (slot + 1) * size]


def hidden_kernel(owners, me_ref, grads_ref, weights_ref, after_ref, out_ref, rows_ref):
    size = weights_ref.shape[0] // owners
    for slot in range(owners):
        start = pl.multiple_of((me_ref[0] ^ distance_of(slot, owners // 2)) * size, size)
        rows_ref[pl.ds(start, size), :] = weights_ref[slot * size : (slot + 1) * size, :]
    out_ref[...] = dot(grads_ref[...], weights_ref[...], TN).astype(BF16)


def enc_kernel(grad_hidden_ref, proj_ref, out_ref, done_ref):
    out_ref[...] = dot(grad_hidden_ref[...], proj_ref[...], NT)
    done_ref[...] = jnp.zeros_like(done_ref)


def combine_kernel(own_ref, *refs):
    *received, after_ref, kept_ref, sent_ref = refs
    cut = kept_ref.shape[0]
    for rows, out_ref in ((slice(cut, None), sent_ref), (slice(0, cut), kept_ref)):
        total = own_ref[rows, :]
        for ref in received:
            total = total + ref[rows, :].astype(F32)
        out_ref[...] = total.astype(out_ref.dtype)


def proj_kernel(owners, count, me_ref, z_ref, *refs):
    parts, refs = refs[: owners * count], refs[owners * count :]
    rows_ref, slice_ref, out_ref, head_ref, outer_ref = refs
    depth, size = parts[0].shape
    for slot in range(owners):
        start = pl.multiple_of((me_ref[0] ^ distance_of(slot, owners // 2)) * size, size)
        for r in range(count):
            outer_ref[r * depth : (r + 1) * depth, pl.ds(start, size)] = parts[slot * count + r][...]
    head = jnp.zeros(head_ref.shape, F32)
    for r in range(count):
        start = pl.multiple_of((z_ref[0] ^ r) * depth, depth)
        rows = outer_ref[r * depth : (r + 1) * depth, :]
        out_ref[pl.ds(start, depth), :] = dot(rows, rows_ref[...], NN)
        head = head + dot(slice_ref[pl.ds(start, depth), :], parts[r][...], TN)
    head_ref[...] = head


def shards(enc, proj, head_weight, shortlist, positives, weight_num, weight_den):
    owners, planes = lax.axis_size("label"), lax.axis_size("dp")
    chips = owners // 2
    row_blocks = max(1, planes // 2)
    me = lax.axis_index("label").astype(jnp.int32)
    z = lax.axis_index("dp").astype(jnp.int32)
    z_low = z & (row_blocks - 1)
    blocks, beam = shortlist.shape
    samples, width = enc.shape
    block = samples // blocks
    size = head_weight.shape[0]
    labels = owners * size
    depth = width // row_blocks
    me_s, z_s = me.reshape(1), z_low.reshape(1)

    got = {0: head_weight}
    for slot in range(1, chips):
        got[slot] = swap(head_weight, "label", distance_of(slot, chips))
    ratio = weight_num.astype(F32) / weight_den.astype(F32)
    ratio = lax.all_gather(ratio, "label", axis=0, tiled=True).reshape(owners, size)
    hidden, enc_t = call(
        inputs_kernel,
        [shape((samples, width), BF16), shape((width, samples), BF16)],
        [enc, proj],
        flops=2 * samples * width * width,
        nbytes=6_000_000,
    )
    for slot in range(1, chips):
        got[slot] = gate(got[slot], hidden)
    for slot in range(chips):
        got[slot + chips] = swap(got[slot], "label", 1)
    slots = slot_of(shortlist, me, chips).astype(jnp.int32).reshape(-1)

    group = shape((chips // 2, width, size), BF16)
    grads, weights, send_first, send_second = call(
        functools.partial(score_kernel, owners, beam, block, row_blocks),
        [shape((labels, samples), BF16), shape((labels, width), BF16), group, group],
        [hidden, positives.T, enc_t, ratio] + [got[slot] for slot in range(owners)],
        scalars=[slots, me_s, z_s],
        scratch=[pltpu.VMEM((labels, block), F32), pltpu.VMEM((labels, min(2 * block, samples)), F32)],
        vmem=16,
        flops=4 * samples * labels * width,
        nbytes=12_000_000,
    )
    from_core = [swap(send_first, "label", 1), swap(send_second, "label", 1)]
    kept = call(
        functools.partial(keep_kernel, row_blocks),
        [shape((width, size), F32)] * chips,
        [enc_t, grads],
        scalars=[z_s],
        flops=samples * labels * width,
        nbytes=4_000_000,
    )
    received, moved = [], None
    for slot in sorted(range(1, chips), key=lambda s: (-(s & 1), -s)):
        moved = (kept[slot] + from_core[1 - slot % 2][slot // 2].astype(F32)).astype(BF16)
        received.append(swap(moved, "label", distance_of(slot, chips)))
    own = kept[0] + from_core[1][0].astype(F32)
    grad_hidden, rows = call(
        functools.partial(hidden_kernel, owners),
        [shape((samples, width), BF16), shape((labels, width), BF16)],
        [grads, weights],
        scalars=[me_s],
        after=[moved],
        vmem=16,
        flops=2 * samples * width * labels,
        nbytes=5_000_000,
    )
    tile = min(256, samples)
    grad_enc, enc_done = pl.pallas_call(
        enc_kernel,
        grid=(samples // tile,),
        out_shape=[shape((samples, width), F32), shape((8, 128), F32)],
        in_specs=[
            pl.BlockSpec((tile, width), lambda i: (i, 0)),
            pl.BlockSpec((width, width), lambda i: (0, 0)),
        ],
        out_specs=[
            pl.BlockSpec((tile, width), lambda i: (i, 0)),
            pl.BlockSpec((8, 128), lambda i: (0, 0)),
        ],
        compiler_params=pltpu.CompilerParams(vmem_limit_bytes=12 * MIB),
        cost_estimate=pl.CostEstimate(
            flops=2 * samples * width * width, bytes_accessed=6_000_000, transcendentals=0
        ),
    )(grad_hidden, proj)

    if row_blocks > 1:
        cut = width // 2
        total, upper = call(
            combine_kernel,
            [shape((cut, size), F32), shape((cut, size), BF16)],
            [own] + received,
            after=[enc_done],
            nbytes=2_000_000,
        )
        span = row_blocks // 2
        total = total + swap(upper, "dp", span).astype(F32)
        while span > 1:
            cut = span // 2 * depth
            total = total[:cut] + swap(total[cut:].astype(BF16), "dp", span // 2).astype(F32)
            span //= 2
    else:
        total = own
        for value in received:
            total = total + value.astype(F32)
    total = total.astype(BF16)
    if planes > 1:
        other = swap(total, "dp", planes // 2)
        total = (total.astype(F32) + other.astype(F32)).astype(BF16)
    parts = {0: total}
    span = 1
    while span < row_blocks:
        for r in range(span):
            parts[r + span] = swap(parts[r], "dp", span)
        span *= 2
    have = {(0, r): parts[r] for r in range(row_blocks)}
    for r in range(row_blocks):
        for slot in range(1, chips):
            have[slot, r] = swap(parts[r], "label", distance_of(slot, chips))
        for slot in range(chips):
            have[slot + chips, r] = swap(have[slot, r], "label", 1)
    proj_slice = lax.dynamic_slice_in_dim(proj, z * (width // planes), width // planes, 1)
    grad_proj, grad_head = call(
        functools.partial(proj_kernel, owners, row_blocks),
        [shape((width, width), F32), shape((width // planes, size), F32)],
        [have[slot, r] for slot in range(owners) for r in range(row_blocks)] + [rows, proj_slice],
        scalars=[me_s, z_s],
        scratch=[pltpu.VMEM((width, labels), BF16)],
        vmem=16,
        flops=2 * labels * width * width,
        nbytes=6_000_000,
    )
    return (grad_enc, grad_proj, grad_head.T)


def solution(mesh):
    placed = (
        P(("dp", "label"), None),
        P(),
        P("label", None),
        P(("dp", "label"), None),
        P(("dp", "label"), None),
        P("label"),
        P("label"),
    )
    return jax.shard_map(
        shards,
        mesh=mesh,
        in_specs=placed,
        out_specs=(P(("dp", "label"), None), P(), P("label", "dp")),
        check_vma=False,
    )
```

```python
import functools

import jax
import jax.numpy as jnp
from jax import lax
from jax.experimental import pallas as pl
from jax.experimental.pallas import tpu as pltpu
from jax.sharding import PartitionSpec as P

BF16 = jnp.bfloat16
F32 = jnp.float32
VMEM = pl.BlockSpec(memory_space=pltpu.VMEM)
SMEM = pl.BlockSpec(memory_space=pltpu.SMEM)
ANY = pl.BlockSpec(memory_space=pl.ANY)
MIB = 1024 * 1024
TAIL = 16
NN = (((1,), (0,)), ((), ()))
NT = (((1,), (1,)), ((), ()))
TN = (((0,), (0,)), ((), ()))


def dot(left, right, dims):
    return lax.dot_general(left, right, dims, preferred_element_type=F32)


def shape(dims, dtype):
    return jax.ShapeDtypeStruct(dims, dtype)


def call(kernel, outs, args, scalars=(), after=(), scratch=(), vmem=8, flops=0, nbytes=0):
    return pl.pallas_call(
        kernel,
        out_shape=outs,
        in_specs=[SMEM] * len(scalars) + [VMEM] * len(args) + [ANY] * len(after),
        out_specs=[VMEM] * len(outs),
        scratch_shapes=list(scratch),
        compiler_params=pltpu.CompilerParams(vmem_limit_bytes=vmem * MIB),
        cost_estimate=pl.CostEstimate(flops=flops, bytes_accessed=nbytes, transcendentals=0),
    )(*scalars, *args, *after)


def gate(value, *after):
    return pl.pallas_call(
        lambda value_ref, *refs: None,
        out_shape=shape(value.shape, value.dtype),
        in_specs=[ANY] * (1 + len(after)),
        out_specs=ANY,
        input_output_aliases={0: 0},
        compiler_params=pltpu.CompilerParams(vmem_limit_bytes=MIB),
    )(value, *after)


def swap(value, axis, distance):
    size = lax.axis_size(axis)
    return lax.ppermute(value, axis, [(i, i ^ distance) for i in range(size)])


def payload_kernel(num_hbm, den_hbm, rows_hbm, out_ref, num_ref, den_ref, sems):
    size, width = rows_hbm.shape
    copies = [
        pltpu.make_async_copy(num_hbm, num_ref, sems.at[0]),
        pltpu.make_async_copy(den_hbm, den_ref, sems.at[1]),
        pltpu.make_async_copy(rows_hbm, out_ref.at[pl.ds(0, size), :], sems.at[2]),
    ]
    for copy in copies:
        copy.start()
    out_ref[size:, size:] = jnp.zeros((TAIL, width - size), BF16)
    copies[0].wait()
    copies[1].wait()
    row = lax.broadcasted_iota(jnp.int32, (TAIL, size), 0)
    both = jnp.where(row == 0, num_ref[...], den_ref[...])
    out_ref[size:, :size] = both.astype(F32).astype(BF16)
    copies[2].wait()


def inputs_kernel(enc_ref, proj_ref, hidden_ref, enc_t_ref):
    samples = enc_ref.shape[0]
    tile = min(256, samples)
    for start in range(0, samples, tile):
        rows = enc_ref[start : start + tile, :]
        enc_t_ref[:, start : start + tile] = rows.T
        hidden_ref[start : start + tile, :] = dot(rows, proj_ref[...], NN).astype(BF16)


def score_kernel(group, beam, block, count, list_ref, me_ref, z_ref, hidden_ref, wanted_ref, enc_t_ref, *refs):
    payloads, refs = refs[:2], refs[-8:]
    grads_ref, kept_ref, sent_ref, weights_ref, scale_ref, logits_ref = refs[-6:]
    samples = hidden_ref.shape[0]
    size = payloads[0].shape[0] - TAIL
    for core in range(2):
        rows = pl.ds(core * size, size)
        weights_ref[rows, :] = payloads[core][:size, :]
        tail = payloads[core][size:, :size].astype(F32)
        ratio = tail[0:1, :] / tail[1:2, :]
        scale_ref[rows, :] = jnp.broadcast_to(ratio, (block, size)).T / block
    logits_ref[...] = dot(weights_ref[...], hidden_ref[...], NT)
    grads_ref[...] = jnp.zeros_like(grads_ref)
    label_iota = lax.broadcasted_iota(jnp.int32, (size, block), 0)

    def one_block(at, carried):
        low = pl.multiple_of(at * block, block)
        for core in range(2):
            cluster = me_ref[0] ^ (2 * group + core)
            place = jnp.int32(-1)
            for beam_slot in range(beam):
                place = jnp.where(list_ref[at * beam + beam_slot] == cluster, beam_slot, place)

            @pl.when(place >= 0)
            def _():
                rows = slice(core * size, (core + 1) * size)
                labels = label_iota + place * size
                target = labels == wanted_ref[0:1, pl.ds(low, block)]
                for column in range(1, wanted_ref.shape[0]):
                    target = target | (labels == wanted_ref[column : column + 1, pl.ds(low, block)])
                share = jax.nn.sigmoid(logits_ref[rows, pl.ds(low, block)]) - jnp.where(target, 1.0, 0.0)
                grads_ref[rows, pl.ds(low, block)] = (scale_ref[rows, :] * share).astype(BF16)

        return carried

    lax.fori_loop(0, samples // block, one_block, 0)
    depth = enc_t_ref.shape[0] // count
    for r in range(count):
        start = pl.multiple_of((z_ref[0] ^ r) * depth, depth)
        outer = dot(enc_t_ref[pl.ds(start, depth), :], grads_ref[...], NT)
        kept_ref[r * depth : (r + 1) * depth, :] = outer[:, :size]
        sent_ref[r * depth : (r + 1) * depth, :] = outer[:, size:].astype(BF16)


def hidden_kernel(owners, me_ref, *refs):
    chips = owners // 2
    grads, payloads, refs = refs[:chips], refs[chips : chips + owners], refs[chips + owners :]
    out_ref, rows_ref, weights_ref = refs[-3:]
    size = payloads[0].shape[0] - TAIL
    for slot in range(owners):
        piece = payloads[slot][:size, :]
        start = pl.multiple_of((me_ref[0] ^ slot) * size, size)
        rows_ref[pl.ds(start, size), :] = piece
        weights_ref[slot * size : (slot + 1) * size, :] = piece
    samples = out_ref.shape[0]
    tile = min(256, samples)
    for low in range(0, samples, tile):
        total = jnp.zeros((tile, out_ref.shape[1]), F32)
        for group in range(chips):
            rows = weights_ref[2 * group * size : 2 * (group + 1) * size, :]
            total = total + dot(grads[group][:, low : low + tile], rows, TN)
        out_ref[low : low + tile, :] = total.astype(BF16)


def enc_kernel(grad_hidden_ref, proj_ref, after_ref, out_ref, done_ref):
    out_ref[...] = dot(grad_hidden_ref[...], proj_ref[...], NT)
    done_ref[...] = jnp.zeros_like(done_ref)


def combine_kernel(own_ref, *refs):
    *received, after_ref, kept_ref, sent_ref = refs
    cut = kept_ref.shape[0]
    for rows, out_ref in ((slice(cut, None), sent_ref), (slice(0, cut), kept_ref)):
        total = own_ref[rows, :]
        for ref in received:
            total = total + ref[rows, :].astype(F32)
        out_ref[...] = total.astype(out_ref.dtype)


def head_kernel(count, z_ref, *refs):
    parts, (slice_ref, whole_ref, head_ref) = refs[:count], refs[count:]
    depth = parts[0].shape[0]
    head = jnp.zeros(head_ref.shape, F32)
    for r in range(count):
        whole_ref[r * depth : (r + 1) * depth, :] = parts[r][...]
        start = pl.multiple_of((z_ref[0] ^ r) * depth, depth)
        head = head + dot(slice_ref[pl.ds(start, depth), :], parts[r][...], TN)
    head_ref[...] = head


def fetch_kernel(rows_any, after_ref, out_ref, sem):
    copy = pltpu.make_async_copy(rows_any, out_ref, sem)
    copy.start()
    copy.wait()


def proj_kernel(count, me_ref, z_ref, *refs):
    *parts, rows_ref, out_ref, outer_ref = refs
    width, size = parts[0].shape
    for distance, part in enumerate(parts):
        start = pl.multiple_of((me_ref[0] ^ distance) * size, size)
        outer_ref[:, pl.ds(start, size)] = part[...]
    depth = width // count
    for r in range(count):
        start = pl.multiple_of((z_ref[0] ^ r) * depth, depth)
        out_ref[pl.ds(start, depth), :] = dot(outer_ref[r * depth : (r + 1) * depth, :], rows_ref[...], NN)


def shards(enc, proj, head_weight, shortlist, positives, weight_num, weight_den):
    owners, planes = lax.axis_size("label"), lax.axis_size("dp")
    chips = owners // 2
    near = [g for g in range(1, chips) if g & (g - 1) == 0]
    far = [g for g in range(1, chips) if g & (g - 1) != 0]
    row_blocks = max(1, planes // 2)
    me = lax.axis_index("label").astype(jnp.int32)
    z = lax.axis_index("dp").astype(jnp.int32)
    z_low = z & (row_blocks - 1)
    blocks, beam = shortlist.shape
    samples, width = enc.shape
    block = samples // blocks
    size = head_weight.shape[0]
    labels = owners * size
    depth = width // row_blocks
    me_s, z_s = me.reshape(1), z_low.reshape(1)
    listed = shortlist.astype(jnp.int32).reshape(-1)

    (payload,) = pl.pallas_call(
        payload_kernel,
        out_shape=[shape((size + TAIL, width), BF16)],
        in_specs=[ANY] * 3,
        out_specs=[VMEM],
        scratch_shapes=[pltpu.VMEM((1, size), jnp.int32)] * 2 + [pltpu.SemaphoreType.DMA((3,))],
        compiler_params=pltpu.CompilerParams(vmem_limit_bytes=56 * MIB),
    )(weight_num.reshape(1, size), weight_den.reshape(1, size), head_weight)
    got = {0: payload}
    for g in near:
        got[2 * g] = swap(payload, "label", 2 * g)
    got[1] = swap(payload, "label", 1)
    hidden, enc_t = call(
        inputs_kernel,
        [shape((samples, width), BF16), shape((width, samples), BF16)],
        [enc, proj],
        flops=2 * samples * width * width,
        nbytes=6_000_000,
    )
    late = gate(payload, hidden) if far else payload
    for g in far:
        got[2 * g] = swap(late, "label", 2 * g)
    for g in near + far:
        got[2 * g] = gate(got[2 * g], hidden)
        got[2 * g + 1] = swap(got[2 * g], "label", 1)

    grads, kept, from_core, moved, received = {}, {}, {}, {}, {}
    order = [0] + near + far
    wanted = positives.T
    for at, g in enumerate(order):
        if at == 0:
            after = [got[2 * n] for n in near]
        else:
            after = [grads[order[at - 1]]]
            if at + 1 < len(order):
                after.append(got[2 * order[at + 1]])
            if at >= 3:
                after.append(moved[order[at - 2]])
        grads[g], kept[g], sent = call(
            functools.partial(score_kernel, g, beam, block, row_blocks),
            [shape((2 * size, samples), BF16), shape((width, size), F32), shape((width, size), BF16)],
            [hidden, wanted, enc_t, got[2 * g], got[2 * g + 1]],
            scalars=[listed, me_s, z_s],
            after=after,
            scratch=[
                pltpu.VMEM((2 * size, width), BF16),
                pltpu.VMEM((2 * size, block), F32),
                pltpu.VMEM((2 * size, samples), F32),
            ],
            flops=8 * samples * size * width,
            nbytes=5_000_000,
        )
        from_core[g] = swap(sent, "label", 1)
        if g:
            moved[g] = (kept[g] + from_core[g].astype(F32)).astype(BF16)
            received[g] = swap(moved[g], "label", 2 * g)
    own = kept[0] + from_core[0].astype(F32)
    received = [received[g] for g in near + far]

    grad_hidden, rows = call(
        functools.partial(hidden_kernel, owners),
        [shape((samples, width), BF16), shape((labels, width), BF16)],
        [grads[g] for g in range(chips)] + [got[d] for d in range(owners)],
        scalars=[me_s],
        after=[moved[g] for g in near + far],
        scratch=[pltpu.VMEM((labels, width), BF16)],
        vmem=12,
        flops=2 * samples * width * labels,
        nbytes=5_000_000,
    )
    tile = min(256, samples)

    def grad_enc_after(value):
        return pl.pallas_call(
            enc_kernel,
            grid=(samples // tile,),
            out_shape=[shape((samples, width), F32), shape((8, 128), F32)],
            in_specs=[
                pl.BlockSpec((tile, width), lambda i: (i, 0)),
                pl.BlockSpec((width, width), lambda i: (0, 0)),
                ANY,
            ],
            out_specs=[
                pl.BlockSpec((tile, width), lambda i: (i, 0)),
                pl.BlockSpec((8, 128), lambda i: (0, 0)),
            ],
            compiler_params=pltpu.CompilerParams(vmem_limit_bytes=12 * MIB),
            cost_estimate=pl.CostEstimate(
                flops=2 * samples * width * width, bytes_accessed=6_000_000, transcendentals=0
            ),
        )(grad_hidden, proj, value)

    if row_blocks > 1:
        cut = width // 2
        total, upper = call(
            combine_kernel,
            [shape((cut, size), F32), shape((cut, size), BF16)],
            [own] + received,
            after=[grad_hidden],
            nbytes=2_000_000,
        )
        span = row_blocks // 2
        grad_enc, enc_done = grad_enc_after(upper)
        total = total + gate(swap(upper, "dp", span), enc_done).astype(F32)
        while span > 1:
            cut = span // 2 * depth
            total = total[:cut] + swap(total[cut:].astype(BF16), "dp", span // 2).astype(F32)
            span //= 2
    else:
        total = own
        for value in received:
            total = total + value.astype(F32)
        grad_enc, enc_done = grad_enc_after(total)
    total = total.astype(BF16)
    if planes > 1:
        other = swap(total, "dp", planes // 2)
        total = (total.astype(F32) + other.astype(F32)).astype(BF16)
    parts = {0: total}
    span = 1
    while span < row_blocks:
        for r in range(span):
            parts[r + span] = swap(parts[r], "dp", span)
        span *= 2
    proj_slice = lax.dynamic_slice_in_dim(proj, z * (width // planes), width // planes, 1)
    whole, grad_head = call(
        functools.partial(head_kernel, row_blocks),
        [shape((width, size), BF16), shape((width // planes, size), F32)],
        [parts[r] for r in range(row_blocks)] + [proj_slice],
        scalars=[z_s],
        flops=2 * size * width * width // planes,
        nbytes=1_000_000,
    )
    (rows,) = pl.pallas_call(
        fetch_kernel,
        out_shape=[shape((labels, width), BF16)],
        in_specs=[ANY, ANY],
        out_specs=[VMEM],
        scratch_shapes=[pltpu.SemaphoreType.DMA],
        compiler_params=pltpu.CompilerParams(vmem_limit_bytes=2 * MIB),
        cost_estimate=pl.CostEstimate(flops=0, bytes_accessed=3_000_000, transcendentals=0),
    )(rows, whole)
    have = {0: whole}
    for g in near + far:
        have[2 * g] = swap(whole, "label", 2 * g)
    if near:
        have[2 * near[0]] = gate(have[2 * near[0]], rows)
    for distance in list(have):
        have[distance + 1] = swap(have[distance], "label", 1)
    (grad_proj,) = call(
        functools.partial(proj_kernel, row_blocks),
        [shape((width, width), F32)],
        [have[distance] for distance in range(owners)] + [rows],
        scalars=[me_s, z_s],
        scratch=[pltpu.VMEM((width, labels), BF16)],
        vmem=16,
        flops=2 * labels * width * width,
        nbytes=6_000_000,
    )
    return (grad_enc, grad_proj, grad_head.T)


def solution(mesh):
    placed = (
        P(("dp", "label"), None),
        P(),
        P("label", None),
        P(("dp", "label"), None),
        P(("dp", "label"), None),
        P("label"),
        P("label"),
    )
    return jax.shard_map(
        shards,
        mesh=mesh,
        in_specs=placed,
        out_specs=(P(("dp", "label"), None), P(), P("label", "dp")),
        check_vma=False,
    )
```

```python
import functools

import jax
import jax.numpy as jnp
from jax import lax
from jax.experimental import pallas as pl
from jax.experimental.pallas import tpu as pltpu
from jax.sharding import PartitionSpec as P

BF16 = jnp.bfloat16
F32 = jnp.float32
VMEM = pl.BlockSpec(memory_space=pltpu.VMEM)
SMEM = pl.BlockSpec(memory_space=pltpu.SMEM)
ANY = pl.BlockSpec(memory_space=pl.ANY)
MIB = 1024 * 1024
TAIL = 16
NN = (((1,), (0,)), ((), ()))
NT = (((1,), (1,)), ((), ()))
TN = (((0,), (0,)), ((), ()))


def dot(left, right, dims):
    return lax.dot_general(left, right, dims, preferred_element_type=F32)


def shape(dims, dtype):
    return jax.ShapeDtypeStruct(dims, dtype)


def call(kernel, outs, args, scalars=(), after=(), scratch=(), vmem=8, flops=0, nbytes=0):
    return pl.pallas_call(
        kernel,
        out_shape=outs,
        in_specs=[SMEM] * len(scalars) + [VMEM] * len(args) + [ANY] * len(after),
        out_specs=[VMEM] * len(outs),
        scratch_shapes=list(scratch),
        compiler_params=pltpu.CompilerParams(vmem_limit_bytes=vmem * MIB),
        cost_estimate=pl.CostEstimate(flops=flops, bytes_accessed=nbytes, transcendentals=0),
    )(*scalars, *args, *after)


def gate(value, *after):
    return pl.pallas_call(
        lambda value_ref, *refs: None,
        out_shape=shape(value.shape, value.dtype),
        in_specs=[ANY] * (1 + len(after)),
        out_specs=ANY,
        input_output_aliases={0: 0},
        compiler_params=pltpu.CompilerParams(vmem_limit_bytes=MIB),
    )(value, *after)


def swap(value, axis, distance):
    size = lax.axis_size(axis)
    return lax.ppermute(value, axis, [(i, i ^ distance) for i in range(size)])


def payload_kernel(num_hbm, den_hbm, rows_hbm, enc_hbm, proj_hbm, wanted_hbm, out_ref, enc_ref, proj_ref, wanted_ref, num_ref, den_ref, sems):
    size, width = rows_hbm.shape
    pairs = [
        (num_hbm, num_ref),
        (den_hbm, den_ref),
        (rows_hbm, out_ref.at[pl.ds(0, size), :]),
        (wanted_hbm, wanted_ref),
        (proj_hbm, proj_ref),
        (enc_hbm, enc_ref),
    ]
    copies = [pltpu.make_async_copy(a, b, sems.at[i]) for i, (a, b) in enumerate(pairs)]
    for copy in copies:
        copy.start()
    out_ref[size:, size:] = jnp.zeros((TAIL, width - size), BF16)
    copies[0].wait()
    copies[1].wait()
    row = lax.broadcasted_iota(jnp.int32, (TAIL, size), 0)
    both = jnp.where(row == 0, num_ref[...], den_ref[...])
    out_ref[size:, :size] = both.astype(F32).astype(BF16)
    for copy in copies[2:]:
        copy.wait()


def inputs_kernel(beam, block, enc_ref, proj_ref, wanted_ref, hidden_ref, enc_t_ref, target_ref):
    samples = enc_ref.shape[0]
    size = target_ref.shape[0] // beam
    label_iota = lax.broadcasted_iota(jnp.int32, (size, block), 0)
    tile = min(256, samples)
    for start in range(0, samples, tile):
        rows = enc_ref[start : start + tile, :]
        enc_t_ref[:, start : start + tile] = rows.T
        hidden_ref[start : start + tile, :] = dot(rows, proj_ref[...], NN).astype(BF16)
        for low in range(start, start + tile, block):
            for place in range(beam):
                labels = label_iota + place * size
                target = labels == wanted_ref[0:1, low : low + block]
                for column in range(1, wanted_ref.shape[0]):
                    target = target | (labels == wanted_ref[column : column + 1, low : low + block])
                target_ref[place * size : (place + 1) * size, low : low + block] = jnp.where(
                    target, 1.0, 0.0
                ).astype(BF16)


def logistic(value):
    bottom = 1.0 + jnp.exp(-jnp.maximum(value, -80.0))
    guess = pl.reciprocal(bottom, approx=True)
    return guess * (2.0 - bottom * guess)


def score_kernel(group, block, count, list_ref, me_ref, z_ref, hidden_ref, target_ref, enc_t_ref, *refs):
    payloads, refs = refs[:2], refs[-8:]
    grads_ref, kept_ref, sent_ref, weights_ref, scale_ref, logits_ref = refs[-6:]
    samples = hidden_ref.shape[0]
    size = payloads[0].shape[0] - TAIL
    for core in range(2):
        rows = pl.ds(core * size, size)
        weights_ref[rows, :] = payloads[core][:size, :]
        tail = payloads[core][size:, :size].astype(F32)
        ratio = tail[0:1, :] / tail[1:2, :]
        scale_ref[rows, :] = jnp.broadcast_to(ratio, (block, size)).T / block
    logits_ref[...] = dot(weights_ref[...], hidden_ref[...], NT)
    grads_ref[...] = jnp.zeros_like(grads_ref)

    def one_block(at, carried):
        low = pl.multiple_of(at * block, block)
        for core in range(2):
            cluster = me_ref[0] ^ (2 * group + core)
            place = jnp.int32(-1)
            for beam_slot in range(list_ref.shape[0]):
                place = jnp.where(list_ref[beam_slot, at] == cluster, beam_slot, place)

            @pl.when(place >= 0)
            def _():
                rows = slice(core * size, (core + 1) * size)
                target = target_ref[pl.ds(pl.multiple_of(place * size, size), size), pl.ds(low, block)]
                share = logistic(logits_ref[rows, pl.ds(low, block)]) - target.astype(F32)
                grads_ref[rows, pl.ds(low, block)] = (scale_ref[rows, :] * share).astype(BF16)

        return carried

    lax.fori_loop(0, samples // block, one_block, 0)
    outer = dot(enc_t_ref[...], grads_ref[...], NT)
    depth = enc_t_ref.shape[0] // count
    for r in range(count):
        rows = pl.ds(pl.multiple_of((z_ref[0] ^ r) * depth, depth), depth)
        kept_ref[rows, :] = outer[r * depth : (r + 1) * depth, :size]
        sent_ref[rows, :] = outer[r * depth : (r + 1) * depth, size:].astype(BF16)


def hidden_kernel(owners, me_ref, *refs):
    chips = owners // 2
    grads, payloads, refs = refs[:chips], refs[chips : chips + owners], refs[chips + owners :]
    out_ref, rows_ref, weights_ref = refs[-3:]
    size = payloads[0].shape[0] - TAIL
    for slot in range(owners):
        piece = payloads[slot][:size, :]
        start = pl.multiple_of((me_ref[0] ^ slot) * size, size)
        rows_ref[pl.ds(start, size), :] = piece
        weights_ref[slot * size : (slot + 1) * size, :] = piece
    samples = out_ref.shape[0]
    tile = min(256, samples)
    for low in range(0, samples, tile):
        total = jnp.zeros((tile, out_ref.shape[1]), F32)
        for group in range(chips):
            rows = weights_ref[2 * group * size : 2 * (group + 1) * size, :]
            total = total + dot(grads[group][:, low : low + tile], rows, TN)
        out_ref[low : low + tile, :] = total.astype(BF16)


def enc_kernel(grad_hidden_ref, proj_ref, after_ref, out_ref, done_ref):
    out_ref[...] = dot(grad_hidden_ref[...], proj_ref[...], NT)
    done_ref[...] = jnp.zeros_like(done_ref)


def combine_kernel(own_ref, *refs):
    *received, after_ref, kept_ref, sent_ref = refs
    cut = kept_ref.shape[0]
    for rows, out_ref in ((slice(cut, None), sent_ref), (slice(0, cut), kept_ref)):
        total = own_ref[rows, :]
        for ref in received:
            total = total + ref[rows, :].astype(F32)
        out_ref[...] = total.astype(out_ref.dtype)


def whole_kernel(*refs):
    *parts, whole_ref = refs
    depth = parts[0].shape[0]
    for r, part in enumerate(parts):
        whole_ref[r * depth : (r + 1) * depth, :] = part[...]


def head_kernel(count, z_ref, rows_any, whole_ref, slice_ref, rows_ref, head_ref, sem):
    copy = pltpu.make_async_copy(rows_any, rows_ref, sem)
    copy.start()
    depth = whole_ref.shape[0] // count
    head = jnp.zeros(head_ref.shape, F32)
    for r in range(count):
        start = pl.multiple_of((z_ref[0] ^ r) * depth, depth)
        head = head + dot(slice_ref[pl.ds(start, depth), :], whole_ref[r * depth : (r + 1) * depth, :], TN)
    head_ref[...] = head
    copy.wait()


def proj_kernel(count, cuts, me_ref, z_ref, *refs):
    *parts, rows_ref, out_hbm, outer_ref, done_ref, sems = refs
    width, size = parts[0].shape
    for distance, part in enumerate(parts):
        start = pl.multiple_of((me_ref[0] ^ distance) * size, size)
        outer_ref[:, pl.ds(start, size)] = part[...]
    depth, height = width // count, width // count // cuts
    copies = []
    for r in range(count):
        for cut in range(cuts):
            low = r * depth + cut * height
            start = pl.multiple_of((z_ref[0] ^ r) * depth + cut * height, height)
            done_ref[low : low + height, :] = dot(outer_ref[low : low + height, :], rows_ref[...], NN)
            copy = pltpu.make_async_copy(
                done_ref.at[pl.ds(low, height), :], out_hbm.at[pl.ds(start, height), :], sems.at[len(copies)]
            )
            copy.start()
            copies.append(copy)
    for copy in copies:
        copy.wait()


def shards(enc, proj, head_weight, shortlist, positives, weight_num, weight_den):
    owners, planes = lax.axis_size("label"), lax.axis_size("dp")
    chips = owners // 2
    near = [g for g in range(1, chips) if g & (g - 1) == 0]
    far = [g for g in range(1, chips) if g & (g - 1) != 0]
    row_blocks = max(1, planes // 2)
    me = lax.axis_index("label").astype(jnp.int32)
    z = lax.axis_index("dp").astype(jnp.int32)
    z_low = z & (row_blocks - 1)
    blocks, beam = shortlist.shape
    samples, width = enc.shape
    block = samples // blocks
    size = head_weight.shape[0]
    labels = owners * size
    depth = width // row_blocks
    me_s, z_s = me.reshape(1), z_low.reshape(1)
    listed = shortlist.astype(jnp.int32).T

    payload, enc_near, proj_near, wanted = pl.pallas_call(
        payload_kernel,
        out_shape=[
            shape((size + TAIL, width), BF16),
            shape((samples, width), BF16),
            shape((width, width), BF16),
            shape((positives.shape[1], samples), jnp.int32),
        ],
        in_specs=[ANY] * 6,
        out_specs=[VMEM] * 4,
        scratch_shapes=[pltpu.VMEM((1, size), jnp.int32)] * 2 + [pltpu.SemaphoreType.DMA((6,))],
        compiler_params=pltpu.CompilerParams(vmem_limit_bytes=48 * MIB),
    )(weight_num.reshape(1, size), weight_den.reshape(1, size), head_weight, enc, proj, positives.T)
    got = {0: payload}
    for g in far + near:
        got[2 * g] = swap(payload, "label", 2 * g)
    got[1] = swap(payload, "label", 1)
    hidden, enc_t, target = call(
        functools.partial(inputs_kernel, beam, block),
        [shape((samples, width), BF16), shape((width, samples), BF16), shape((beam * size, samples), BF16)],
        [enc_near, proj_near, wanted],
        flops=2 * samples * width * width,
        nbytes=6_000_000,
    )
    grads, kept, from_core, moved, received = {}, {}, {}, {}, {}
    order = [0] + far + near
    for at, g in enumerate(order):
        if at + 1 < len(order):
            ahead = order[at + 1]
            got[2 * ahead] = gate(got[2 * ahead], hidden if at < 2 else grads[order[at - 2]])
            got[2 * ahead + 1] = swap(got[2 * ahead], "label", 1)
        after = [] if at == 0 else [grads[order[at - 1]]]
        if at + 1 < len(order) and at > 0:
            after.append(got[2 * order[at + 1]])
        if at >= 3:
            after.append(moved[order[at - 2]])
        grads[g], kept[g], sent = call(
            functools.partial(score_kernel, g, block, row_blocks),
            [shape((2 * size, samples), BF16), shape((width, size), F32), shape((width, size), BF16)],
            [hidden, target, enc_t, got[2 * g], got[2 * g + 1]],
            scalars=[listed, me_s, z_s],
            after=after,
            scratch=[
                pltpu.VMEM((2 * size, width), BF16),
                pltpu.VMEM((2 * size, block), F32),
                pltpu.VMEM((2 * size, samples), F32),
            ],
            flops=8 * samples * size * width,
            nbytes=5_000_000,
        )
        from_core[g] = swap(sent, "label", 1)
        if g:
            moved[g] = (kept[g] + from_core[g].astype(F32)).astype(BF16)
            received[g] = swap(moved[g], "label", 2 * g)
    own = kept[0] + from_core[0].astype(F32)
    received = [received[g] for g in far + near]

    grad_hidden, rows = call(
        functools.partial(hidden_kernel, owners),
        [shape((samples, width), BF16), shape((labels, width), BF16)],
        [grads[g] for g in range(chips)] + [got[d] for d in range(owners)],
        scalars=[me_s],
        after=[moved[g] for g in far + near],
        scratch=[pltpu.VMEM((labels, width), BF16)],
        vmem=12,
        flops=2 * samples * width * labels,
        nbytes=5_000_000,
    )
    tile = min(256, samples)

    def grad_enc_after(value):
        return pl.pallas_call(
            enc_kernel,
            grid=(samples // tile,),
            out_shape=[shape((samples, width), F32), shape((8, 128), F32)],
            in_specs=[
                pl.BlockSpec((tile, width), lambda i: (i, 0)),
                pl.BlockSpec((width, width), lambda i: (0, 0)),
                ANY,
            ],
            out_specs=[
                pl.BlockSpec((tile, width), lambda i: (i, 0)),
                pl.BlockSpec((8, 128), lambda i: (0, 0)),
            ],
            compiler_params=pltpu.CompilerParams(vmem_limit_bytes=12 * MIB),
            cost_estimate=pl.CostEstimate(
                flops=2 * samples * width * width, bytes_accessed=6_000_000, transcendentals=0
            ),
        )(grad_hidden, proj, value)

    if row_blocks > 1:
        cut = width // 2
        total, upper = call(
            combine_kernel,
            [shape((cut, size), F32), shape((cut, size), BF16)],
            [own] + received,
            after=[grad_hidden],
            nbytes=2_000_000,
        )
        span = row_blocks // 2
        total = total + swap(upper, "dp", span).astype(F32)
        while span > 1:
            cut = span // 2 * depth
            total = total[:cut] + swap(total[cut:].astype(BF16), "dp", span // 2).astype(F32)
            span //= 2
    else:
        total = own
        for value in received:
            total = total + value.astype(F32)
    total = total.astype(BF16)
    grad_enc, enc_done = grad_enc_after(total)
    if planes > 1:
        other = gate(swap(total, "dp", planes // 2), enc_done)
        total = (total.astype(F32) + other.astype(F32)).astype(BF16)
    parts = {0: total}
    span = 1
    while span < row_blocks:
        for r in range(span):
            parts[r + span] = swap(parts[r], "dp", span)
        span *= 2
    proj_slice = lax.dynamic_slice_in_dim(proj, z * (width // planes), width // planes, 1)
    (whole,) = call(whole_kernel, [shape((width, size), BF16)], [parts[r] for r in range(row_blocks)], vmem=2)
    rows, grad_head = pl.pallas_call(
        functools.partial(head_kernel, row_blocks),
        out_shape=[shape((labels, width), BF16), shape((width // planes, size), F32)],
        in_specs=[SMEM, ANY, VMEM, VMEM],
        out_specs=[VMEM, VMEM],
        scratch_shapes=[pltpu.SemaphoreType.DMA],
        compiler_params=pltpu.CompilerParams(vmem_limit_bytes=4 * MIB),
        cost_estimate=pl.CostEstimate(
            flops=2 * size * width * width // planes, bytes_accessed=3_000_000, transcendentals=0
        ),
    )(z_s, rows, whole, proj_slice)
    have = {0: whole}
    for g in near + far:
        have[2 * g] = gate(swap(whole, "label", 2 * g), rows)
    for distance in list(have):
        have[distance + 1] = swap(have[distance], "label", 1)
    cuts = 2
    grad_proj = pl.pallas_call(
        functools.partial(proj_kernel, row_blocks, cuts),
        out_shape=shape((width, width), F32),
        in_specs=[SMEM] * 2 + [VMEM] * (owners + 1),
        out_specs=ANY,
        scratch_shapes=[
            pltpu.VMEM((width, labels), BF16),
            pltpu.VMEM((width, width), F32),
            pltpu.SemaphoreType.DMA((row_blocks * cuts,)),
        ],
        compiler_params=pltpu.CompilerParams(vmem_limit_bytes=16 * MIB),
        cost_estimate=pl.CostEstimate(
            flops=2 * labels * width * width, bytes_accessed=6_000_000, transcendentals=0
        ),
    )(me_s, z_s, *[have[distance] for distance in range(owners)], rows)
    return (grad_enc, grad_proj, grad_head.T)


def solution(mesh):
    placed = (
        P(("dp", "label"), None),
        P(),
        P("label", None),
        P(("dp", "label"), None),
        P(("dp", "label"), None),
        P("label"),
        P("label"),
    )
    return jax.shard_map(
        shards,
        mesh=mesh,
        in_specs=placed,
        out_specs=(P(("dp", "label"), None), P(), P("label", "dp")),
        check_vma=False,
    )
```

```python
import functools

import jax
import jax.numpy as jnp
from jax import lax
from jax.experimental import pallas as pl
from jax.experimental.pallas import tpu as pltpu
from jax.sharding import PartitionSpec as P

BF16 = jnp.bfloat16
F32 = jnp.float32
VMEM = pl.BlockSpec(memory_space=pltpu.VMEM)
SMEM = pl.BlockSpec(memory_space=pltpu.SMEM)
ANY = pl.BlockSpec(memory_space=pl.ANY)
MIB = 1024 * 1024
TAIL = 16
NN = (((1,), (0,)), ((), ()))
NT = (((1,), (1,)), ((), ()))
TN = (((0,), (0,)), ((), ()))


def dot(left, right, dims):
    return lax.dot_general(left, right, dims, preferred_element_type=F32)


def shape(dims, dtype):
    return jax.ShapeDtypeStruct(dims, dtype)


def call(kernel, outs, args, scalars=(), after=(), scratch=(), vmem=8, flops=0, nbytes=0):
    return pl.pallas_call(
        kernel,
        out_shape=outs,
        in_specs=[SMEM] * len(scalars) + [VMEM] * len(args) + [ANY] * len(after),
        out_specs=[VMEM] * len(outs),
        scratch_shapes=list(scratch),
        compiler_params=pltpu.CompilerParams(vmem_limit_bytes=vmem * MIB),
        cost_estimate=pl.CostEstimate(flops=flops, bytes_accessed=nbytes, transcendentals=0),
    )(*scalars, *args, *after)


def gate(value, *after):
    return pl.pallas_call(
        lambda value_ref, *refs: None,
        out_shape=shape(value.shape, value.dtype),
        in_specs=[ANY] * (1 + len(after)),
        out_specs=ANY,
        input_output_aliases={0: 0},
        compiler_params=pltpu.CompilerParams(vmem_limit_bytes=MIB),
    )(value, *after)


def swap(value, axis, distance):
    size = lax.axis_size(axis)
    return lax.ppermute(value, axis, [(i, i ^ distance) for i in range(size)])


def payload_kernel(num_hbm, den_hbm, rows_hbm, out_ref, num_ref, den_ref, sems):
    size, width = rows_hbm.shape
    copies = [
        pltpu.make_async_copy(num_hbm, num_ref, sems.at[0]),
        pltpu.make_async_copy(den_hbm, den_ref, sems.at[1]),
        pltpu.make_async_copy(rows_hbm, out_ref.at[pl.ds(0, size), :], sems.at[2]),
    ]
    for copy in copies:
        copy.start()
    out_ref[size:, size:] = jnp.zeros((TAIL, width - size), BF16)
    copies[0].wait()
    copies[1].wait()
    row = lax.broadcasted_iota(jnp.int32, (TAIL, size), 0)
    both = jnp.where(row == 0, num_ref[...], den_ref[...])
    out_ref[size:, :size] = both.astype(F32).astype(BF16)
    copies[2].wait()


def target_kernel(beam, block, wanted_ref, target_ref):
    samples = wanted_ref.shape[1]
    size = target_ref.shape[0] // beam
    label_iota = lax.broadcasted_iota(jnp.int32, (size, block), 0)
    for low in range(0, samples, block):
        for place in range(beam):
            labels = label_iota + place * size
            target = labels == wanted_ref[0:1, low : low + block]
            for column in range(1, wanted_ref.shape[0]):
                target = target | (labels == wanted_ref[column : column + 1, low : low + block])
            target_ref[place * size : (place + 1) * size, low : low + block] = jnp.where(
                target, 1.0, 0.0
            ).astype(BF16)


def inputs_kernel(enc_ref, proj_ref, after_ref, hidden_t_ref):
    samples = enc_ref.shape[0]
    tile = min(256, samples)
    for start in range(0, samples, tile):
        hidden = dot(enc_ref[start : start + tile, :], proj_ref[...], NN).astype(BF16)
        hidden_t_ref[:, start : start + tile] = hidden.T


def logistic(value):
    bottom = 1.0 + jnp.exp(-jnp.maximum(value, -80.0))
    guess = pl.reciprocal(bottom, approx=True)
    return guess * (2.0 - bottom * guess)


def score_kernel(group, block, count, list_ref, me_ref, z_ref, hidden_t_ref, target_ref, enc_ref, *refs):
    payloads, refs = refs[:2], refs[-8:]
    grads_ref, kept_ref, sent_ref, weights_ref, scale_ref, logits_ref = refs[-6:]
    samples = enc_ref.shape[0]
    size = payloads[0].shape[0] - TAIL
    for core in range(2):
        rows = pl.ds(core * size, size)
        weights_ref[rows, :] = payloads[core][:size, :]
        tail = payloads[core][size:, :size].astype(F32)
        ratio = tail[0:1, :] / tail[1:2, :]
        scale_ref[rows, :] = jnp.broadcast_to(ratio, (block, size)).T / block
    logits_ref[...] = dot(weights_ref[...], hidden_t_ref[...], NN)
    grads_ref[...] = jnp.zeros_like(grads_ref)

    def one_block(at, carried):
        low = pl.multiple_of(at * block, block)
        for core in range(2):
            cluster = me_ref[0] ^ (2 * group + core)
            place = jnp.int32(-1)
            for beam_slot in range(list_ref.shape[0]):
                place = jnp.where(list_ref[beam_slot, at] == cluster, beam_slot, place)

            @pl.when(place >= 0)
            def _():
                rows = slice(core * size, (core + 1) * size)
                target = target_ref[pl.ds(pl.multiple_of(place * size, size), size), pl.ds(low, block)]
                share = logistic(logits_ref[rows, pl.ds(low, block)]) - target.astype(F32)
                grads_ref[rows, pl.ds(low, block)] = (scale_ref[rows, :] * share).astype(BF16)

        return carried

    lax.fori_loop(0, samples // block, one_block, 0)
    outer = dot(grads_ref[...], enc_ref[...], NN)
    depth = size // count
    for r in range(count):
        rows = pl.ds(pl.multiple_of((z_ref[0] ^ r) * depth, depth), depth)
        kept_ref[rows, :] = outer[r * depth : (r + 1) * depth, :]
        sent_ref[rows, :] = outer[size + r * depth : size + (r + 1) * depth, :].astype(BF16)


def hidden_kernel(owners, me_ref, *refs):
    chips = owners // 2
    grads, payloads, refs = refs[:chips], refs[chips : chips + owners], refs[chips + owners :]
    out_ref, rows_ref, weights_ref = refs[-3:]
    size = payloads[0].shape[0] - TAIL
    for slot in range(owners):
        piece = payloads[slot][:size, :]
        start = pl.multiple_of((me_ref[0] ^ slot) * size, size)
        rows_ref[pl.ds(start, size), :] = piece
        weights_ref[slot * size : (slot + 1) * size, :] = piece
    samples = out_ref.shape[0]
    tile = min(256, samples)
    for low in range(0, samples, tile):
        total = jnp.zeros((tile, out_ref.shape[1]), F32)
        for group in range(chips):
            rows = weights_ref[2 * group * size : 2 * (group + 1) * size, :]
            total = total + dot(grads[group][:, low : low + tile], rows, TN)
        out_ref[low : low + tile, :] = total.astype(BF16)


def enc_kernel(grad_hidden_ref, proj_ref, after_ref, out_ref, done_ref):
    out_ref[...] = dot(grad_hidden_ref[...], proj_ref[...], NT)
    done_ref[...] = jnp.zeros_like(done_ref)


def combine_kernel(own_ref, *refs):
    *received, after_ref, kept_ref, sent_ref = refs
    cut = kept_ref.shape[0]
    for rows, out_ref in ((slice(cut, None), sent_ref), (slice(0, cut), kept_ref)):
        total = own_ref[rows, :]
        for ref in received:
            total = total + ref[rows, :].astype(F32)
        out_ref[...] = total.astype(out_ref.dtype)


def whole_kernel(z_ref, *refs):
    *parts, whole_ref, rows_ref = refs
    depth = parts[0].shape[0]
    for r, part in enumerate(parts):
        rows_ref[pl.ds(pl.multiple_of((z_ref[0] ^ r) * depth, depth), depth), :] = part[...]
    whole_ref[...] = rows_ref[...].T


def head_kernel(rows_any, whole_ref, slice_ref, rows_ref, head_ref, sem):
    copy = pltpu.make_async_copy(rows_any, rows_ref, sem)
    copy.start()
    head_ref[...] = dot(slice_ref[...], whole_ref[...], TN)
    copy.wait()


def proj_kernel(cuts, me_ref, *refs):
    *parts, rows_ref, out_hbm, outer_ref, done_ref, sems = refs
    width, size = parts[0].shape
    for distance, part in enumerate(parts):
        start = pl.multiple_of((me_ref[0] ^ distance) * size, size)
        outer_ref[:, pl.ds(start, size)] = part[...]
    height = width // cuts
    copies = []
    for cut in range(cuts):
        rows = pl.ds(cut * height, height)
        done_ref[rows, :] = dot(outer_ref[rows, :], rows_ref[...], NN)
        copy = pltpu.make_async_copy(done_ref.at[rows, :], out_hbm.at[rows, :], sems.at[cut])
        copy.start()
        copies.append(copy)
    for copy in copies:
        copy.wait()


def shards(enc, proj, head_weight, shortlist, positives, weight_num, weight_den):
    owners, planes = lax.axis_size("label"), lax.axis_size("dp")
    chips = owners // 2
    near = [g for g in range(1, chips) if g & (g - 1) == 0]
    far = [g for g in range(1, chips) if g & (g - 1) != 0]
    row_blocks = max(1, planes // 2)
    me = lax.axis_index("label").astype(jnp.int32)
    z = lax.axis_index("dp").astype(jnp.int32)
    z_low = z & (row_blocks - 1)
    blocks, beam = shortlist.shape
    samples, width = enc.shape
    block = samples // blocks
    size = head_weight.shape[0]
    labels = owners * size
    depth = size // row_blocks
    me_s, z_s = me.reshape(1), z_low.reshape(1)
    listed = shortlist.astype(jnp.int32).T

    payload = pl.pallas_call(
        payload_kernel,
        out_shape=shape((size + TAIL, width), BF16),
        in_specs=[ANY] * 3,
        out_specs=VMEM,
        scratch_shapes=[pltpu.VMEM((1, size), jnp.int32)] * 2 + [pltpu.SemaphoreType.DMA((3,))],
        compiler_params=pltpu.CompilerParams(vmem_limit_bytes=56 * MIB),
    )(weight_num.reshape(1, size), weight_den.reshape(1, size), head_weight)
    got = {0: payload}
    for g in far + near:
        got[2 * g] = swap(payload, "label", 2 * g)
    got[1] = swap(payload, "label", 1)
    (target,) = call(
        functools.partial(target_kernel, beam, block),
        [shape((beam * size, samples), BF16)],
        [positives.T],
        vmem=2,
        nbytes=8_000_000,
    )
    (hidden_t,) = call(
        inputs_kernel,
        [shape((width, samples), BF16)],
        [enc, proj],
        after=[target],
        flops=2 * samples * width * width,
        nbytes=6_000_000,
    )
    grads, kept, from_core, moved, received = {}, {}, {}, {}, {}
    order = [0] + far + near
    for at, g in enumerate(order):
        after = [] if at == 0 else [grads[order[at - 1]]]
        if at and at + 1 < len(order):
            after.append(got[2 * order[at + 1]])
        if at >= 3:
            after.append(moved[order[at - 2]])
        grads[g], kept[g], sent = call(
            functools.partial(score_kernel, g, block, row_blocks),
            [shape((2 * size, samples), BF16), shape((size, width), F32), shape((size, width), BF16)],
            [hidden_t, target, enc, got[2 * g], got[2 * g + 1]],
            scalars=[listed, me_s, z_s],
            after=after,
            scratch=[
                pltpu.VMEM((2 * size, width), BF16),
                pltpu.VMEM((2 * size, block), F32),
                pltpu.VMEM((2 * size, samples), F32),
            ],
            flops=8 * samples * size * width,
            nbytes=5_000_000,
        )
        for ahead in order[1:3] if at == 0 else order[at + 2 : at + 3]:
            got[2 * ahead] = gate(got[2 * ahead], grads[g])
            got[2 * ahead + 1] = swap(got[2 * ahead], "label", 1)
        from_core[g] = swap(sent, "label", 1)
        if g:
            moved[g] = (kept[g] + from_core[g].astype(F32)).astype(BF16)
            received[g] = swap(moved[g], "label", 2 * g)
    own = kept[0] + from_core[0].astype(F32)
    received = [received[g] for g in far + near]

    grad_hidden, rows = call(
        functools.partial(hidden_kernel, owners),
        [shape((samples, width), BF16), shape((labels, width), BF16)],
        [grads[g] for g in range(chips)] + [got[d] for d in range(owners)],
        scalars=[me_s],
        after=[moved[g] for g in far + near],
        scratch=[pltpu.VMEM((labels, width), BF16)],
        vmem=12,
        flops=2 * samples * width * labels,
        nbytes=5_000_000,
    )
    tile = min(256, samples)

    def grad_enc_after(value):
        return pl.pallas_call(
            enc_kernel,
            grid=(samples // tile,),
            out_shape=[shape((samples, width), F32), shape((8, 128), F32)],
            in_specs=[
                pl.BlockSpec((tile, width), lambda i: (i, 0)),
                pl.BlockSpec((width, width), lambda i: (0, 0)),
                ANY,
            ],
            out_specs=[
                pl.BlockSpec((tile, width), lambda i: (i, 0)),
                pl.BlockSpec((8, 128), lambda i: (0, 0)),
            ],
            compiler_params=pltpu.CompilerParams(vmem_limit_bytes=12 * MIB),
            cost_estimate=pl.CostEstimate(
                flops=2 * samples * width * width, bytes_accessed=6_000_000, transcendentals=0
            ),
        )(grad_hidden, proj, value)

    if row_blocks > 1:
        cut = size // 2
        total, upper = call(
            combine_kernel,
            [shape((cut, width), F32), shape((cut, width), BF16)],
            [own] + received,
            after=[grad_hidden],
            nbytes=2_000_000,
        )
        span = row_blocks // 2
        total = total + swap(upper, "dp", span).astype(F32)
        while span > 1:
            cut = span // 2 * depth
            total = total[:cut] + swap(total[cut:].astype(BF16), "dp", span // 2).astype(F32)
            span //= 2
    else:
        total = own
        for value in received:
            total = total + value.astype(F32)
    total = total.astype(BF16)
    grad_enc, enc_done = grad_enc_after(total)
    if planes > 1:
        other = gate(swap(total, "dp", planes // 2), enc_done)
        total = (total.astype(F32) + other.astype(F32)).astype(BF16)
    parts = {0: total}
    span = 1
    while span < row_blocks:
        for r in range(span):
            parts[r + span] = swap(parts[r], "dp", span)
        span *= 2
    proj_slice = lax.dynamic_slice_in_dim(proj, z * (width // planes), width // planes, 1)
    (whole,) = call(
        whole_kernel,
        [shape((width, size), BF16)],
        [parts[r] for r in range(row_blocks)],
        scalars=[z_s],
        scratch=[pltpu.VMEM((size, width), BF16)],
        vmem=4,
    )
    rows, grad_head = pl.pallas_call(
        head_kernel,
        out_shape=[shape((labels, width), BF16), shape((width // planes, size), F32)],
        in_specs=[ANY, VMEM, VMEM],
        out_specs=[VMEM, VMEM],
        scratch_shapes=[pltpu.SemaphoreType.DMA],
        compiler_params=pltpu.CompilerParams(vmem_limit_bytes=4 * MIB),
        cost_estimate=pl.CostEstimate(
            flops=2 * size * width * width // planes, bytes_accessed=3_000_000, transcendentals=0
        ),
    )(rows, whole, proj_slice)
    have = {0: whole}
    for g in near + far:
        have[2 * g] = gate(swap(whole, "label", 2 * g), rows)
    for distance in list(have):
        have[distance + 1] = swap(have[distance], "label", 1)
    cuts = 4
    grad_proj = pl.pallas_call(
        functools.partial(proj_kernel, cuts),
        out_shape=shape((width, width), F32),
        in_specs=[SMEM] + [VMEM] * (owners + 1),
        out_specs=ANY,
        scratch_shapes=[
            pltpu.VMEM((width, labels), BF16),
            pltpu.VMEM((width, width), F32),
            pltpu.SemaphoreType.DMA((cuts,)),
        ],
        compiler_params=pltpu.CompilerParams(vmem_limit_bytes=16 * MIB),
        cost_estimate=pl.CostEstimate(
            flops=2 * labels * width * width, bytes_accessed=6_000_000, transcendentals=0
        ),
    )(me_s, *[have[distance] for distance in range(owners)], rows)
    return (grad_enc, grad_proj, grad_head.T)


def solution(mesh):
    placed = (
        P(("dp", "label"), None),
        P(),
        P("label", None),
        P(("dp", "label"), None),
        P(("dp", "label"), None),
        P("label"),
        P("label"),
    )
    return jax.shard_map(
        shards,
        mesh=mesh,
        in_specs=placed,
        out_specs=(P(("dp", "label"), None), P(), P("label", "dp")),
        check_vma=False,
    )
```

```python
import functools

import jax
import jax.numpy as jnp
from jax import lax
from jax.experimental import pallas as pl
from jax.experimental.pallas import tpu as pltpu
from jax.sharding import PartitionSpec as P

BF16 = jnp.bfloat16
F32 = jnp.float32
VMEM = pl.BlockSpec(memory_space=pltpu.VMEM)
SMEM = pl.BlockSpec(memory_space=pltpu.SMEM)
ANY = pl.BlockSpec(memory_space=pl.ANY)
MIB = 1024 * 1024
TAIL = 16
NN = (((1,), (0,)), ((), ()))
NT = (((1,), (1,)), ((), ()))
TN = (((0,), (0,)), ((), ()))


def dot(left, right, dims):
    return lax.dot_general(left, right, dims, preferred_element_type=F32)


def shape(dims, dtype):
    return jax.ShapeDtypeStruct(dims, dtype)


def call(kernel, outs, args, scalars=(), after=(), scratch=(), vmem=8, flops=0, nbytes=0):
    return pl.pallas_call(
        kernel,
        out_shape=outs,
        in_specs=[SMEM] * len(scalars) + [VMEM] * len(args) + [ANY] * len(after),
        out_specs=[VMEM] * len(outs),
        scratch_shapes=list(scratch),
        compiler_params=pltpu.CompilerParams(vmem_limit_bytes=vmem * MIB),
        cost_estimate=pl.CostEstimate(flops=flops, bytes_accessed=nbytes, transcendentals=0),
    )(*scalars, *args, *after)


def gate(value, *after):
    return pl.pallas_call(
        lambda value_ref, *refs: None,
        out_shape=shape(value.shape, value.dtype),
        in_specs=[ANY] * (1 + len(after)),
        out_specs=ANY,
        input_output_aliases={0: 0},
        compiler_params=pltpu.CompilerParams(vmem_limit_bytes=MIB),
    )(value, *after)


def swap(value, axis, distance):
    size = lax.axis_size(axis)
    return lax.ppermute(value, axis, [(i, i ^ distance) for i in range(size)])


def payload_kernel(num_hbm, den_hbm, rows_hbm, out_ref, num_ref, den_ref, sems):
    size, width = rows_hbm.shape
    copies = [
        pltpu.make_async_copy(num_hbm, num_ref, sems.at[0]),
        pltpu.make_async_copy(den_hbm, den_ref, sems.at[1]),
        pltpu.make_async_copy(rows_hbm, out_ref.at[pl.ds(0, size), :], sems.at[2]),
    ]
    for copy in copies:
        copy.start()
    out_ref[size:, size:] = jnp.zeros((TAIL, width - size), BF16)
    copies[0].wait()
    copies[1].wait()
    row = lax.broadcasted_iota(jnp.int32, (TAIL, size), 0)
    both = jnp.where(row == 0, num_ref[...], den_ref[...])
    out_ref[size:, :size] = both.astype(F32).astype(BF16)
    copies[2].wait()


def target_kernel(beam, block, wanted_ref, payload_ref, target_ref, copy_ref):
    copy_ref[...] = payload_ref[...]
    samples = wanted_ref.shape[1]
    size = target_ref.shape[0] // beam
    label_iota = lax.broadcasted_iota(jnp.int32, (size, block), 0)
    for low in range(0, samples, block):
        for place in range(beam):
            labels = label_iota + place * size
            target = labels == wanted_ref[0:1, low : low + block]
            for column in range(1, wanted_ref.shape[0]):
                target = target | (labels == wanted_ref[column : column + 1, low : low + block])
            target_ref[place * size : (place + 1) * size, low : low + block] = jnp.where(
                target, 1.0, 0.0
            ).astype(BF16)


def inputs_kernel(enc_ref, proj_ref, after_ref, hidden_t_ref):
    samples = enc_ref.shape[0]
    tile = min(256, samples)
    for start in range(0, samples, tile):
        hidden = dot(enc_ref[start : start + tile, :], proj_ref[...], NN).astype(BF16)
        hidden_t_ref[:, start : start + tile] = hidden.T


def logistic(value):
    bottom = 1.0 + jnp.exp(-jnp.maximum(value, -80.0))
    guess = pl.reciprocal(bottom, approx=True)
    return guess * (2.0 - bottom * guess)


def score_kernel(group, block, count, places_ref, z_ref, hidden_t_ref, target_ref, enc_ref, *refs):
    payloads, refs = refs[:2], refs[-6:]
    grads_ref, kept_ref, sent_ref, weights_ref, scale_ref, logits_ref = refs
    samples = enc_ref.shape[0]
    size = payloads[0].shape[0] - TAIL
    blocks = samples // block
    for core in range(2):
        rows = pl.ds(core * size, size)
        weights_ref[rows, :] = payloads[core][:size, :]
        tail = payloads[core][size:, :size].astype(F32)
        ratio = tail[0:1, :] / tail[1:2, :]
        scale_ref[rows, :] = jnp.broadcast_to(ratio, (block, size)).T
    tile = min(2 * block, samples)
    for start in range(0, samples, tile):
        logits_ref[:, start : start + tile] = dot(
            weights_ref[...], hidden_t_ref[:, start : start + tile], NN
        )
        for low in range(start, start + tile, block):
            for core in range(2):
                place = places_ref[(2 * group + core) * blocks + low // block]
                factor = jnp.where(place >= 0, 1.0 / block, 0.0)
                first = pl.multiple_of(jnp.maximum(place, 0) * size, size)
                rows = slice(core * size, (core + 1) * size)
                target = target_ref[pl.ds(first, size), low : low + block].astype(F32)
                share = logistic(logits_ref[rows, low : low + block]) - target
                grads_ref[rows, low : low + block] = (scale_ref[rows, :] * factor * share).astype(BF16)
    outer = dot(grads_ref[...], enc_ref[...], NN)
    depth = size // count
    for r in range(count):
        rows = pl.ds(pl.multiple_of((z_ref[0] ^ r) * depth, depth), depth)
        kept_ref[rows, :] = outer[r * depth : (r + 1) * depth, :]
        sent_ref[rows, :] = outer[size + r * depth : size + (r + 1) * depth, :].astype(BF16)


def hidden_kernel(owners, me_ref, *refs):
    chips = owners // 2
    grads, payloads, refs = refs[:chips], refs[chips : chips + owners], refs[chips + owners :]
    out_ref, rows_ref, weights_ref = refs[-3:]
    size = payloads[0].shape[0] - TAIL
    for slot in range(owners):
        piece = payloads[slot][:size, :]
        start = pl.multiple_of((me_ref[0] ^ slot) * size, size)
        rows_ref[pl.ds(start, size), :] = piece
        weights_ref[slot * size : (slot + 1) * size, :] = piece
    samples = out_ref.shape[0]
    tile = min(256, samples)
    for low in range(0, samples, tile):
        total = jnp.zeros((tile, out_ref.shape[1]), F32)
        for group in range(chips):
            rows = weights_ref[2 * group * size : 2 * (group + 1) * size, :]
            total = total + dot(grads[group][:, low : low + tile], rows, TN)
        out_ref[low : low + tile, :] = total.astype(BF16)


def enc_kernel(grad_hidden_ref, proj_ref, after_ref, out_ref, done_ref):
    out_ref[...] = dot(grad_hidden_ref[...], proj_ref[...], NT)
    done_ref[...] = jnp.zeros_like(done_ref)


def combine_kernel(own_ref, *refs):
    *received, after_ref, kept_ref, sent_ref = refs
    cut = kept_ref.shape[0]
    for rows, out_ref in ((slice(cut, None), sent_ref), (slice(0, cut), kept_ref)):
        total = own_ref[rows, :]
        for ref in received:
            total = total + ref[rows, :].astype(F32)
        out_ref[...] = total.astype(out_ref.dtype)


def whole_kernel(z_ref, *refs):
    *parts, whole_ref, rows_ref = refs
    depth = parts[0].shape[0]
    for r, part in enumerate(parts):
        rows_ref[pl.ds(pl.multiple_of((z_ref[0] ^ r) * depth, depth), depth), :] = part[...]
    whole_ref[...] = rows_ref[...].T


def head_kernel(rows_any, whole_ref, slice_ref, rows_ref, head_ref, sem):
    copy = pltpu.make_async_copy(rows_any, rows_ref, sem)
    copy.start()
    head_ref[...] = dot(slice_ref[...], whole_ref[...], TN)
    copy.wait()


def proj_kernel(cuts, me_ref, *refs):
    *parts, rows_ref, out_hbm, outer_ref, done_ref, sems = refs
    width, size = parts[0].shape
    for distance, part in enumerate(parts):
        start = pl.multiple_of((me_ref[0] ^ distance) * size, size)
        outer_ref[:, pl.ds(start, size)] = part[...]
    height = width // cuts
    copies = []
    for cut in range(cuts):
        rows = pl.ds(cut * height, height)
        done_ref[rows, :] = dot(outer_ref[rows, :], rows_ref[...], NN)
        copy = pltpu.make_async_copy(done_ref.at[rows, :], out_hbm.at[rows, :], sems.at[cut])
        copy.start()
        copies.append(copy)
    for copy in copies:
        copy.wait()


def shards(enc, proj, head_weight, shortlist, positives, weight_num, weight_den):
    owners, planes = lax.axis_size("label"), lax.axis_size("dp")
    chips = owners // 2
    near = [g for g in range(1, chips) if g & (g - 1) == 0]
    far = [g for g in range(1, chips) if g & (g - 1) != 0]
    row_blocks = max(1, planes // 2)
    me = lax.axis_index("label").astype(jnp.int32)
    z = lax.axis_index("dp").astype(jnp.int32)
    z_low = z & (row_blocks - 1)
    blocks, beam = shortlist.shape
    samples, width = enc.shape
    block = samples // blocks
    size = head_weight.shape[0]
    labels = owners * size
    depth = size // row_blocks
    me_s, z_s = me.reshape(1), z_low.reshape(1)
    payload = pl.pallas_call(
        payload_kernel,
        out_shape=shape((size + TAIL, width), BF16),
        in_specs=[ANY] * 3,
        out_specs=VMEM,
        scratch_shapes=[pltpu.VMEM((1, size), jnp.int32)] * 2 + [pltpu.SemaphoreType.DMA((3,))],
        compiler_params=pltpu.CompilerParams(vmem_limit_bytes=56 * MIB),
    )(weight_num.reshape(1, size), weight_den.reshape(1, size), head_weight)
    got = {0: payload}
    for g in near:
        got[2 * g] = swap(payload, "label", 2 * g)
    got[1] = swap(payload, "label", 1)
    target, late = call(
        functools.partial(target_kernel, beam, block),
        [shape((beam * size, samples), BF16), shape(payload.shape, BF16)],
        [positives.T, payload],
        vmem=4,
        nbytes=8_000_000,
    )
    (hidden_t,) = call(
        inputs_kernel,
        [shape((width, samples), BF16)],
        [enc, proj],
        after=[target],
        flops=2 * samples * width * width,
        nbytes=6_000_000,
    )
    for g in far:
        got[2 * g] = swap(late, "label", 2 * g)
    for g in near:
        got[2 * g] = gate(got[2 * g], hidden_t)
        got[2 * g + 1] = swap(got[2 * g], "label", 1)
    clusters = me ^ jnp.arange(owners, dtype=jnp.int32)
    listing = shortlist.astype(jnp.int32)[None, :, :] == clusters[:, None, None]
    places = jnp.max(jnp.where(listing, jnp.arange(beam, dtype=jnp.int32), -1), axis=2).reshape(-1)
    grads, kept, from_core, moved, received = {}, {}, {}, {}, {}
    order = [0] + near + far
    for at, g in enumerate(order):
        after = [got[2 * n] for n in near] if at == 0 else [grads[order[at - 1]]]
        if at and at + 1 < len(order):
            after.append(got[2 * order[at + 1]])
        if at >= 3:
            after.append(moved[order[at - 2]])
        grads[g], kept[g], sent = call(
            functools.partial(score_kernel, g, block, row_blocks),
            [shape((2 * size, samples), BF16), shape((size, width), F32), shape((size, width), BF16)],
            [hidden_t, target, enc, got[2 * g], got[2 * g + 1]],
            scalars=[places, z_s],
            after=after,
            scratch=[
                pltpu.VMEM((2 * size, width), BF16),
                pltpu.VMEM((2 * size, block), F32),
                pltpu.VMEM((2 * size, samples), F32),
            ],
            flops=8 * samples * size * width,
            nbytes=5_000_000,
        )
        for ahead in [n for n in order[at + 2 : at + 3] if n in far]:
            got[2 * ahead] = gate(got[2 * ahead], grads[g])
            got[2 * ahead + 1] = swap(got[2 * ahead], "label", 1)
        from_core[g] = swap(sent, "label", 1)
        if g:
            moved[g] = (kept[g] + from_core[g].astype(F32)).astype(BF16)
            received[g] = swap(moved[g], "label", 2 * g)
    own = kept[0] + from_core[0].astype(F32)
    received = [received[g] for g in near + far]

    grad_hidden, rows = call(
        functools.partial(hidden_kernel, owners),
        [shape((samples, width), BF16), shape((labels, width), BF16)],
        [grads[g] for g in range(chips)] + [got[d] for d in range(owners)],
        scalars=[me_s],
        after=[moved[g] for g in near + far],
        scratch=[pltpu.VMEM((labels, width), BF16)],
        vmem=12,
        flops=2 * samples * width * labels,
        nbytes=5_000_000,
    )
    tile = min(256, samples)

    def grad_enc_after(value):
        return pl.pallas_call(
            enc_kernel,
            grid=(samples // tile,),
            out_shape=[shape((samples, width), F32), shape((8, 128), F32)],
            in_specs=[
                pl.BlockSpec((tile, width), lambda i: (i, 0)),
                pl.BlockSpec((width, width), lambda i: (0, 0)),
                ANY,
            ],
            out_specs=[
                pl.BlockSpec((tile, width), lambda i: (i, 0)),
                pl.BlockSpec((8, 128), lambda i: (0, 0)),
            ],
            compiler_params=pltpu.CompilerParams(vmem_limit_bytes=12 * MIB),
            cost_estimate=pl.CostEstimate(
                flops=2 * samples * width * width, bytes_accessed=6_000_000, transcendentals=0
            ),
        )(grad_hidden, proj, value)

    if row_blocks > 1:
        cut = size // 2
        total, upper = call(
            combine_kernel,
            [shape((cut, width), F32), shape((cut, width), BF16)],
            [own] + received,
            after=[grad_hidden],
            nbytes=2_000_000,
        )
        span = row_blocks // 2
        grad_enc, enc_done = grad_enc_after(upper)
        total = total + gate(swap(upper, "dp", span), enc_done).astype(F32)
        while span > 1:
            cut = span // 2 * depth
            total = total[:cut] + swap(total[cut:].astype(BF16), "dp", span // 2).astype(F32)
            span //= 2
    else:
        total = own
        for value in received:
            total = total + value.astype(F32)
        grad_enc, enc_done = grad_enc_after(total)
    total = total.astype(BF16)
    if planes > 1:
        other = swap(total, "dp", planes // 2)
        total = (total.astype(F32) + other.astype(F32)).astype(BF16)
    parts = {0: total}
    span = 1
    while span < row_blocks:
        for r in range(span):
            parts[r + span] = swap(parts[r], "dp", span)
        span *= 2
    proj_slice = lax.dynamic_slice_in_dim(proj, z * (width // planes), width // planes, 1)
    (whole,) = call(
        whole_kernel,
        [shape((width, size), BF16)],
        [parts[r] for r in range(row_blocks)],
        scalars=[z_s],
        scratch=[pltpu.VMEM((size, width), BF16)],
        vmem=4,
    )
    rows, grad_head = pl.pallas_call(
        head_kernel,
        out_shape=[shape((labels, width), BF16), shape((width // planes, size), F32)],
        in_specs=[ANY, VMEM, VMEM],
        out_specs=[VMEM, VMEM],
        scratch_shapes=[pltpu.SemaphoreType.DMA],
        compiler_params=pltpu.CompilerParams(vmem_limit_bytes=4 * MIB),
        cost_estimate=pl.CostEstimate(
            flops=2 * size * width * width // planes, bytes_accessed=3_000_000, transcendentals=0
        ),
    )(rows, whole, proj_slice)
    have = {0: whole}
    for g in near + far:
        have[2 * g] = gate(swap(whole, "label", 2 * g), rows)
    for distance in list(have):
        have[distance + 1] = swap(have[distance], "label", 1)
    cuts = 4
    grad_proj = pl.pallas_call(
        functools.partial(proj_kernel, cuts),
        out_shape=shape((width, width), F32),
        in_specs=[SMEM] + [VMEM] * (owners + 1),
        out_specs=ANY,
        scratch_shapes=[
            pltpu.VMEM((width, labels), BF16),
            pltpu.VMEM((width, width), F32),
            pltpu.SemaphoreType.DMA((cuts,)),
        ],
        compiler_params=pltpu.CompilerParams(vmem_limit_bytes=16 * MIB),
        cost_estimate=pl.CostEstimate(
            flops=2 * labels * width * width, bytes_accessed=6_000_000, transcendentals=0
        ),
    )(me_s, *[have[distance] for distance in range(owners)], rows)
    return (grad_enc, grad_proj, grad_head.T)


def solution(mesh):
    placed = (
        P(("dp", "label"), None),
        P(),
        P("label", None),
        P(("dp", "label"), None),
        P(("dp", "label"), None),
        P("label"),
        P("label"),
    )
    return jax.shard_map(
        shards,
        mesh=mesh,
        in_specs=placed,
        out_specs=(P(("dp", "label"), None), P(), P("label", "dp")),
        check_vma=False,
    )
```

```python
import functools

import jax
import jax.numpy as jnp
from jax import lax
from jax.experimental import pallas as pl
from jax.experimental.pallas import tpu as pltpu
from jax.sharding import PartitionSpec as P

BF16 = jnp.bfloat16
F32 = jnp.float32
VMEM = pl.BlockSpec(memory_space=pltpu.VMEM)
SMEM = pl.BlockSpec(memory_space=pltpu.SMEM)
ANY = pl.BlockSpec(memory_space=pl.ANY)
MIB = 1024 * 1024
TAIL = 16
NN = (((1,), (0,)), ((), ()))
NT = (((1,), (1,)), ((), ()))
TN = (((0,), (0,)), ((), ()))


def dot(left, right, dims):
    return lax.dot_general(left, right, dims, preferred_element_type=F32)


def shape(dims, dtype):
    return jax.ShapeDtypeStruct(dims, dtype)


def call(kernel, outs, args, scalars=(), after=(), scratch=(), vmem=8, flops=0, nbytes=0):
    return pl.pallas_call(
        kernel,
        out_shape=outs,
        in_specs=[SMEM] * len(scalars) + [VMEM] * len(args) + [ANY] * len(after),
        out_specs=[VMEM] * len(outs),
        scratch_shapes=list(scratch),
        compiler_params=pltpu.CompilerParams(vmem_limit_bytes=vmem * MIB),
        cost_estimate=pl.CostEstimate(flops=flops, bytes_accessed=nbytes, transcendentals=0),
    )(*scalars, *args, *after)


def gate(value, *after):
    return pl.pallas_call(
        lambda value_ref, *refs: None,
        out_shape=shape(value.shape, value.dtype),
        in_specs=[ANY] * (1 + len(after)),
        out_specs=ANY,
        input_output_aliases={0: 0},
        compiler_params=pltpu.CompilerParams(vmem_limit_bytes=MIB),
    )(value, *after)


def swap(value, axis, distance):
    size = lax.axis_size(axis)
    return lax.ppermute(value, axis, [(i, i ^ distance) for i in range(size)])


def payload_kernel(num_hbm, den_hbm, rows_hbm, out_ref, num_ref, den_ref, sems):
    size, width = rows_hbm.shape
    copies = [
        pltpu.make_async_copy(num_hbm, num_ref, sems.at[0]),
        pltpu.make_async_copy(den_hbm, den_ref, sems.at[1]),
        pltpu.make_async_copy(rows_hbm, out_ref.at[pl.ds(0, size), :], sems.at[2]),
    ]
    for copy in copies:
        copy.start()
    out_ref[size:, size:] = jnp.zeros((TAIL, width - size), BF16)
    copies[0].wait()
    copies[1].wait()
    row = lax.broadcasted_iota(jnp.int32, (TAIL, size), 0)
    both = jnp.where(row == 0, num_ref[...], den_ref[...])
    out_ref[size:, :size] = both.astype(F32).astype(BF16)
    copies[2].wait()


def target_kernel(beam, block, wanted_ref, target_ref):
    samples = wanted_ref.shape[1]
    size = target_ref.shape[0] // beam
    label_iota = lax.broadcasted_iota(jnp.int32, (size, block), 0)
    for low in range(0, samples, block):
        for place in range(beam):
            labels = label_iota + place * size
            target = labels == wanted_ref[0:1, low : low + block]
            for column in range(1, wanted_ref.shape[0]):
                target = target | (labels == wanted_ref[column : column + 1, low : low + block])
            target_ref[place * size : (place + 1) * size, low : low + block] = jnp.where(
                target, 1.0, 0.0
            ).astype(BF16)


def inputs_kernel(enc_ref, proj_ref, after_ref, hidden_t_ref):
    samples = enc_ref.shape[0]
    tile = min(256, samples)
    for start in range(0, samples, tile):
        hidden = dot(enc_ref[start : start + tile, :], proj_ref[...], NN).astype(BF16)
        hidden_t_ref[:, start : start + tile] = hidden.T


def logistic(value):
    bottom = 1.0 + jnp.exp(-jnp.maximum(value, -80.0))
    guess = pl.reciprocal(bottom, approx=True)
    return guess * (2.0 - bottom * guess)


def score_kernel(group, block, count, list_ref, me_ref, z_ref, hidden_t_ref, target_ref, enc_ref, *refs):
    payloads, refs = refs[:2], refs[-6:]
    grads_ref, kept_ref, sent_ref, weights_ref, scale_ref, logits_ref = refs
    samples = enc_ref.shape[0]
    size = payloads[0].shape[0] - TAIL
    for core in range(2):
        rows = pl.ds(core * size, size)
        weights_ref[rows, :] = payloads[core][:size, :]
        tail = payloads[core][size:, :size].astype(F32)
        ratio = tail[0:1, :] / tail[1:2, :]
        scale_ref[rows, :] = jnp.broadcast_to(ratio, (block, size)).T
    tile = min(2 * block, samples)
    for start in range(0, samples, tile):
        logits_ref[:, start : start + tile] = dot(
            weights_ref[...], hidden_t_ref[:, start : start + tile], NN
        )
        for low in range(start, start + tile, block):
            for core in range(2):
                cluster = me_ref[0] ^ (2 * group + core)
                place = jnp.int32(-1)
                for beam_slot in range(list_ref.shape[0]):
                    place = jnp.where(list_ref[beam_slot, low // block] == cluster, beam_slot, place)
                factor = jnp.where(place >= 0, 1.0 / block, 0.0)
                first = pl.multiple_of(jnp.maximum(place, 0) * size, size)
                rows = slice(core * size, (core + 1) * size)
                target = target_ref[pl.ds(first, size), low : low + block].astype(F32)
                share = logistic(logits_ref[rows, low : low + block]) - target
                grads_ref[rows, low : low + block] = (scale_ref[rows, :] * factor * share).astype(BF16)
    outer = dot(grads_ref[...], enc_ref[...], NN)
    depth = size // count
    for r in range(count):
        rows = pl.ds(pl.multiple_of((z_ref[0] ^ r) * depth, depth), depth)
        kept_ref[rows, :] = outer[r * depth : (r + 1) * depth, :]
        sent_ref[rows, :] = outer[size + r * depth : size + (r + 1) * depth, :].astype(BF16)


def hidden_kernel(owners, me_ref, *refs):
    chips = owners // 2
    grads, payloads, refs = refs[:chips], refs[chips : chips + owners], refs[chips + owners :]
    out_ref, rows_ref, weights_ref = refs[-3:]
    size = payloads[0].shape[0] - TAIL
    for slot in range(owners):
        piece = payloads[slot][:size, :]
        start = pl.multiple_of((me_ref[0] ^ slot) * size, size)
        rows_ref[pl.ds(start, size), :] = piece
        weights_ref[slot * size : (slot + 1) * size, :] = piece
    samples = out_ref.shape[0]
    tile = min(256, samples)
    for low in range(0, samples, tile):
        total = jnp.zeros((tile, out_ref.shape[1]), F32)
        for group in range(chips):
            rows = weights_ref[2 * group * size : 2 * (group + 1) * size, :]
            total = total + dot(grads[group][:, low : low + tile], rows, TN)
        out_ref[low : low + tile, :] = total.astype(BF16)


def enc_kernel(grad_hidden_ref, proj_ref, after_ref, out_ref, done_ref):
    out_ref[...] = dot(grad_hidden_ref[...], proj_ref[...], NT)
    done_ref[...] = jnp.zeros_like(done_ref)


def combine_kernel(own_ref, *refs):
    *received, after_ref, kept_ref, sent_ref = refs
    cut = kept_ref.shape[0]
    for rows, out_ref in ((slice(cut, None), sent_ref), (slice(0, cut), kept_ref)):
        total = own_ref[rows, :]
        for ref in received:
            total = total + ref[rows, :].astype(F32)
        out_ref[...] = total.astype(out_ref.dtype)


def whole_kernel(z_ref, *refs):
    *parts, whole_ref, rows_ref = refs
    depth = parts[0].shape[0]
    for r, part in enumerate(parts):
        rows_ref[pl.ds(pl.multiple_of((z_ref[0] ^ r) * depth, depth), depth), :] = part[...]
    whole_ref[...] = rows_ref[...].T


def head_kernel(rows_any, whole_ref, slice_ref, rows_ref, head_ref, sem):
    copy = pltpu.make_async_copy(rows_any, rows_ref, sem)
    copy.start()
    head_ref[...] = dot(slice_ref[...], whole_ref[...], TN)
    copy.wait()


def proj_kernel(cuts, me_ref, *refs):
    *parts, rows_ref, out_hbm, outer_ref, done_ref, sems = refs
    width, size = parts[0].shape
    for distance, part in enumerate(parts):
        start = pl.multiple_of((me_ref[0] ^ distance) * size, size)
        outer_ref[:, pl.ds(start, size)] = part[...]
    height = width // cuts
    copies = []
    for cut in range(cuts):
        rows = pl.ds(cut * height, height)
        done_ref[rows, :] = dot(outer_ref[rows, :], rows_ref[...], NN)
        copy = pltpu.make_async_copy(done_ref.at[rows, :], out_hbm.at[rows, :], sems.at[cut])
        copy.start()
        copies.append(copy)
    for copy in copies:
        copy.wait()


def shards(enc, proj, head_weight, shortlist, positives, weight_num, weight_den):
    owners, planes = lax.axis_size("label"), lax.axis_size("dp")
    chips = owners // 2
    near = [g for g in range(1, chips) if g & (g - 1) == 0]
    far = [g for g in range(1, chips) if g & (g - 1) != 0]
    row_blocks = max(1, planes // 2)
    me = lax.axis_index("label").astype(jnp.int32)
    z = lax.axis_index("dp").astype(jnp.int32)
    z_low = z & (row_blocks - 1)
    blocks, beam = shortlist.shape
    samples, width = enc.shape
    block = samples // blocks
    size = head_weight.shape[0]
    labels = owners * size
    depth = size // row_blocks
    me_s, z_s = me.reshape(1), z_low.reshape(1)
    listed = shortlist.astype(jnp.int32).T

    payload = pl.pallas_call(
        payload_kernel,
        out_shape=shape((size + TAIL, width), BF16),
        in_specs=[ANY] * 3,
        out_specs=VMEM,
        scratch_shapes=[pltpu.VMEM((1, size), jnp.int32)] * 2 + [pltpu.SemaphoreType.DMA((3,))],
        compiler_params=pltpu.CompilerParams(vmem_limit_bytes=56 * MIB),
    )(weight_num.reshape(1, size), weight_den.reshape(1, size), head_weight)
    got = {0: payload}
    for g in near + far:
        got[2 * g] = swap(payload, "label", 2 * g)
    got[1] = swap(payload, "label", 1)
    (target,) = call(
        functools.partial(target_kernel, beam, block),
        [shape((beam * size, samples), BF16)],
        [positives.T],
        vmem=2,
        nbytes=8_000_000,
    )
    (hidden_t,) = call(
        inputs_kernel,
        [shape((width, samples), BF16)],
        [enc, proj],
        after=[target],
        flops=2 * samples * width * width,
        nbytes=6_000_000,
    )
    for g in near:
        got[2 * g] = gate(got[2 * g], hidden_t)
        got[2 * g + 1] = swap(got[2 * g], "label", 1)
    grads, kept, from_core, moved, received = {}, {}, {}, {}, {}
    order = [0] + near + far
    for at, g in enumerate(order):
        after = [got[2 * n] for n in near] if at == 0 else [grads[order[at - 1]]]
        if at and at + 1 < len(order):
            after.append(got[2 * order[at + 1]])
        if at >= 3:
            after.append(moved[order[at - 2]])
        grads[g], kept[g], sent = call(
            functools.partial(score_kernel, g, block, row_blocks),
            [shape((2 * size, samples), BF16), shape((size, width), F32), shape((size, width), BF16)],
            [hidden_t, target, enc, got[2 * g], got[2 * g + 1]],
            scalars=[listed, me_s, z_s],
            after=after,
            scratch=[
                pltpu.VMEM((2 * size, width), BF16),
                pltpu.VMEM((2 * size, block), F32),
                pltpu.VMEM((2 * size, samples), F32),
            ],
            flops=8 * samples * size * width,
            nbytes=5_000_000,
        )
        for ahead in [n for n in order[at + 2 : at + 3] if n in far]:
            got[2 * ahead] = gate(got[2 * ahead], grads[g])
            got[2 * ahead + 1] = swap(got[2 * ahead], "label", 1)
        from_core[g] = swap(sent, "label", 1)
        if g:
            moved[g] = (kept[g] + from_core[g].astype(F32)).astype(BF16)
            received[g] = swap(moved[g], "label", 2 * g)
    own = kept[0] + from_core[0].astype(F32)
    received = [received[g] for g in near + far]

    grad_hidden, rows = call(
        functools.partial(hidden_kernel, owners),
        [shape((samples, width), BF16), shape((labels, width), BF16)],
        [grads[g] for g in range(chips)] + [got[d] for d in range(owners)],
        scalars=[me_s],
        after=[moved[g] for g in near + far],
        scratch=[pltpu.VMEM((labels, width), BF16)],
        vmem=12,
        flops=2 * samples * width * labels,
        nbytes=5_000_000,
    )
    tile = min(256, samples)

    def grad_enc_after(value):
        return pl.pallas_call(
            enc_kernel,
            grid=(samples // tile,),
            out_shape=[shape((samples, width), F32), shape((8, 128), F32)],
            in_specs=[
                pl.BlockSpec((tile, width), lambda i: (i, 0)),
                pl.BlockSpec((width, width), lambda i: (0, 0)),
                ANY,
            ],
            out_specs=[
                pl.BlockSpec((tile, width), lambda i: (i, 0)),
                pl.BlockSpec((8, 128), lambda i: (0, 0)),
            ],
            compiler_params=pltpu.CompilerParams(vmem_limit_bytes=12 * MIB),
            cost_estimate=pl.CostEstimate(
                flops=2 * samples * width * width, bytes_accessed=6_000_000, transcendentals=0
            ),
        )(grad_hidden, proj, value)

    if row_blocks > 1:
        cut = size // 2
        total, upper = call(
            combine_kernel,
            [shape((cut, width), F32), shape((cut, width), BF16)],
            [own] + received,
            after=[grad_hidden],
            nbytes=2_000_000,
        )
        span = row_blocks // 2
        total = total + swap(upper, "dp", span).astype(F32)
        while span > 1:
            cut = span // 2 * depth
            total = total[:cut] + swap(total[cut:].astype(BF16), "dp", span // 2).astype(F32)
            span //= 2
    else:
        total = own
        for value in received:
            total = total + value.astype(F32)
    total = total.astype(BF16)
    grad_enc, enc_done = grad_enc_after(total)
    if planes > 1:
        other = gate(swap(total, "dp", planes // 2), enc_done)
        total = (total.astype(F32) + other.astype(F32)).astype(BF16)
    parts = {0: total}
    span = 1
    while span < row_blocks:
        for r in range(span):
            parts[r + span] = swap(parts[r], "dp", span)
        span *= 2
    proj_slice = lax.dynamic_slice_in_dim(proj, z * (width // planes), width // planes, 1)
    (whole,) = call(
        whole_kernel,
        [shape((width, size), BF16)],
        [parts[r] for r in range(row_blocks)],
        scalars=[z_s],
        scratch=[pltpu.VMEM((size, width), BF16)],
        vmem=4,
    )
    rows, grad_head = pl.pallas_call(
        head_kernel,
        out_shape=[shape((labels, width), BF16), shape((width // planes, size), F32)],
        in_specs=[ANY, VMEM, VMEM],
        out_specs=[VMEM, VMEM],
        scratch_shapes=[pltpu.SemaphoreType.DMA],
        compiler_params=pltpu.CompilerParams(vmem_limit_bytes=4 * MIB),
        cost_estimate=pl.CostEstimate(
            flops=2 * size * width * width // planes, bytes_accessed=3_000_000, transcendentals=0
        ),
    )(rows, whole, proj_slice)
    have = {0: whole}
    for g in near + far:
        have[2 * g] = gate(swap(whole, "label", 2 * g), rows)
    for distance in list(have):
        have[distance + 1] = swap(have[distance], "label", 1)
    cuts = 4
    grad_proj = pl.pallas_call(
        functools.partial(proj_kernel, cuts),
        out_shape=shape((width, width), F32),
        in_specs=[SMEM] + [VMEM] * (owners + 1),
        out_specs=ANY,
        scratch_shapes=[
            pltpu.VMEM((width, labels), BF16),
            pltpu.VMEM((width, width), F32),
            pltpu.SemaphoreType.DMA((cuts,)),
        ],
        compiler_params=pltpu.CompilerParams(vmem_limit_bytes=16 * MIB),
        cost_estimate=pl.CostEstimate(
            flops=2 * labels * width * width, bytes_accessed=6_000_000, transcendentals=0
        ),
    )(me_s, *[have[distance] for distance in range(owners)], rows)
    return (grad_enc, grad_proj, grad_head.T)


def solution(mesh):
    placed = (
        P(("dp", "label"), None),
        P(),
        P("label", None),
        P(("dp", "label"), None),
        P(("dp", "label"), None),
        P("label"),
        P("label"),
    )
    return jax.shard_map(
        shards,
        mesh=mesh,
        in_specs=placed,
        out_specs=(P(("dp", "label"), None), P(), P("label", "dp")),
        check_vma=False,
    )
```

```python
import functools

import jax
import jax.numpy as jnp
from jax import lax
from jax.experimental import pallas as pl
from jax.experimental.pallas import tpu as pltpu
from jax.sharding import PartitionSpec as P

BF16 = jnp.bfloat16
F32 = jnp.float32
VMEM = pl.BlockSpec(memory_space=pltpu.VMEM)
SMEM = pl.BlockSpec(memory_space=pltpu.SMEM)
ANY = pl.BlockSpec(memory_space=pl.ANY)
MIB = 1024 * 1024
TAIL = 16
NN = (((1,), (0,)), ((), ()))
NT = (((1,), (1,)), ((), ()))
TN = (((0,), (0,)), ((), ()))


def dot(left, right, dims):
    return lax.dot_general(left, right, dims, preferred_element_type=F32)


def shape(dims, dtype):
    return jax.ShapeDtypeStruct(dims, dtype)


def call(kernel, outs, args, scalars=(), after=(), scratch=(), vmem=8, flops=0, nbytes=0):
    return pl.pallas_call(
        kernel,
        out_shape=outs,
        in_specs=[SMEM] * len(scalars) + [VMEM] * len(args) + [ANY] * len(after),
        out_specs=[VMEM] * len(outs),
        scratch_shapes=list(scratch),
        compiler_params=pltpu.CompilerParams(vmem_limit_bytes=vmem * MIB),
        cost_estimate=pl.CostEstimate(flops=flops, bytes_accessed=nbytes, transcendentals=0),
    )(*scalars, *args, *after)


def gate(value, *after):
    return pl.pallas_call(
        lambda value_ref, *refs: None,
        out_shape=shape(value.shape, value.dtype),
        in_specs=[ANY] * (1 + len(after)),
        out_specs=ANY,
        input_output_aliases={0: 0},
        compiler_params=pltpu.CompilerParams(vmem_limit_bytes=MIB),
    )(value, *after)


def swap(value, axis, distance):
    size = lax.axis_size(axis)
    return lax.ppermute(value, axis, [(i, i ^ distance) for i in range(size)])


def payload_kernel(num_hbm, den_hbm, rows_hbm, out_ref, num_ref, den_ref, sems):
    size, width = rows_hbm.shape
    copies = [
        pltpu.make_async_copy(num_hbm, num_ref, sems.at[0]),
        pltpu.make_async_copy(den_hbm, den_ref, sems.at[1]),
        pltpu.make_async_copy(rows_hbm, out_ref.at[pl.ds(0, size), :], sems.at[2]),
    ]
    for copy in copies:
        copy.start()
    out_ref[size:, size:] = jnp.zeros((TAIL, width - size), BF16)
    copies[0].wait()
    copies[1].wait()
    row = lax.broadcasted_iota(jnp.int32, (TAIL, size), 0)
    both = jnp.where(row == 0, num_ref[...], den_ref[...])
    out_ref[size:, :size] = both.astype(F32).astype(BF16)
    copies[2].wait()


def target_kernel(beam, block, wanted_ref, target_ref):
    samples = wanted_ref.shape[1]
    size = target_ref.shape[0] // beam
    label_iota = lax.broadcasted_iota(jnp.int32, (size, block), 0)
    for low in range(0, samples, block):
        for place in range(beam):
            labels = label_iota + place * size
            target = labels == wanted_ref[0:1, low : low + block]
            for column in range(1, wanted_ref.shape[0]):
                target = target | (labels == wanted_ref[column : column + 1, low : low + block])
            target_ref[place * size : (place + 1) * size, low : low + block] = jnp.where(
                target, 1.0, 0.0
            ).astype(BF16)


def inputs_kernel(enc_ref, proj_ref, after_ref, hidden_t_ref):
    samples = enc_ref.shape[0]
    tile = min(256, samples)
    for start in range(0, samples, tile):
        hidden = dot(enc_ref[start : start + tile, :], proj_ref[...], NN).astype(BF16)
        hidden_t_ref[:, start : start + tile] = hidden.T


def logistic(value):
    bottom = 1.0 + jnp.exp(-jnp.maximum(value, -80.0))
    guess = pl.reciprocal(bottom, approx=True)
    return guess * (2.0 - bottom * guess)


def score_kernel(group, block, count, list_ref, me_ref, z_ref, hidden_t_ref, target_ref, enc_ref, *refs):
    payloads, refs = refs[:2], refs[-6:]
    grads_ref, kept_ref, sent_ref, weights_ref, scale_ref, logits_ref = refs
    samples = enc_ref.shape[0]
    size = payloads[0].shape[0] - TAIL
    for core in range(2):
        rows = pl.ds(core * size, size)
        weights_ref[rows, :] = payloads[core][:size, :]
        tail = payloads[core][size:, :size].astype(F32)
        ratio = tail[0:1, :] / tail[1:2, :]
        scale_ref[rows, :] = jnp.broadcast_to(ratio, (block, size)).T
    tile = min(2 * block, samples)
    for start in range(0, samples, tile):
        logits_ref[:, start : start + tile] = dot(
            weights_ref[...], hidden_t_ref[:, start : start + tile], NN
        )
        for low in range(start, start + tile, block):
            for core in range(2):
                cluster = me_ref[0] ^ (2 * group + core)
                place = jnp.int32(-1)
                for beam_slot in range(list_ref.shape[0]):
                    place = jnp.where(list_ref[beam_slot, low // block] == cluster, beam_slot, place)
                factor = jnp.where(place >= 0, 1.0 / block, 0.0)
                first = pl.multiple_of(jnp.maximum(place, 0) * size, size)
                rows = slice(core * size, (core + 1) * size)
                target = target_ref[pl.ds(first, size), low : low + block].astype(F32)
                share = logistic(logits_ref[rows, low : low + block]) - target
                grads_ref[rows, low : low + block] = (scale_ref[rows, :] * factor * share).astype(BF16)
    outer = dot(grads_ref[...], enc_ref[...], NN)
    depth = size // count
    for r in range(count):
        rows = pl.ds(pl.multiple_of((z_ref[0] ^ r) * depth, depth), depth)
        kept_ref[rows, :] = outer[r * depth : (r + 1) * depth, :]
        sent_ref[rows, :] = outer[size + r * depth : size + (r + 1) * depth, :].astype(BF16)


def hidden_kernel(owners, me_ref, *refs):
    chips = owners // 2
    grads, payloads, refs = refs[:chips], refs[chips : chips + owners], refs[chips + owners :]
    out_ref, rows_ref, weights_ref = refs[-3:]
    size = payloads[0].shape[0] - TAIL
    for slot in range(owners):
        piece = payloads[slot][:size, :]
        start = pl.multiple_of((me_ref[0] ^ slot) * size, size)
        rows_ref[pl.ds(start, size), :] = piece
        weights_ref[slot * size : (slot + 1) * size, :] = piece
    samples = out_ref.shape[0]
    tile = min(256, samples)
    for low in range(0, samples, tile):
        total = jnp.zeros((tile, out_ref.shape[1]), F32)
        for group in range(chips):
            rows = weights_ref[2 * group * size : 2 * (group + 1) * size, :]
            total = total + dot(grads[group][:, low : low + tile], rows, TN)
        out_ref[low : low + tile, :] = total.astype(BF16)


def enc_kernel(grad_hidden_ref, proj_ref, after_ref, out_ref, done_ref):
    out_ref[...] = dot(grad_hidden_ref[...], proj_ref[...], NT)
    done_ref[...] = jnp.zeros_like(done_ref)


def combine_kernel(own_ref, *refs):
    *received, after_ref, kept_ref, sent_ref = refs
    cut = kept_ref.shape[0]
    for rows, out_ref in ((slice(cut, None), sent_ref), (slice(0, cut), kept_ref)):
        total = own_ref[rows, :]
        for ref in received:
            total = total + ref[rows, :].astype(F32)
        out_ref[...] = total.astype(out_ref.dtype)


def whole_kernel(z_ref, *refs):
    *parts, whole_ref, rows_ref = refs
    depth = parts[0].shape[0]
    for r, part in enumerate(parts):
        rows_ref[pl.ds(pl.multiple_of((z_ref[0] ^ r) * depth, depth), depth), :] = part[...]
    whole_ref[...] = rows_ref[...].T


def head_kernel(rows_any, whole_ref, slice_ref, rows_ref, head_ref, sem):
    copy = pltpu.make_async_copy(rows_any, rows_ref, sem)
    copy.start()
    head_ref[...] = dot(slice_ref[...], whole_ref[...], TN)
    copy.wait()


def proj_kernel(cuts, me_ref, *refs):
    *parts, rows_ref, out_hbm, outer_ref, done_ref, sems = refs
    width, size = parts[0].shape
    for distance, part in enumerate(parts):
        start = pl.multiple_of((me_ref[0] ^ distance) * size, size)
        outer_ref[:, pl.ds(start, size)] = part[...]
    height = width // cuts
    copies = []
    for cut in range(cuts):
        rows = pl.ds(cut * height, height)
        done_ref[rows, :] = dot(outer_ref[rows, :], rows_ref[...], NN)
        copy = pltpu.make_async_copy(done_ref.at[rows, :], out_hbm.at[rows, :], sems.at[cut])
        copy.start()
        copies.append(copy)
    for copy in copies:
        copy.wait()


def shards(enc, proj, head_weight, shortlist, positives, weight_num, weight_den):
    owners, planes = lax.axis_size("label"), lax.axis_size("dp")
    chips = owners // 2
    near = [g for g in range(1, chips) if g & (g - 1) == 0]
    far = [g for g in range(1, chips) if g & (g - 1) != 0]
    row_blocks = max(1, planes // 2)
    me = lax.axis_index("label").astype(jnp.int32)
    z = lax.axis_index("dp").astype(jnp.int32)
    z_low = z & (row_blocks - 1)
    blocks, beam = shortlist.shape
    samples, width = enc.shape
    block = samples // blocks
    size = head_weight.shape[0]
    labels = owners * size
    depth = size // row_blocks
    me_s, z_s = me.reshape(1), z_low.reshape(1)
    listed = shortlist.astype(jnp.int32).T

    payload = pl.pallas_call(
        payload_kernel,
        out_shape=shape((size + TAIL, width), BF16),
        in_specs=[ANY] * 3,
        out_specs=VMEM,
        scratch_shapes=[pltpu.VMEM((1, size), jnp.int32)] * 2 + [pltpu.SemaphoreType.DMA((3,))],
        compiler_params=pltpu.CompilerParams(vmem_limit_bytes=56 * MIB),
    )(weight_num.reshape(1, size), weight_den.reshape(1, size), head_weight)
    got = {0: payload}
    for g in far + near:
        got[2 * g] = swap(payload, "label", 2 * g)
    got[1] = swap(payload, "label", 1)
    (target,) = call(
        functools.partial(target_kernel, beam, block),
        [shape((beam * size, samples), BF16)],
        [positives.T],
        vmem=2,
        nbytes=8_000_000,
    )
    (hidden_t,) = call(
        inputs_kernel,
        [shape((width, samples), BF16)],
        [enc, proj],
        after=[target],
        flops=2 * samples * width * width,
        nbytes=6_000_000,
    )
    grads, kept, from_core, moved, received = {}, {}, {}, {}, {}
    order = [0] + far + near
    for at, g in enumerate(order):
        after = [grads[order[at - 1]]] if at else []
        if at + 1 < len(order):
            ahead = 2 * order[at + 1]
            got[ahead] = gate(got[ahead], grads[order[at - 1]] if at else hidden_t)
            got[ahead + 1] = swap(got[ahead], "label", 1)
            after.append(got[ahead])
        if at >= 3:
            after.append(moved[order[at - 2]])
        grads[g], kept[g], sent = call(
            functools.partial(score_kernel, g, block, row_blocks),
            [shape((2 * size, samples), BF16), shape((size, width), F32), shape((size, width), BF16)],
            [hidden_t, target, enc, got[2 * g], got[2 * g + 1]],
            scalars=[listed, me_s, z_s],
            after=after,
            scratch=[
                pltpu.VMEM((2 * size, width), BF16),
                pltpu.VMEM((2 * size, block), F32),
                pltpu.VMEM((2 * size, samples), F32),
            ],
            flops=8 * samples * size * width,
            nbytes=5_000_000,
        )
        from_core[g] = swap(sent, "label", 1)
        if g:
            moved[g] = (kept[g] + from_core[g].astype(F32)).astype(BF16)
            received[g] = swap(moved[g], "label", 2 * g)
    own = kept[0] + from_core[0].astype(F32)
    received = [received[g] for g in far + near]

    grad_hidden, rows = call(
        functools.partial(hidden_kernel, owners),
        [shape((samples, width), BF16), shape((labels, width), BF16)],
        [grads[g] for g in range(chips)] + [got[d] for d in range(owners)],
        scalars=[me_s],
        after=[moved[g] for g in far + near],
        scratch=[pltpu.VMEM((labels, width), BF16)],
        vmem=12,
        flops=2 * samples * width * labels,
        nbytes=5_000_000,
    )
    tile = min(256, samples)

    def grad_enc_after(value):
        return pl.pallas_call(
            enc_kernel,
            grid=(samples // tile,),
            out_shape=[shape((samples, width), F32), shape((8, 128), F32)],
            in_specs=[
                pl.BlockSpec((tile, width), lambda i: (i, 0)),
                pl.BlockSpec((width, width), lambda i: (0, 0)),
                ANY,
            ],
            out_specs=[
                pl.BlockSpec((tile, width), lambda i: (i, 0)),
                pl.BlockSpec((8, 128), lambda i: (0, 0)),
            ],
            compiler_params=pltpu.CompilerParams(vmem_limit_bytes=12 * MIB),
            cost_estimate=pl.CostEstimate(
                flops=2 * samples * width * width, bytes_accessed=6_000_000, transcendentals=0
            ),
        )(grad_hidden, proj, value)

    if row_blocks > 1:
        cut = size // 2
        total, upper = call(
            combine_kernel,
            [shape((cut, width), F32), shape((cut, width), BF16)],
            [own] + received,
            after=[grad_hidden],
            nbytes=2_000_000,
        )
        span = row_blocks // 2
        total = total + swap(upper, "dp", span).astype(F32)
        while span > 1:
            cut = span // 2 * depth
            total = total[:cut] + swap(total[cut:].astype(BF16), "dp", span // 2).astype(F32)
            span //= 2
    else:
        total = own
        for value in received:
            total = total + value.astype(F32)
    total = total.astype(BF16)
    grad_enc, enc_done = grad_enc_after(total)
    if planes > 1:
        other = gate(swap(total, "dp", planes // 2), enc_done)
        total = (total.astype(F32) + other.astype(F32)).astype(BF16)
    parts = {0: total}
    span = 1
    while span < row_blocks:
        for r in range(span):
            parts[r + span] = swap(parts[r], "dp", span)
        span *= 2
    proj_slice = lax.dynamic_slice_in_dim(proj, z * (width // planes), width // planes, 1)
    (whole,) = call(
        whole_kernel,
        [shape((width, size), BF16)],
        [parts[r] for r in range(row_blocks)],
        scalars=[z_s],
        scratch=[pltpu.VMEM((size, width), BF16)],
        vmem=4,
    )
    rows, grad_head = pl.pallas_call(
        head_kernel,
        out_shape=[shape((labels, width), BF16), shape((width // planes, size), F32)],
        in_specs=[ANY, VMEM, VMEM],
        out_specs=[VMEM, VMEM],
        scratch_shapes=[pltpu.SemaphoreType.DMA],
        compiler_params=pltpu.CompilerParams(vmem_limit_bytes=4 * MIB),
        cost_estimate=pl.CostEstimate(
            flops=2 * size * width * width // planes, bytes_accessed=3_000_000, transcendentals=0
        ),
    )(rows, whole, proj_slice)
    have = {0: whole}
    for g in near + far:
        have[2 * g] = gate(swap(whole, "label", 2 * g), rows)
    for distance in list(have):
        have[distance + 1] = swap(have[distance], "label", 1)
    cuts = 4
    grad_proj = pl.pallas_call(
        functools.partial(proj_kernel, cuts),
        out_shape=shape((width, width), F32),
        in_specs=[SMEM] + [VMEM] * (owners + 1),
        out_specs=ANY,
        scratch_shapes=[
            pltpu.VMEM((width, labels), BF16),
            pltpu.VMEM((width, width), F32),
            pltpu.SemaphoreType.DMA((cuts,)),
        ],
        compiler_params=pltpu.CompilerParams(vmem_limit_bytes=16 * MIB),
        cost_estimate=pl.CostEstimate(
            flops=2 * labels * width * width, bytes_accessed=6_000_000, transcendentals=0
        ),
    )(me_s, *[have[distance] for distance in range(owners)], rows)
    return (grad_enc, grad_proj, grad_head.T)


def solution(mesh):
    placed = (
        P(("dp", "label"), None),
        P(),
        P("label", None),
        P(("dp", "label"), None),
        P(("dp", "label"), None),
        P("label"),
        P("label"),
    )
    return jax.shard_map(
        shards,
        mesh=mesh,
        in_specs=placed,
        out_specs=(P(("dp", "label"), None), P(), P("label", "dp")),
        check_vma=False,
    )
```

```python
import functools

import jax
import jax.numpy as jnp
from jax import lax
from jax.experimental import pallas as pl
from jax.experimental.pallas import tpu as pltpu
from jax.sharding import PartitionSpec as P

BF16 = jnp.bfloat16
F32 = jnp.float32
VMEM = pl.BlockSpec(memory_space=pltpu.VMEM)
SMEM = pl.BlockSpec(memory_space=pltpu.SMEM)
ANY = pl.BlockSpec(memory_space=pl.ANY)
MIB = 1024 * 1024
TAIL = 16
NN = (((1,), (0,)), ((), ()))
NT = (((1,), (1,)), ((), ()))
TN = (((0,), (0,)), ((), ()))


def dot(left, right, dims):
    return lax.dot_general(left, right, dims, preferred_element_type=F32)


def shape(dims, dtype):
    return jax.ShapeDtypeStruct(dims, dtype)


def call(kernel, outs, args, scalars=(), after=(), scratch=(), vmem=8, flops=0, nbytes=0):
    return pl.pallas_call(
        kernel,
        out_shape=outs,
        in_specs=[SMEM] * len(scalars) + [VMEM] * len(args) + [ANY] * len(after),
        out_specs=[VMEM] * len(outs),
        scratch_shapes=list(scratch),
        compiler_params=pltpu.CompilerParams(vmem_limit_bytes=vmem * MIB),
        cost_estimate=pl.CostEstimate(flops=flops, bytes_accessed=nbytes, transcendentals=0),
    )(*scalars, *args, *after)


def gate(value, *after):
    return pl.pallas_call(
        lambda value_ref, *refs: None,
        out_shape=shape(value.shape, value.dtype),
        in_specs=[ANY] * (1 + len(after)),
        out_specs=ANY,
        input_output_aliases={0: 0},
        compiler_params=pltpu.CompilerParams(vmem_limit_bytes=MIB),
    )(value, *after)


def swap(value, axis, distance):
    size = lax.axis_size(axis)
    return lax.ppermute(value, axis, [(i, i ^ distance) for i in range(size)])


def payload_kernel(num_hbm, den_hbm, rows_hbm, out_ref, num_ref, den_ref, sems):
    size, width = rows_hbm.shape
    copies = [
        pltpu.make_async_copy(num_hbm, num_ref, sems.at[0]),
        pltpu.make_async_copy(den_hbm, den_ref, sems.at[1]),
        pltpu.make_async_copy(rows_hbm, out_ref.at[pl.ds(0, size), :], sems.at[2]),
    ]
    for copy in copies:
        copy.start()
    out_ref[size:, size:] = jnp.zeros((TAIL, width - size), BF16)
    copies[0].wait()
    copies[1].wait()
    row = lax.broadcasted_iota(jnp.int32, (TAIL, size), 0)
    both = jnp.where(row == 0, num_ref[...], den_ref[...])
    out_ref[size:, :size] = both.astype(F32).astype(BF16)
    copies[2].wait()


def target_kernel(beam, block, wanted_ref, after_ref, target_ref):
    samples = wanted_ref.shape[1]
    size = target_ref.shape[0] // beam
    label_iota = lax.broadcasted_iota(jnp.int32, (size, block), 0)
    for low in range(0, samples, block):
        for place in range(beam):
            labels = label_iota + place * size
            target = labels == wanted_ref[0:1, low : low + block]
            for column in range(1, wanted_ref.shape[0]):
                target = target | (labels == wanted_ref[column : column + 1, low : low + block])
            target_ref[place * size : (place + 1) * size, low : low + block] = jnp.where(
                target, 1.0, 0.0
            ).astype(BF16)


def inputs_kernel(enc_ref, proj_ref, hidden_t_ref):
    samples = enc_ref.shape[0]
    tile = min(256, samples)
    for start in range(0, samples, tile):
        hidden = dot(enc_ref[start : start + tile, :], proj_ref[...], NN).astype(BF16)
        hidden_t_ref[:, start : start + tile] = hidden.T


def logistic(value):
    bottom = 1.0 + jnp.exp(-jnp.maximum(value, -80.0))
    guess = pl.reciprocal(bottom, approx=True)
    return guess * (2.0 - bottom * guess)


def score_kernel(group, block, count, list_ref, me_ref, z_ref, hidden_t_ref, target_ref, enc_ref, *refs):
    payloads, refs = refs[:2], refs[-6:]
    grads_ref, kept_ref, sent_ref, weights_ref, scale_ref, logits_ref = refs
    samples = enc_ref.shape[0]
    size = payloads[0].shape[0] - TAIL
    for core in range(2):
        rows = pl.ds(core * size, size)
        weights_ref[rows, :] = payloads[core][:size, :]
        tail = payloads[core][size:, :size].astype(F32)
        ratio = tail[0:1, :] / tail[1:2, :]
        scale_ref[rows, :] = jnp.broadcast_to(ratio, (block, size)).T
    tile = min(2 * block, samples)
    for start in range(0, samples, tile):
        logits_ref[:, start : start + tile] = dot(
            weights_ref[...], hidden_t_ref[:, start : start + tile], NN
        )
        for low in range(start, start + tile, block):
            for core in range(2):
                cluster = me_ref[0] ^ (2 * group + core)
                place = jnp.int32(-1)
                for beam_slot in range(list_ref.shape[0]):
                    place = jnp.where(list_ref[beam_slot, low // block] == cluster, beam_slot, place)
                factor = jnp.where(place >= 0, 1.0 / block, 0.0)
                first = pl.multiple_of(jnp.maximum(place, 0) * size, size)
                rows = slice(core * size, (core + 1) * size)
                target = target_ref[pl.ds(first, size), low : low + block].astype(F32)
                share = logistic(logits_ref[rows, low : low + block]) - target
                grads_ref[rows, low : low + block] = (scale_ref[rows, :] * factor * share).astype(BF16)
    outer = dot(grads_ref[...], enc_ref[...], NN)
    depth = size // count
    for r in range(count):
        rows = pl.ds(pl.multiple_of((z_ref[0] ^ r) * depth, depth), depth)
        kept_ref[rows, :] = outer[r * depth : (r + 1) * depth, :]
        sent_ref[rows, :] = outer[size + r * depth : size + (r + 1) * depth, :].astype(BF16)


def hidden_kernel(owners, me_ref, *refs):
    chips = owners // 2
    grads, payloads, refs = refs[:chips], refs[chips : chips + owners], refs[chips + owners :]
    out_ref, rows_ref, weights_ref = refs[-3:]
    size = payloads[0].shape[0] - TAIL
    for slot in range(owners):
        piece = payloads[slot][:size, :]
        start = pl.multiple_of((me_ref[0] ^ slot) * size, size)
        rows_ref[pl.ds(start, size), :] = piece
        weights_ref[slot * size : (slot + 1) * size, :] = piece
    samples = out_ref.shape[0]
    tile = min(256, samples)
    for low in range(0, samples, tile):
        total = jnp.zeros((tile, out_ref.shape[1]), F32)
        for group in range(chips):
            rows = weights_ref[2 * group * size : 2 * (group + 1) * size, :]
            total = total + dot(grads[group][:, low : low + tile], rows, TN)
        out_ref[low : low + tile, :] = total.astype(BF16)


def enc_kernel(grad_hidden_ref, proj_ref, after_ref, out_ref, done_ref):
    out_ref[...] = dot(grad_hidden_ref[...], proj_ref[...], NT)
    done_ref[...] = jnp.zeros_like(done_ref)


def combine_kernel(own_ref, *refs):
    *received, after_ref, kept_ref, sent_ref = refs
    cut = kept_ref.shape[0]
    for rows, out_ref in ((slice(cut, None), sent_ref), (slice(0, cut), kept_ref)):
        total = own_ref[rows, :]
        for ref in received:
            total = total + ref[rows, :].astype(F32)
        out_ref[...] = total.astype(out_ref.dtype)


def whole_kernel(z_ref, *refs):
    *parts, whole_ref, rows_ref = refs
    depth = parts[0].shape[0]
    for r, part in enumerate(parts):
        rows_ref[pl.ds(pl.multiple_of((z_ref[0] ^ r) * depth, depth), depth), :] = part[...]
    whole_ref[...] = rows_ref[...].T


def head_kernel(rows_any, whole_ref, slice_ref, rows_ref, head_ref, sem):
    copy = pltpu.make_async_copy(rows_any, rows_ref, sem)
    copy.start()
    head_ref[...] = dot(slice_ref[...], whole_ref[...], TN)
    copy.wait()


def proj_kernel(cuts, me_ref, *refs):
    *parts, rows_ref, out_hbm, outer_ref, done_ref, sems = refs
    width, size = parts[0].shape
    for distance, part in enumerate(parts):
        start = pl.multiple_of((me_ref[0] ^ distance) * size, size)
        outer_ref[:, pl.ds(start, size)] = part[...]
    height = width // cuts
    copies = []
    for cut in range(cuts):
        rows = pl.ds(cut * height, height)
        done_ref[rows, :] = dot(outer_ref[rows, :], rows_ref[...], NN)
        copy = pltpu.make_async_copy(done_ref.at[rows, :], out_hbm.at[rows, :], sems.at[cut])
        copy.start()
        copies.append(copy)
    for copy in copies:
        copy.wait()


def shards(enc, proj, head_weight, shortlist, positives, weight_num, weight_den):
    owners, planes = lax.axis_size("label"), lax.axis_size("dp")
    chips = owners // 2
    near = [g for g in range(1, chips) if g & (g - 1) == 0]
    far = [g for g in range(1, chips) if g & (g - 1) != 0]
    row_blocks = max(1, planes // 2)
    me = lax.axis_index("label").astype(jnp.int32)
    z = lax.axis_index("dp").astype(jnp.int32)
    z_low = z & (row_blocks - 1)
    blocks, beam = shortlist.shape
    samples, width = enc.shape
    block = samples // blocks
    size = head_weight.shape[0]
    labels = owners * size
    depth = size // row_blocks
    me_s, z_s = me.reshape(1), z_low.reshape(1)
    listed = shortlist.astype(jnp.int32).T

    payload = pl.pallas_call(
        payload_kernel,
        out_shape=shape((size + TAIL, width), BF16),
        in_specs=[ANY] * 3,
        out_specs=VMEM,
        scratch_shapes=[pltpu.VMEM((1, size), jnp.int32)] * 2 + [pltpu.SemaphoreType.DMA((3,))],
        compiler_params=pltpu.CompilerParams(vmem_limit_bytes=56 * MIB),
    )(weight_num.reshape(1, size), weight_den.reshape(1, size), head_weight)
    got = {0: payload}
    for g in far + near:
        got[2 * g] = swap(payload, "label", 2 * g)
    got[1] = swap(payload, "label", 1)
    (hidden_t,) = call(
        inputs_kernel,
        [shape((width, samples), BF16)],
        [enc, proj],
        flops=2 * samples * width * width,
        nbytes=6_000_000,
    )
    (target,) = call(
        functools.partial(target_kernel, beam, block),
        [shape((beam * size, samples), BF16)],
        [positives.T],
        after=[hidden_t],
        vmem=2,
        nbytes=8_000_000,
    )
    grads, kept, from_core, moved, received = {}, {}, {}, {}, {}
    order = [0] + far + near
    for at, g in enumerate(order):
        after = [grads[order[at - 1]]] if at else []
        if at == 1 and len(order) > 2:
            after.append(got[2 * order[2]])
        if at >= 3:
            after.append(moved[order[at - 2]])
        grads[g], kept[g], sent = call(
            functools.partial(score_kernel, g, block, row_blocks),
            [shape((2 * size, samples), BF16), shape((size, width), F32), shape((size, width), BF16)],
            [hidden_t, target, enc, got[2 * g], got[2 * g + 1]],
            scalars=[listed, me_s, z_s],
            after=after,
            scratch=[
                pltpu.VMEM((2 * size, width), BF16),
                pltpu.VMEM((2 * size, block), F32),
                pltpu.VMEM((2 * size, samples), F32),
            ],
            flops=8 * samples * size * width,
            nbytes=5_000_000,
        )
        for ahead in order[1:3] if at == 0 else order[at + 1 : at + 2] if at > 1 else []:
            got[2 * ahead] = gate(got[2 * ahead], grads[g])
            got[2 * ahead + 1] = swap(got[2 * ahead], "label", 1)
        from_core[g] = swap(sent, "label", 1)
        if g:
            moved[g] = (kept[g] + from_core[g].astype(F32)).astype(BF16)
            received[g] = swap(moved[g], "label", 2 * g)
    own = kept[0] + from_core[0].astype(F32)
    received = [received[g] for g in far + near]

    grad_hidden, rows = call(
        functools.partial(hidden_kernel, owners),
        [shape((samples, width), BF16), shape((labels, width), BF16)],
        [grads[g] for g in range(chips)] + [got[d] for d in range(owners)],
        scalars=[me_s],
        after=[moved[g] for g in far + near],
        scratch=[pltpu.VMEM((labels, width), BF16)],
        vmem=12,
        flops=2 * samples * width * labels,
        nbytes=5_000_000,
    )
    tile = min(256, samples)

    def grad_enc_after(value):
        return pl.pallas_call(
            enc_kernel,
            grid=(samples // tile,),
            out_shape=[shape((samples, width), F32), shape((8, 128), F32)],
            in_specs=[
                pl.BlockSpec((tile, width), lambda i: (i, 0)),
                pl.BlockSpec((width, width), lambda i: (0, 0)),
                ANY,
            ],
            out_specs=[
                pl.BlockSpec((tile, width), lambda i: (i, 0)),
                pl.BlockSpec((8, 128), lambda i: (0, 0)),
            ],
            compiler_params=pltpu.CompilerParams(vmem_limit_bytes=12 * MIB),
            cost_estimate=pl.CostEstimate(
                flops=2 * samples * width * width, bytes_accessed=6_000_000, transcendentals=0
            ),
        )(grad_hidden, proj, value)

    if row_blocks > 1:
        cut = size // 2
        total, upper = call(
            combine_kernel,
            [shape((cut, width), F32), shape((cut, width), BF16)],
            [own] + received,
            after=[grad_hidden],
            nbytes=2_000_000,
        )
        span = row_blocks // 2
        total = total + swap(upper, "dp", span).astype(F32)
        while span > 1:
            cut = span // 2 * depth
            total = total[:cut] + swap(total[cut:].astype(BF16), "dp", span // 2).astype(F32)
            span //= 2
    else:
        total = own
        for value in received:
            total = total + value.astype(F32)
    total = total.astype(BF16)
    grad_enc, enc_done = grad_enc_after(total)
    if planes > 1:
        other = gate(swap(total, "dp", planes // 2), enc_done)
        total = (total.astype(F32) + other.astype(F32)).astype(BF16)
    parts = {0: total}
    span = 1
    while span < row_blocks:
        for r in range(span):
            parts[r + span] = swap(parts[r], "dp", span)
        span *= 2
    proj_slice = lax.dynamic_slice_in_dim(proj, z * (width // planes), width // planes, 1)
    (whole,) = call(
        whole_kernel,
        [shape((width, size), BF16)],
        [parts[r] for r in range(row_blocks)],
        scalars=[z_s],
        scratch=[pltpu.VMEM((size, width), BF16)],
        vmem=4,
    )
    rows, grad_head = pl.pallas_call(
        head_kernel,
        out_shape=[shape((labels, width), BF16), shape((width // planes, size), F32)],
        in_specs=[ANY, VMEM, VMEM],
        out_specs=[VMEM, VMEM],
        scratch_shapes=[pltpu.SemaphoreType.DMA],
        compiler_params=pltpu.CompilerParams(vmem_limit_bytes=4 * MIB),
        cost_estimate=pl.CostEstimate(
            flops=2 * size * width * width // planes, bytes_accessed=3_000_000, transcendentals=0
        ),
    )(rows, whole, proj_slice)
    have = {0: whole}
    for g in near + far:
        have[2 * g] = gate(swap(whole, "label", 2 * g), rows)
    for distance in list(have):
        have[distance + 1] = swap(have[distance], "label", 1)
    cuts = 4
    grad_proj = pl.pallas_call(
        functools.partial(proj_kernel, cuts),
        out_shape=shape((width, width), F32),
        in_specs=[SMEM] + [VMEM] * (owners + 1),
        out_specs=ANY,
        scratch_shapes=[
            pltpu.VMEM((width, labels), BF16),
            pltpu.VMEM((width, width), F32),
            pltpu.SemaphoreType.DMA((cuts,)),
        ],
        compiler_params=pltpu.CompilerParams(vmem_limit_bytes=16 * MIB),
        cost_estimate=pl.CostEstimate(
            flops=2 * labels * width * width, bytes_accessed=6_000_000, transcendentals=0
        ),
    )(me_s, *[have[distance] for distance in range(owners)], rows)
    return (grad_enc, grad_proj, grad_head.T)


def solution(mesh):
    placed = (
        P(("dp", "label"), None),
        P(),
        P("label", None),
        P(("dp", "label"), None),
        P(("dp", "label"), None),
        P("label"),
        P("label"),
    )
    return jax.shard_map(
        shards,
        mesh=mesh,
        in_specs=placed,
        out_specs=(P(("dp", "label"), None), P(), P("label", "dp")),
        check_vma=False,
    )
```

```python
import functools

import jax
import jax.numpy as jnp
from jax import lax
from jax.experimental import pallas as pl
from jax.experimental.pallas import tpu as pltpu
from jax.sharding import PartitionSpec as P

BF16 = jnp.bfloat16
F32 = jnp.float32
VMEM = pl.BlockSpec(memory_space=pltpu.VMEM)
SMEM = pl.BlockSpec(memory_space=pltpu.SMEM)
ANY = pl.BlockSpec(memory_space=pl.ANY)
MIB = 1024 * 1024
TAIL = 16
NN = (((1,), (0,)), ((), ()))
NT = (((1,), (1,)), ((), ()))
TN = (((0,), (0,)), ((), ()))


def dot(left, right, dims):
    return lax.dot_general(left, right, dims, preferred_element_type=F32)


def shape(dims, dtype):
    return jax.ShapeDtypeStruct(dims, dtype)


def call(kernel, outs, args, scalars=(), after=(), scratch=(), vmem=8, flops=0, nbytes=0):
    return pl.pallas_call(
        kernel,
        out_shape=outs,
        in_specs=[SMEM] * len(scalars) + [VMEM] * len(args) + [ANY] * len(after),
        out_specs=[VMEM] * len(outs),
        scratch_shapes=list(scratch),
        compiler_params=pltpu.CompilerParams(vmem_limit_bytes=vmem * MIB),
        cost_estimate=pl.CostEstimate(flops=flops, bytes_accessed=nbytes, transcendentals=0),
    )(*scalars, *args, *after)


def gate(value, *after):
    return pl.pallas_call(
        lambda value_ref, *refs: None,
        out_shape=shape(value.shape, value.dtype),
        in_specs=[ANY] * (1 + len(after)),
        out_specs=ANY,
        input_output_aliases={0: 0},
        compiler_params=pltpu.CompilerParams(vmem_limit_bytes=MIB),
    )(value, *after)


def swap(value, axis, distance):
    size = lax.axis_size(axis)
    return lax.ppermute(value, axis, [(i, i ^ distance) for i in range(size)])


def payload_kernel(num_hbm, den_hbm, rows_hbm, out_ref, num_ref, den_ref, sems):
    size, width = rows_hbm.shape
    copies = [
        pltpu.make_async_copy(num_hbm, num_ref, sems.at[0]),
        pltpu.make_async_copy(den_hbm, den_ref, sems.at[1]),
        pltpu.make_async_copy(rows_hbm, out_ref.at[pl.ds(0, size), :], sems.at[2]),
    ]
    for copy in copies:
        copy.start()
    out_ref[size:, size:] = jnp.zeros((TAIL, width - size), BF16)
    copies[0].wait()
    copies[1].wait()
    row = lax.broadcasted_iota(jnp.int32, (TAIL, size), 0)
    both = jnp.where(row == 0, num_ref[...], den_ref[...])
    out_ref[size:, :size] = both.astype(F32).astype(BF16)
    copies[2].wait()


def target_kernel(beam, block, wanted_ref, target_ref):
    samples = wanted_ref.shape[1]
    size = target_ref.shape[0] // beam
    label_iota = lax.broadcasted_iota(jnp.int32, (size, block), 0)
    for low in range(0, samples, block):
        for place in range(beam):
            labels = label_iota + place * size
            target = labels == wanted_ref[0:1, low : low + block]
            for column in range(1, wanted_ref.shape[0]):
                target = target | (labels == wanted_ref[column : column + 1, low : low + block])
            target_ref[place * size : (place + 1) * size, low : low + block] = jnp.where(
                target, 1.0, 0.0
            ).astype(BF16)


def inputs_kernel(enc_ref, proj_ref, after_ref, hidden_t_ref):
    samples = enc_ref.shape[0]
    tile = min(256, samples)
    for start in range(0, samples, tile):
        hidden = dot(enc_ref[start : start + tile, :], proj_ref[...], NN).astype(BF16)
        hidden_t_ref[:, start : start + tile] = hidden.T


def logistic(value):
    bottom = 1.0 + jnp.exp(-jnp.maximum(value, -80.0))
    guess = pl.reciprocal(bottom, approx=True)
    return guess * (2.0 - bottom * guess)


def score_kernel(group, block, count, list_ref, me_ref, z_ref, hidden_t_ref, target_ref, enc_ref, *refs):
    payloads, refs = refs[:2], refs[-6:]
    grads_ref, kept_ref, sent_ref, weights_ref, scale_ref, logits_ref = refs
    samples = enc_ref.shape[0]
    size = payloads[0].shape[0] - TAIL
    for core in range(2):
        rows = pl.ds(core * size, size)
        weights_ref[rows, :] = payloads[core][:size, :]
        tail = payloads[core][size:, :size].astype(F32)
        ratio = tail[0:1, :] / tail[1:2, :]
        scale_ref[rows, :] = jnp.broadcast_to(ratio, (block, size)).T
    tile = min(2 * block, samples)
    for start in range(0, samples, tile):
        logits_ref[:, start : start + tile] = dot(
            weights_ref[...], hidden_t_ref[:, start : start + tile], NN
        )
        for low in range(start, start + tile, block):
            for core in range(2):
                cluster = me_ref[0] ^ (2 * group + core)
                place = jnp.int32(-1)
                for beam_slot in range(list_ref.shape[0]):
                    place = jnp.where(list_ref[beam_slot, low // block] == cluster, beam_slot, place)
                factor = jnp.where(place >= 0, 1.0 / block, 0.0)
                first = pl.multiple_of(jnp.maximum(place, 0) * size, size)
                rows = slice(core * size, (core + 1) * size)
                target = target_ref[pl.ds(first, size), low : low + block].astype(F32)
                share = logistic(logits_ref[rows, low : low + block]) - target
                grads_ref[rows, low : low + block] = (scale_ref[rows, :] * factor * share).astype(BF16)
    outer = dot(grads_ref[...], enc_ref[...], NN)
    depth = size // count
    for r in range(count):
        rows = pl.ds(pl.multiple_of((z_ref[0] ^ r) * depth, depth), depth)
        kept_ref[rows, :] = outer[r * depth : (r + 1) * depth, :]
        sent_ref[rows, :] = outer[size + r * depth : size + (r + 1) * depth, :].astype(BF16)


def hidden_kernel(owners, me_ref, *refs):
    chips = owners // 2
    grads, payloads, refs = refs[:chips], refs[chips : chips + owners], refs[chips + owners :]
    out_ref, rows_ref, weights_ref = refs[-3:]
    size = payloads[0].shape[0] - TAIL
    for slot in range(owners):
        piece = payloads[slot][:size, :]
        start = pl.multiple_of((me_ref[0] ^ slot) * size, size)
        rows_ref[pl.ds(start, size), :] = piece
        weights_ref[slot * size : (slot + 1) * size, :] = piece
    samples = out_ref.shape[0]
    tile = min(256, samples)
    for low in range(0, samples, tile):
        total = jnp.zeros((tile, out_ref.shape[1]), F32)
        for group in range(chips):
            rows = weights_ref[2 * group * size : 2 * (group + 1) * size, :]
            total = total + dot(grads[group][:, low : low + tile], rows, TN)
        out_ref[low : low + tile, :] = total.astype(BF16)


def enc_kernel(grad_hidden_ref, proj_ref, after_ref, out_ref, done_ref):
    out_ref[...] = dot(grad_hidden_ref[...], proj_ref[...], NT)
    done_ref[...] = jnp.zeros_like(done_ref)


def combine_kernel(own_ref, *refs):
    *received, after_ref, kept_ref, sent_ref = refs
    cut = kept_ref.shape[0]
    for rows, out_ref in ((slice(cut, None), sent_ref), (slice(0, cut), kept_ref)):
        total = own_ref[rows, :]
        for ref in received:
            total = total + ref[rows, :].astype(F32)
        out_ref[...] = total.astype(out_ref.dtype)


def whole_kernel(z_ref, *refs):
    *parts, whole_ref, rows_ref = refs
    depth = parts[0].shape[0]
    for r, part in enumerate(parts):
        rows_ref[pl.ds(pl.multiple_of((z_ref[0] ^ r) * depth, depth), depth), :] = part[...]
    whole_ref[...] = rows_ref[...].T


def head_kernel(rows_any, whole_ref, slice_ref, rows_ref, head_ref, sem):
    copy = pltpu.make_async_copy(rows_any, rows_ref, sem)
    copy.start()
    head_ref[...] = dot(slice_ref[...], whole_ref[...], TN)
    copy.wait()


def proj_kernel(cuts, me_ref, *refs):
    *parts, rows_ref, out_hbm, outer_ref, done_ref, sems = refs
    width, size = parts[0].shape
    for distance, part in enumerate(parts):
        start = pl.multiple_of((me_ref[0] ^ distance) * size, size)
        outer_ref[:, pl.ds(start, size)] = part[...]
    height = width // cuts
    copies = []
    for cut in range(cuts):
        rows = pl.ds(cut * height, height)
        done_ref[rows, :] = dot(outer_ref[rows, :], rows_ref[...], NN)
        copy = pltpu.make_async_copy(done_ref.at[rows, :], out_hbm.at[rows, :], sems.at[cut])
        copy.start()
        copies.append(copy)
    for copy in copies:
        copy.wait()


def shards(enc, proj, head_weight, shortlist, positives, weight_num, weight_den):
    owners, planes = lax.axis_size("label"), lax.axis_size("dp")
    chips = owners // 2
    near = [g for g in range(1, chips) if g & (g - 1) == 0]
    far = [g for g in range(1, chips) if g & (g - 1) != 0]
    row_blocks = max(1, planes // 2)
    me = lax.axis_index("label").astype(jnp.int32)
    z = lax.axis_index("dp").astype(jnp.int32)
    z_low = z & (row_blocks - 1)
    blocks, beam = shortlist.shape
    samples, width = enc.shape
    block = samples // blocks
    size = head_weight.shape[0]
    labels = owners * size
    depth = size // row_blocks
    me_s, z_s = me.reshape(1), z_low.reshape(1)
    listed = shortlist.astype(jnp.int32).T

    payload = pl.pallas_call(
        payload_kernel,
        out_shape=shape((size + TAIL, width), BF16),
        in_specs=[ANY] * 3,
        out_specs=VMEM,
        scratch_shapes=[pltpu.VMEM((1, size), jnp.int32)] * 2 + [pltpu.SemaphoreType.DMA((3,))],
        compiler_params=pltpu.CompilerParams(vmem_limit_bytes=56 * MIB),
    )(weight_num.reshape(1, size), weight_den.reshape(1, size), head_weight)
    got = {0: payload}
    for g in far + near:
        got[2 * g] = swap(payload, "label", 2 * g)
    got[1] = swap(payload, "label", 1)
    (target,) = call(
        functools.partial(target_kernel, beam, block),
        [shape((beam * size, samples), BF16)],
        [positives.T],
        vmem=2,
        nbytes=8_000_000,
    )
    (hidden_t,) = call(
        inputs_kernel,
        [shape((width, samples), BF16)],
        [enc, proj],
        after=[target],
        flops=2 * samples * width * width,
        nbytes=6_000_000,
    )
    grads, kept, from_core, moved, received = {}, {}, {}, {}, {}
    order = [0] + far + near
    for at, g in enumerate(order):
        after = [grads[order[at - 1]]] if at else []
        if at == 1:
            after.extend(got[2 * ahead] for ahead in order[2:])
        if at >= 3:
            after.append(moved[order[at - 2]])
        grads[g], kept[g], sent = call(
            functools.partial(score_kernel, g, block, row_blocks),
            [shape((2 * size, samples), BF16), shape((size, width), F32), shape((size, width), BF16)],
            [hidden_t, target, enc, got[2 * g], got[2 * g + 1]],
            scalars=[listed, me_s, z_s],
            after=after,
            scratch=[
                pltpu.VMEM((2 * size, width), BF16),
                pltpu.VMEM((2 * size, block), F32),
                pltpu.VMEM((2 * size, samples), F32),
            ],
            flops=8 * samples * size * width,
            nbytes=5_000_000,
        )
        for ahead in order[1:] if at == 0 else []:
            got[2 * ahead] = gate(got[2 * ahead], grads[g])
            got[2 * ahead + 1] = swap(got[2 * ahead], "label", 1)
        from_core[g] = swap(sent, "label", 1)
        if g:
            moved[g] = (kept[g] + from_core[g].astype(F32)).astype(BF16)
            received[g] = swap(moved[g], "label", 2 * g)
    own = kept[0] + from_core[0].astype(F32)
    received = [received[g] for g in far + near]

    grad_hidden, rows = call(
        functools.partial(hidden_kernel, owners),
        [shape((samples, width), BF16), shape((labels, width), BF16)],
        [grads[g] for g in range(chips)] + [got[d] for d in range(owners)],
        scalars=[me_s],
        after=[moved[g] for g in far + near],
        scratch=[pltpu.VMEM((labels, width), BF16)],
        vmem=12,
        flops=2 * samples * width * labels,
        nbytes=5_000_000,
    )
    tile = min(256, samples)

    def grad_enc_after(value):
        return pl.pallas_call(
            enc_kernel,
            grid=(samples // tile,),
            out_shape=[shape((samples, width), F32), shape((8, 128), F32)],
            in_specs=[
                pl.BlockSpec((tile, width), lambda i: (i, 0)),
                pl.BlockSpec((width, width), lambda i: (0, 0)),
                ANY,
            ],
            out_specs=[
                pl.BlockSpec((tile, width), lambda i: (i, 0)),
                pl.BlockSpec((8, 128), lambda i: (0, 0)),
            ],
            compiler_params=pltpu.CompilerParams(vmem_limit_bytes=12 * MIB),
            cost_estimate=pl.CostEstimate(
                flops=2 * samples * width * width, bytes_accessed=6_000_000, transcendentals=0
            ),
        )(grad_hidden, proj, value)

    if row_blocks > 1:
        cut = size // 2
        total, upper = call(
            combine_kernel,
            [shape((cut, width), F32), shape((cut, width), BF16)],
            [own] + received,
            after=[grad_hidden],
            nbytes=2_000_000,
        )
        span = row_blocks // 2
        total = total + swap(upper, "dp", span).astype(F32)
        while span > 1:
            cut = span // 2 * depth
            total = total[:cut] + swap(total[cut:].astype(BF16), "dp", span // 2).astype(F32)
            span //= 2
    else:
        total = own
        for value in received:
            total = total + value.astype(F32)
    total = total.astype(BF16)
    grad_enc, enc_done = grad_enc_after(total)
    if planes > 1:
        other = gate(swap(total, "dp", planes // 2), enc_done)
        total = (total.astype(F32) + other.astype(F32)).astype(BF16)
    parts = {0: total}
    span = 1
    while span < row_blocks:
        for r in range(span):
            parts[r + span] = swap(parts[r], "dp", span)
        span *= 2
    proj_slice = lax.dynamic_slice_in_dim(proj, z * (width // planes), width // planes, 1)
    (whole,) = call(
        whole_kernel,
        [shape((width, size), BF16)],
        [parts[r] for r in range(row_blocks)],
        scalars=[z_s],
        scratch=[pltpu.VMEM((size, width), BF16)],
        vmem=4,
    )
    rows, grad_head = pl.pallas_call(
        head_kernel,
        out_shape=[shape((labels, width), BF16), shape((width // planes, size), F32)],
        in_specs=[ANY, VMEM, VMEM],
        out_specs=[VMEM, VMEM],
        scratch_shapes=[pltpu.SemaphoreType.DMA],
        compiler_params=pltpu.CompilerParams(vmem_limit_bytes=4 * MIB),
        cost_estimate=pl.CostEstimate(
            flops=2 * size * width * width // planes, bytes_accessed=3_000_000, transcendentals=0
        ),
    )(rows, whole, proj_slice)
    have = {0: whole}
    for g in near + far:
        have[2 * g] = gate(swap(whole, "label", 2 * g), rows)
    for distance in list(have):
        have[distance + 1] = swap(have[distance], "label", 1)
    cuts = 4
    grad_proj = pl.pallas_call(
        functools.partial(proj_kernel, cuts),
        out_shape=shape((width, width), F32),
        in_specs=[SMEM] + [VMEM] * (owners + 1),
        out_specs=ANY,
        scratch_shapes=[
            pltpu.VMEM((width, labels), BF16),
            pltpu.VMEM((width, width), F32),
            pltpu.SemaphoreType.DMA((cuts,)),
        ],
        compiler_params=pltpu.CompilerParams(vmem_limit_bytes=16 * MIB),
        cost_estimate=pl.CostEstimate(
            flops=2 * labels * width * width, bytes_accessed=6_000_000, transcendentals=0
        ),
    )(me_s, *[have[distance] for distance in range(owners)], rows)
    return (grad_enc, grad_proj, grad_head.T)


def solution(mesh):
    placed = (
        P(("dp", "label"), None),
        P(),
        P("label", None),
        P(("dp", "label"), None),
        P(("dp", "label"), None),
        P("label"),
        P("label"),
    )
    return jax.shard_map(
        shards,
        mesh=mesh,
        in_specs=placed,
        out_specs=(P(("dp", "label"), None), P(), P("label", "dp")),
        check_vma=False,
    )
```

```python
import functools

import jax
import jax.numpy as jnp
from jax import lax
from jax.experimental import pallas as pl
from jax.experimental.pallas import tpu as pltpu
from jax.sharding import PartitionSpec as P

BF16 = jnp.bfloat16
F32 = jnp.float32
VMEM = pl.BlockSpec(memory_space=pltpu.VMEM)
SMEM = pl.BlockSpec(memory_space=pltpu.SMEM)
ANY = pl.BlockSpec(memory_space=pl.ANY)
MIB = 1024 * 1024
TAIL = 16
NN = (((1,), (0,)), ((), ()))
NT = (((1,), (1,)), ((), ()))
TN = (((0,), (0,)), ((), ()))


def dot(left, right, dims):
    return lax.dot_general(left, right, dims, preferred_element_type=F32)


def shape(dims, dtype):
    return jax.ShapeDtypeStruct(dims, dtype)


def call(kernel, outs, args, scalars=(), after=(), scratch=(), vmem=8, flops=0, nbytes=0):
    return pl.pallas_call(
        kernel,
        out_shape=outs,
        in_specs=[SMEM] * len(scalars) + [VMEM] * len(args) + [ANY] * len(after),
        out_specs=[VMEM] * len(outs),
        scratch_shapes=list(scratch),
        compiler_params=pltpu.CompilerParams(vmem_limit_bytes=vmem * MIB),
        cost_estimate=pl.CostEstimate(flops=flops, bytes_accessed=nbytes, transcendentals=0),
    )(*scalars, *args, *after)


def gate(value, *after):
    return pl.pallas_call(
        lambda value_ref, *refs: None,
        out_shape=shape(value.shape, value.dtype),
        in_specs=[ANY] * (1 + len(after)),
        out_specs=ANY,
        input_output_aliases={0: 0},
        compiler_params=pltpu.CompilerParams(vmem_limit_bytes=MIB),
    )(value, *after)


def swap(value, axis, distance):
    size = lax.axis_size(axis)
    return lax.ppermute(value, axis, [(i, i ^ distance) for i in range(size)])


def payload_kernel(num_hbm, den_hbm, rows_hbm, out_ref, num_ref, den_ref, sems):
    size, width = rows_hbm.shape
    copies = [
        pltpu.make_async_copy(num_hbm, num_ref, sems.at[0]),
        pltpu.make_async_copy(den_hbm, den_ref, sems.at[1]),
        pltpu.make_async_copy(rows_hbm, out_ref.at[pl.ds(0, size), :], sems.at[2]),
    ]
    for copy in copies:
        copy.start()
    out_ref[size:, size:] = jnp.zeros((TAIL, width - size), BF16)
    copies[0].wait()
    copies[1].wait()
    row = lax.broadcasted_iota(jnp.int32, (TAIL, size), 0)
    both = jnp.where(row == 0, num_ref[...], den_ref[...])
    out_ref[size:, :size] = both.astype(F32).astype(BF16)
    copies[2].wait()


def target_kernel(beam, block, wanted_ref, target_ref):
    samples = wanted_ref.shape[1]
    size = target_ref.shape[0] // beam
    label_iota = lax.broadcasted_iota(jnp.int32, (size, block), 0)
    for low in range(0, samples, block):
        for place in range(beam):
            labels = label_iota + place * size
            target = labels == wanted_ref[0:1, low : low + block]
            for column in range(1, wanted_ref.shape[0]):
                target = target | (labels == wanted_ref[column : column + 1, low : low + block])
            target_ref[place * size : (place + 1) * size, low : low + block] = jnp.where(
                target, 1.0, 0.0
            ).astype(BF16)


def inputs_kernel(enc_ref, proj_ref, after_ref, hidden_t_ref):
    samples = enc_ref.shape[0]
    tile = min(256, samples)
    for start in range(0, samples, tile):
        hidden = dot(enc_ref[start : start + tile, :], proj_ref[...], NN).astype(BF16)
        hidden_t_ref[:, start : start + tile] = hidden.T


def logistic(value):
    bottom = 1.0 + jnp.exp(-jnp.maximum(value, -80.0))
    guess = pl.reciprocal(bottom, approx=True)
    return guess * (2.0 - bottom * guess)


def score_kernel(group, block, count, list_ref, me_ref, z_ref, hidden_t_ref, target_ref, enc_ref, *refs):
    payloads, refs = refs[:2], refs[-6:]
    grads_ref, kept_ref, sent_ref, weights_ref, scale_ref, logits_ref = refs
    samples = enc_ref.shape[0]
    size = payloads[0].shape[0] - TAIL
    for core in range(2):
        rows = pl.ds(core * size, size)
        weights_ref[rows, :] = payloads[core][:size, :]
        tail = payloads[core][size:, :size].astype(F32)
        ratio = tail[0:1, :] / tail[1:2, :]
        scale_ref[rows, :] = jnp.broadcast_to(ratio, (block, size)).T
    tile = min(2 * block, samples)
    for start in range(0, samples, tile):
        logits_ref[:, start : start + tile] = dot(
            weights_ref[...], hidden_t_ref[:, start : start + tile], NN
        )
        for low in range(start, start + tile, block):
            for core in range(2):
                cluster = me_ref[0] ^ (2 * group + core)
                place = jnp.int32(-1)
                for beam_slot in range(list_ref.shape[0]):
                    place = jnp.where(list_ref[beam_slot, low // block] == cluster, beam_slot, place)
                factor = jnp.where(place >= 0, 1.0 / block, 0.0)
                first = pl.multiple_of(jnp.maximum(place, 0) * size, size)
                rows = slice(core * size, (core + 1) * size)
                target = target_ref[pl.ds(first, size), low : low + block].astype(F32)
                share = logistic(logits_ref[rows, low : low + block]) - target
                grads_ref[rows, low : low + block] = (scale_ref[rows, :] * factor * share).astype(BF16)
    outer = dot(grads_ref[...], enc_ref[...], NN)
    depth = size // count
    for r in range(count):
        rows = pl.ds(pl.multiple_of((z_ref[0] ^ r) * depth, depth), depth)
        kept_ref[rows, :] = outer[r * depth : (r + 1) * depth, :]
        sent_ref[rows, :] = outer[size + r * depth : size + (r + 1) * depth, :].astype(BF16)


def hidden_kernel(owners, me_ref, *refs):
    chips = owners // 2
    grads, payloads, refs = refs[:chips], refs[chips : chips + owners], refs[chips + owners :]
    out_ref, rows_ref, weights_ref = refs[-3:]
    size = payloads[0].shape[0] - TAIL
    for slot in range(owners):
        piece = payloads[slot][:size, :]
        start = pl.multiple_of((me_ref[0] ^ slot) * size, size)
        rows_ref[pl.ds(start, size), :] = piece
        weights_ref[slot * size : (slot + 1) * size, :] = piece
    samples = out_ref.shape[0]
    tile = min(256, samples)
    for low in range(0, samples, tile):
        total = jnp.zeros((tile, out_ref.shape[1]), F32)
        for group in range(chips):
            rows = weights_ref[2 * group * size : 2 * (group + 1) * size, :]
            total = total + dot(grads[group][:, low : low + tile], rows, TN)
        out_ref[low : low + tile, :] = total.astype(BF16)


def enc_kernel(grad_hidden_ref, proj_ref, after_ref, out_ref, done_ref):
    out_ref[...] = dot(grad_hidden_ref[...], proj_ref[...], NT)
    done_ref[...] = jnp.zeros_like(done_ref)


def combine_kernel(own_ref, *refs):
    *received, after_ref, kept_ref, sent_ref = refs
    cut = kept_ref.shape[0]
    for rows, out_ref in ((slice(cut, None), sent_ref), (slice(0, cut), kept_ref)):
        total = own_ref[rows, :]
        for ref in received:
            total = total + ref[rows, :].astype(F32)
        out_ref[...] = total.astype(out_ref.dtype)


def head_kernel(count, z_ref, *refs):
    parts, (slice_ref, rows_any, rows_ref, head_ref, whole_ref, sem) = refs[:count], refs[count:]
    copy = pltpu.make_async_copy(rows_any, rows_ref, sem)
    copy.start()
    depth = parts[0].shape[0]
    for r, part in enumerate(parts):
        whole_ref[pl.ds(pl.multiple_of((z_ref[0] ^ r) * depth, depth), depth), :] = part[...]
    head_ref[...] = dot(whole_ref[...], slice_ref[...], NN).T
    copy.wait()


def proj_kernel(count, cuts, me_ref, z_ref, *refs):
    *parts, rows_ref, out_hbm, outer_ref, done_ref, sems = refs
    depth, width = parts[0].shape
    for at, part in enumerate(parts):
        start = (me_ref[0] ^ (at // count)) * (depth * count) + (z_ref[0] ^ (at % count)) * depth
        outer_ref[pl.ds(pl.multiple_of(start, depth), depth), :] = part[...]
    height = width // cuts
    copies = []
    for cut in range(cuts):
        rows = pl.ds(cut * height, height)
        done_ref[rows, :] = dot(outer_ref[:, rows], rows_ref[...], TN)
        copy = pltpu.make_async_copy(done_ref.at[rows, :], out_hbm.at[rows, :], sems.at[cut])
        copy.start()
        copies.append(copy)
    for copy in copies:
        copy.wait()


def shards(enc, proj, head_weight, shortlist, positives, weight_num, weight_den):
    owners, planes = lax.axis_size("label"), lax.axis_size("dp")
    chips = owners // 2
    near = [g for g in range(1, chips) if g & (g - 1) == 0]
    far = [g for g in range(1, chips) if g & (g - 1) != 0]
    row_blocks = max(1, planes // 2)
    me = lax.axis_index("label").astype(jnp.int32)
    z = lax.axis_index("dp").astype(jnp.int32)
    z_low = z & (row_blocks - 1)
    blocks, beam = shortlist.shape
    samples, width = enc.shape
    block = samples // blocks
    size = head_weight.shape[0]
    labels = owners * size
    depth = size // row_blocks
    me_s, z_s = me.reshape(1), z_low.reshape(1)
    listed = shortlist.astype(jnp.int32).T

    payload = pl.pallas_call(
        payload_kernel,
        out_shape=shape((size + TAIL, width), BF16),
        in_specs=[ANY] * 3,
        out_specs=VMEM,
        scratch_shapes=[pltpu.VMEM((1, size), jnp.int32)] * 2 + [pltpu.SemaphoreType.DMA((3,))],
        compiler_params=pltpu.CompilerParams(vmem_limit_bytes=56 * MIB),
    )(weight_num.reshape(1, size), weight_den.reshape(1, size), head_weight)
    got = {0: payload}
    for g in far + near:
        got[2 * g] = swap(payload, "label", 2 * g)
    got[1] = swap(payload, "label", 1)
    (target,) = call(
        functools.partial(target_kernel, beam, block),
        [shape((beam * size, samples), BF16)],
        [positives.T],
        vmem=2,
        nbytes=8_000_000,
    )
    (hidden_t,) = call(
        inputs_kernel,
        [shape((width, samples), BF16)],
        [enc, proj],
        after=[target],
        flops=2 * samples * width * width,
        nbytes=6_000_000,
    )
    grads, kept, from_core, moved, received = {}, {}, {}, {}, {}
    order = [0] + far + near
    for at, g in enumerate(order):
        after = [grads[order[at - 1]]] if at else []
        if at == 1:
            after.extend(got[2 * ahead] for ahead in order[2:])
        if at >= 3:
            after.append(moved[order[at - 2]])
        grads[g], kept[g], sent = call(
            functools.partial(score_kernel, g, block, row_blocks),
            [shape((2 * size, samples), BF16), shape((size, width), F32), shape((size, width), BF16)],
            [hidden_t, target, enc, got[2 * g], got[2 * g + 1]],
            scalars=[listed, me_s, z_s],
            after=after,
            scratch=[
                pltpu.VMEM((2 * size, width), BF16),
                pltpu.VMEM((2 * size, block), F32),
                pltpu.VMEM((2 * size, samples), F32),
            ],
            flops=8 * samples * size * width,
            nbytes=5_000_000,
        )
        for ahead in order[1:] if at == 0 else []:
            got[2 * ahead] = gate(got[2 * ahead], grads[g])
            got[2 * ahead + 1] = swap(got[2 * ahead], "label", 1)
        from_core[g] = swap(sent, "label", 1)
        if g:
            moved[g] = (kept[g] + from_core[g].astype(F32)).astype(BF16)
            received[g] = swap(moved[g], "label", 2 * g)
    own = kept[0] + from_core[0].astype(F32)
    received = [received[g] for g in far + near]

    grad_hidden, rows = call(
        functools.partial(hidden_kernel, owners),
        [shape((samples, width), BF16), shape((labels, width), BF16)],
        [grads[g] for g in range(chips)] + [got[d] for d in range(owners)],
        scalars=[me_s],
        after=[moved[g] for g in far + near],
        scratch=[pltpu.VMEM((labels, width), BF16)],
        vmem=12,
        flops=2 * samples * width * labels,
        nbytes=5_000_000,
    )
    tile = min(256, samples)

    def grad_enc_after(value):
        return pl.pallas_call(
            enc_kernel,
            grid=(samples // tile,),
            out_shape=[shape((samples, width), F32), shape((8, 128), F32)],
            in_specs=[
                pl.BlockSpec((tile, width), lambda i: (i, 0)),
                pl.BlockSpec((width, width), lambda i: (0, 0)),
                ANY,
            ],
            out_specs=[
                pl.BlockSpec((tile, width), lambda i: (i, 0)),
                pl.BlockSpec((8, 128), lambda i: (0, 0)),
            ],
            compiler_params=pltpu.CompilerParams(vmem_limit_bytes=12 * MIB),
            cost_estimate=pl.CostEstimate(
                flops=2 * samples * width * width, bytes_accessed=6_000_000, transcendentals=0
            ),
        )(grad_hidden, proj, value)

    if row_blocks > 1:
        cut = size // 2
        total, upper = call(
            combine_kernel,
            [shape((cut, width), F32), shape((cut, width), BF16)],
            [own] + received,
            after=[grad_hidden],
            nbytes=2_000_000,
        )
        span = row_blocks // 2
        total = total + swap(upper, "dp", span).astype(F32)
        while span > 1:
            cut = span // 2 * depth
            total = total[:cut] + swap(total[cut:].astype(BF16), "dp", span // 2).astype(F32)
            span //= 2
    else:
        total = own
        for value in received:
            total = total + value.astype(F32)
    total = total.astype(BF16)
    grad_enc, enc_done = grad_enc_after(total)
    if planes > 1:
        other = gate(swap(total, "dp", planes // 2), enc_done)
        total = (total.astype(F32) + other.astype(F32)).astype(BF16)
    parts = {0: total}
    span = 1
    while span < row_blocks:
        for r in range(span):
            parts[r + span] = swap(parts[r], "dp", span)
        span *= 2
    proj_slice = lax.dynamic_slice_in_dim(proj, z * (width // planes), width // planes, 1)
    rows, grad_head = pl.pallas_call(
        functools.partial(head_kernel, row_blocks),
        out_shape=[shape((labels, width), BF16), shape((width // planes, size), F32)],
        in_specs=[SMEM] + [VMEM] * (row_blocks + 1) + [ANY],
        out_specs=[VMEM, VMEM],
        scratch_shapes=[pltpu.VMEM((size, width), BF16), pltpu.SemaphoreType.DMA],
        compiler_params=pltpu.CompilerParams(vmem_limit_bytes=4 * MIB),
        cost_estimate=pl.CostEstimate(
            flops=2 * size * width * width // planes, bytes_accessed=3_000_000, transcendentals=0
        ),
    )(z_s, *[parts[r] for r in range(row_blocks)], proj_slice, rows)
    have = {(0, r): parts[r] for r in range(row_blocks)}
    for r in range(row_blocks):
        for g in near + far:
            have[2 * g, r] = swap(parts[r], "label", 2 * g)
    if near:
        last = (2 * near[0], row_blocks - 1)
        have[last] = gate(have[last], rows)
    for distance, r in list(have):
        have[distance + 1, r] = swap(have[distance, r], "label", 1)
    cuts = 3
    grad_proj = pl.pallas_call(
        functools.partial(proj_kernel, row_blocks, cuts),
        out_shape=shape((width, width), F32),
        in_specs=[SMEM] * 2 + [VMEM] * (owners * row_blocks + 1),
        out_specs=ANY,
        scratch_shapes=[
            pltpu.VMEM((labels, width), BF16),
            pltpu.VMEM((width, width), F32),
            pltpu.SemaphoreType.DMA((cuts,)),
        ],
        compiler_params=pltpu.CompilerParams(vmem_limit_bytes=16 * MIB),
        cost_estimate=pl.CostEstimate(
            flops=2 * labels * width * width, bytes_accessed=6_000_000, transcendentals=0
        ),
    )(me_s, z_s, *[have[distance, r] for distance in range(owners) for r in range(row_blocks)], rows)
    return (grad_enc, grad_proj, grad_head.T)


def solution(mesh):
    placed = (
        P(("dp", "label"), None),
        P(),
        P("label", None),
        P(("dp", "label"), None),
        P(("dp", "label"), None),
        P("label"),
        P("label"),
    )
    return jax.shard_map(
        shards,
        mesh=mesh,
        in_specs=placed,
        out_specs=(P(("dp", "label"), None), P(), P("label", "dp")),
        check_vma=False,
    )
```

```python
import functools

import jax
import jax.numpy as jnp
from jax import lax
from jax.experimental import pallas as pl
from jax.experimental.pallas import tpu as pltpu
from jax.sharding import PartitionSpec as P

BF16 = jnp.bfloat16
F32 = jnp.float32
VMEM = pl.BlockSpec(memory_space=pltpu.VMEM)
SMEM = pl.BlockSpec(memory_space=pltpu.SMEM)
ANY = pl.BlockSpec(memory_space=pl.ANY)
MIB = 1024 * 1024
TAIL = 16
NN = (((1,), (0,)), ((), ()))
NT = (((1,), (1,)), ((), ()))
TN = (((0,), (0,)), ((), ()))


def dot(left, right, dims):
    return lax.dot_general(left, right, dims, preferred_element_type=F32)


def shape(dims, dtype):
    return jax.ShapeDtypeStruct(dims, dtype)


def call(kernel, outs, args, scalars=(), after=(), scratch=(), vmem=8, flops=0, nbytes=0):
    return pl.pallas_call(
        kernel,
        out_shape=outs,
        in_specs=[SMEM] * len(scalars) + [VMEM] * len(args) + [ANY] * len(after),
        out_specs=[VMEM] * len(outs),
        scratch_shapes=list(scratch),
        compiler_params=pltpu.CompilerParams(vmem_limit_bytes=vmem * MIB),
        cost_estimate=pl.CostEstimate(flops=flops, bytes_accessed=nbytes, transcendentals=0),
    )(*scalars, *args, *after)


def gate(value, *after):
    return pl.pallas_call(
        lambda value_ref, *refs: None,
        out_shape=shape(value.shape, value.dtype),
        in_specs=[ANY] * (1 + len(after)),
        out_specs=ANY,
        input_output_aliases={0: 0},
        compiler_params=pltpu.CompilerParams(vmem_limit_bytes=MIB),
    )(value, *after)


def swap(value, axis, distance):
    size = lax.axis_size(axis)
    return lax.ppermute(value, axis, [(i, i ^ distance) for i in range(size)])


def payload_kernel(num_hbm, den_hbm, rows_hbm, out_ref, num_ref, den_ref, sems):
    size, width = rows_hbm.shape
    copies = [
        pltpu.make_async_copy(num_hbm, num_ref, sems.at[0]),
        pltpu.make_async_copy(den_hbm, den_ref, sems.at[1]),
        pltpu.make_async_copy(rows_hbm, out_ref.at[pl.ds(0, size), :], sems.at[2]),
    ]
    for copy in copies:
        copy.start()
    out_ref[size:, size:] = jnp.zeros((TAIL, width - size), BF16)
    copies[0].wait()
    copies[1].wait()
    row = lax.broadcasted_iota(jnp.int32, (TAIL, size), 0)
    both = jnp.where(row == 0, num_ref[...], den_ref[...])
    out_ref[size:, :size] = both.astype(F32).astype(BF16)
    copies[2].wait()


def target_kernel(beam, block, wanted_ref, target_ref):
    samples = wanted_ref.shape[1]
    size = target_ref.shape[0] // beam
    label_iota = lax.broadcasted_iota(jnp.int32, (size, block), 0)
    for low in range(0, samples, block):
        for place in range(beam):
            labels = label_iota + place * size
            target = labels == wanted_ref[0:1, low : low + block]
            for column in range(1, wanted_ref.shape[0]):
                target = target | (labels == wanted_ref[column : column + 1, low : low + block])
            target_ref[place * size : (place + 1) * size, low : low + block] = jnp.where(
                target, 1.0, 0.0
            ).astype(BF16)


def inputs_kernel(enc_ref, proj_ref, after_ref, hidden_t_ref):
    samples = enc_ref.shape[0]
    tile = min(256, samples)
    for start in range(0, samples, tile):
        hidden = dot(enc_ref[start : start + tile, :], proj_ref[...], NN).astype(BF16)
        hidden_t_ref[:, start : start + tile] = hidden.T


def logistic(value):
    bottom = 1.0 + jnp.exp(-jnp.maximum(value, -80.0))
    guess = pl.reciprocal(bottom, approx=True)
    return guess * (2.0 - bottom * guess)


def score_kernel(group, block, count, list_ref, me_ref, z_ref, hidden_t_ref, target_ref, enc_ref, *refs):
    payloads, refs = refs[:2], refs[-6:]
    grads_ref, kept_ref, sent_ref, weights_ref, scale_ref, logits_ref = refs
    samples = enc_ref.shape[0]
    size = payloads[0].shape[0] - TAIL
    for core in range(2):
        rows = pl.ds(core * size, size)
        weights_ref[rows, :] = payloads[core][:size, :]
        tail = payloads[core][size:, :size].astype(F32)
        ratio = tail[0:1, :] / tail[1:2, :]
        scale_ref[rows, :] = jnp.broadcast_to(ratio, (block, size)).T
    tile = min(2 * block, samples)
    for start in range(0, samples, tile):
        logits_ref[:, start : start + tile] = dot(
            weights_ref[...], hidden_t_ref[:, start : start + tile], NN
        )
        for low in range(start, start + tile, block):
            for core in range(2):
                cluster = me_ref[0] ^ (2 * group + core)
                place = jnp.int32(-1)
                for beam_slot in range(list_ref.shape[0]):
                    place = jnp.where(list_ref[beam_slot, low // block] == cluster, beam_slot, place)
                factor = jnp.where(place >= 0, 1.0 / block, 0.0)
                first = pl.multiple_of(jnp.maximum(place, 0) * size, size)
                rows = slice(core * size, (core + 1) * size)
                target = target_ref[pl.ds(first, size), low : low + block].astype(F32)
                share = logistic(logits_ref[rows, low : low + block]) - target
                grads_ref[rows, low : low + block] = (scale_ref[rows, :] * factor * share).astype(BF16)
    outer = dot(grads_ref[...], enc_ref[...], NN)
    depth = size // count
    for r in range(count):
        rows = pl.ds(pl.multiple_of((z_ref[0] ^ r) * depth, depth), depth)
        kept_ref[rows, :] = outer[r * depth : (r + 1) * depth, :]
        sent_ref[rows, :] = outer[size + r * depth : size + (r + 1) * depth, :].astype(BF16)


def hidden_kernel(owners, me_ref, *refs):
    chips = owners // 2
    grads, payloads, refs = refs[:chips], refs[chips : chips + owners], refs[chips + owners :]
    out_ref, rows_ref, weights_ref = refs[-3:]
    size = payloads[0].shape[0] - TAIL
    for slot in range(owners):
        piece = payloads[slot][:size, :]
        start = pl.multiple_of((me_ref[0] ^ slot) * size, size)
        rows_ref[pl.ds(start, size), :] = piece
        weights_ref[slot * size : (slot + 1) * size, :] = piece
    samples = out_ref.shape[0]
    tile = min(256, samples)
    for low in range(0, samples, tile):
        total = jnp.zeros((tile, out_ref.shape[1]), F32)
        for group in range(chips):
            rows = weights_ref[2 * group * size : 2 * (group + 1) * size, :]
            total = total + dot(grads[group][:, low : low + tile], rows, TN)
        out_ref[low : low + tile, :] = total.astype(BF16)


def enc_kernel(grad_hidden_ref, proj_ref, after_ref, out_ref, done_ref):
    out_ref[...] = dot(grad_hidden_ref[...], proj_ref[...], NT)
    done_ref[...] = jnp.zeros_like(done_ref)


def combine_kernel(own_ref, *refs):
    *received, after_ref, kept_ref, sent_ref = refs
    cut = kept_ref.shape[0]
    for rows, out_ref in ((slice(cut, None), sent_ref), (slice(0, cut), kept_ref)):
        total = own_ref[rows, :]
        for ref in received:
            total = total + ref[rows, :].astype(F32)
        out_ref[...] = total.astype(out_ref.dtype)


def whole_kernel(z_ref, *refs):
    *parts, whole_ref, rows_ref = refs
    depth = parts[0].shape[0]
    for r, part in enumerate(parts):
        rows_ref[pl.ds(pl.multiple_of((z_ref[0] ^ r) * depth, depth), depth), :] = part[...]
    whole_ref[...] = rows_ref[...].T


def head_kernel(rows_any, whole_ref, slice_ref, rows_ref, head_ref, sem):
    copy = pltpu.make_async_copy(rows_any, rows_ref, sem)
    copy.start()
    head_ref[...] = dot(slice_ref[...], whole_ref[...], TN)
    copy.wait()


def proj_kernel(cuts, me_ref, *refs):
    *parts, rows_ref, out_hbm, outer_ref, done_ref, sems = refs
    width, size = parts[0].shape
    for distance, part in enumerate(parts):
        start = pl.multiple_of((me_ref[0] ^ distance) * size, size)
        outer_ref[:, pl.ds(start, size)] = part[...]
    height = width // cuts
    copies = []
    for cut in range(cuts):
        rows = pl.ds(cut * height, height)
        done_ref[rows, :] = dot(outer_ref[rows, :], rows_ref[...], NN)
        copy = pltpu.make_async_copy(done_ref.at[rows, :], out_hbm.at[rows, :], sems.at[cut])
        copy.start()
        copies.append(copy)
    for copy in copies:
        copy.wait()


def shards(enc, proj, head_weight, shortlist, positives, weight_num, weight_den):
    owners, planes = lax.axis_size("label"), lax.axis_size("dp")
    chips = owners // 2
    near = [g for g in range(1, chips) if g & (g - 1) == 0]
    far = [g for g in range(1, chips) if g & (g - 1) != 0]
    row_blocks = max(1, planes // 2)
    me = lax.axis_index("label").astype(jnp.int32)
    z = lax.axis_index("dp").astype(jnp.int32)
    z_low = z & (row_blocks - 1)
    blocks, beam = shortlist.shape
    samples, width = enc.shape
    block = samples // blocks
    size = head_weight.shape[0]
    labels = owners * size
    depth = size // row_blocks
    me_s, z_s = me.reshape(1), z_low.reshape(1)
    listed = shortlist.astype(jnp.int32).T

    payload = pl.pallas_call(
        payload_kernel,
        out_shape=shape((size + TAIL, width), BF16),
        in_specs=[ANY] * 3,
        out_specs=VMEM,
        scratch_shapes=[pltpu.VMEM((1, size), jnp.int32)] * 2 + [pltpu.SemaphoreType.DMA((3,))],
        compiler_params=pltpu.CompilerParams(vmem_limit_bytes=56 * MIB),
    )(weight_num.reshape(1, size), weight_den.reshape(1, size), head_weight)
    got = {0: payload}
    for g in far + near:
        got[2 * g] = swap(payload, "label", 2 * g)
    got[1] = swap(payload, "label", 1)
    (target,) = call(
        functools.partial(target_kernel, beam, block),
        [shape((beam * size, samples), BF16)],
        [positives.T],
        vmem=2,
        nbytes=8_000_000,
    )
    (hidden_t,) = call(
        inputs_kernel,
        [shape((width, samples), BF16)],
        [enc, proj],
        after=[target],
        flops=2 * samples * width * width,
        nbytes=6_000_000,
    )
    grads, kept, from_core, moved, received = {}, {}, {}, {}, {}
    order = [0] + far + near
    for at, g in enumerate(order):
        after = [grads[order[at - 1]]] if at else []
        if at == 1:
            after.extend(got[2 * ahead] for ahead in order[2:])
        if at >= 3:
            after.append(moved[order[at - 2]])
        grads[g], kept[g], sent = call(
            functools.partial(score_kernel, g, block, row_blocks),
            [shape((2 * size, samples), BF16), shape((size, width), F32), shape((size, width), BF16)],
            [hidden_t, target, enc, got[2 * g], got[2 * g + 1]],
            scalars=[listed, me_s, z_s],
            after=after,
            scratch=[
                pltpu.VMEM((2 * size, width), BF16),
                pltpu.VMEM((2 * size, block), F32),
                pltpu.VMEM((2 * size, samples), F32),
            ],
            flops=8 * samples * size * width,
            nbytes=5_000_000,
        )
        for ahead in order[1:] if at == 0 else []:
            got[2 * ahead] = gate(got[2 * ahead], grads[g])
            got[2 * ahead + 1] = swap(got[2 * ahead], "label", 1)
        from_core[g] = swap(sent, "label", 1)
        if g:
            moved[g] = (kept[g] + from_core[g].astype(F32)).astype(BF16)
            received[g] = swap(moved[g], "label", 2 * g)
    own = kept[0] + from_core[0].astype(F32)
    received = [received[g] for g in far + near]

    grad_hidden, rows = call(
        functools.partial(hidden_kernel, owners),
        [shape((samples, width), BF16), shape((labels, width), BF16)],
        [grads[g] for g in range(chips)] + [got[d] for d in range(owners)],
        scalars=[me_s],
        after=[moved[g] for g in far + near],
        scratch=[pltpu.VMEM((labels, width), BF16)],
        vmem=12,
        flops=2 * samples * width * labels,
        nbytes=5_000_000,
    )
    tile = min(256, samples)

    def grad_enc_after(value):
        return pl.pallas_call(
            enc_kernel,
            grid=(samples // tile,),
            out_shape=[shape((samples, width), F32), shape((8, 128), F32)],
            in_specs=[
                pl.BlockSpec((tile, width), lambda i: (i, 0)),
                pl.BlockSpec((width, width), lambda i: (0, 0)),
                ANY,
            ],
            out_specs=[
                pl.BlockSpec((tile, width), lambda i: (i, 0)),
                pl.BlockSpec((8, 128), lambda i: (0, 0)),
            ],
            compiler_params=pltpu.CompilerParams(vmem_limit_bytes=12 * MIB),
            cost_estimate=pl.CostEstimate(
                flops=2 * samples * width * width, bytes_accessed=6_000_000, transcendentals=0
            ),
        )(grad_hidden, proj, value)

    grad_enc, enc_done = grad_enc_after(own)
    if row_blocks > 1:
        cut = size // 2
        total, upper = call(
            combine_kernel,
            [shape((cut, width), F32), shape((cut, width), BF16)],
            [own] + received,
            after=[enc_done],
            nbytes=2_000_000,
        )
        span = row_blocks // 2
        total = total + swap(upper, "dp", span).astype(F32)
        while span > 1:
            cut = span // 2 * depth
            total = total[:cut] + swap(total[cut:].astype(BF16), "dp", span // 2).astype(F32)
            span //= 2
    else:
        total = own
        for value in received:
            total = total + value.astype(F32)
    total = total.astype(BF16)
    if planes > 1:
        other = swap(total, "dp", planes // 2)
        total = (total.astype(F32) + other.astype(F32)).astype(BF16)
    parts = {0: total}
    span = 1
    while span < row_blocks:
        for r in range(span):
            parts[r + span] = swap(parts[r], "dp", span)
        span *= 2
    proj_slice = lax.dynamic_slice_in_dim(proj, z * (width // planes), width // planes, 1)
    (whole,) = call(
        whole_kernel,
        [shape((width, size), BF16)],
        [parts[r] for r in range(row_blocks)],
        scalars=[z_s],
        scratch=[pltpu.VMEM((size, width), BF16)],
        vmem=4,
    )
    rows, grad_head = pl.pallas_call(
        head_kernel,
        out_shape=[shape((labels, width), BF16), shape((width // planes, size), F32)],
        in_specs=[ANY, VMEM, VMEM],
        out_specs=[VMEM, VMEM],
        scratch_shapes=[pltpu.SemaphoreType.DMA],
        compiler_params=pltpu.CompilerParams(vmem_limit_bytes=4 * MIB),
        cost_estimate=pl.CostEstimate(
            flops=2 * size * width * width // planes, bytes_accessed=3_000_000, transcendentals=0
        ),
    )(rows, whole, proj_slice)
    have = {0: whole}
    for g in near + far:
        have[2 * g] = gate(swap(whole, "label", 2 * g), rows)
    for distance in list(have):
        have[distance + 1] = swap(have[distance], "label", 1)
    cuts = max(1, width // 256)
    grad_proj = pl.pallas_call(
        functools.partial(proj_kernel, cuts),
        out_shape=shape((width, width), F32),
        in_specs=[SMEM] + [VMEM] * (owners + 1),
        out_specs=ANY,
        scratch_shapes=[
            pltpu.VMEM((width, labels), BF16),
            pltpu.VMEM((width, width), F32),
            pltpu.SemaphoreType.DMA((cuts,)),
        ],
        compiler_params=pltpu.CompilerParams(vmem_limit_bytes=16 * MIB),
        cost_estimate=pl.CostEstimate(
            flops=2 * labels * width * width, bytes_accessed=6_000_000, transcendentals=0
        ),
    )(me_s, *[have[distance] for distance in range(owners)], rows)
    return (grad_enc, grad_proj, grad_head.T)


def solution(mesh):
    placed = (
        P(("dp", "label"), None),
        P(),
        P("label", None),
        P(("dp", "label"), None),
        P(("dp", "label"), None),
        P("label"),
        P("label"),
    )
    return jax.shard_map(
        shards,
        mesh=mesh,
        in_specs=placed,
        out_specs=(P(("dp", "label"), None), P(), P("label", "dp")),
        check_vma=False,
    )
```

```python
import functools

import jax
import jax.numpy as jnp
from jax import lax
from jax.experimental import pallas as pl
from jax.experimental.pallas import tpu as pltpu
from jax.sharding import PartitionSpec as P

BF16 = jnp.bfloat16
F32 = jnp.float32
VMEM = pl.BlockSpec(memory_space=pltpu.VMEM)
SMEM = pl.BlockSpec(memory_space=pltpu.SMEM)
ANY = pl.BlockSpec(memory_space=pl.ANY)
MIB = 1024 * 1024
TAIL = 16
NN = (((1,), (0,)), ((), ()))
NT = (((1,), (1,)), ((), ()))
TN = (((0,), (0,)), ((), ()))


def dot(left, right, dims):
    return lax.dot_general(left, right, dims, preferred_element_type=F32)


def shape(dims, dtype):
    return jax.ShapeDtypeStruct(dims, dtype)


def call(kernel, outs, args, scalars=(), after=(), scratch=(), vmem=8, flops=0, nbytes=0):
    return pl.pallas_call(
        kernel,
        out_shape=outs,
        in_specs=[SMEM] * len(scalars) + [VMEM] * len(args) + [ANY] * len(after),
        out_specs=[VMEM] * len(outs),
        scratch_shapes=list(scratch),
        compiler_params=pltpu.CompilerParams(vmem_limit_bytes=vmem * MIB),
        cost_estimate=pl.CostEstimate(flops=flops, bytes_accessed=nbytes, transcendentals=0),
    )(*scalars, *args, *after)


def gate(value, *after):
    return pl.pallas_call(
        lambda value_ref, *refs: None,
        out_shape=shape(value.shape, value.dtype),
        in_specs=[ANY] * (1 + len(after)),
        out_specs=ANY,
        input_output_aliases={0: 0},
        compiler_params=pltpu.CompilerParams(vmem_limit_bytes=MIB),
    )(value, *after)


def swap(value, axis, distance):
    size = lax.axis_size(axis)
    return lax.ppermute(value, axis, [(i, i ^ distance) for i in range(size)])


def payload_kernel(num_hbm, den_hbm, rows_hbm, out_ref, num_ref, den_ref, sems):
    size, width = rows_hbm.shape
    copies = [
        pltpu.make_async_copy(num_hbm, num_ref, sems.at[0]),
        pltpu.make_async_copy(den_hbm, den_ref, sems.at[1]),
        pltpu.make_async_copy(rows_hbm, out_ref.at[pl.ds(0, size), :], sems.at[2]),
    ]
    for copy in copies:
        copy.start()
    out_ref[size:, size:] = jnp.zeros((TAIL, width - size), BF16)
    copies[0].wait()
    copies[1].wait()
    row = lax.broadcasted_iota(jnp.int32, (TAIL, size), 0)
    both = jnp.where(row == 0, num_ref[...], den_ref[...])
    out_ref[size:, :size] = both.astype(F32).astype(BF16)
    copies[2].wait()


def target_kernel(beam, block, wanted_ref, target_ref):
    samples = wanted_ref.shape[1]
    size = target_ref.shape[0] // beam
    label_iota = lax.broadcasted_iota(jnp.int32, (size, block), 0)
    for low in range(0, samples, block):
        for place in range(beam):
            labels = label_iota + place * size
            target = labels == wanted_ref[0:1, low : low + block]
            for column in range(1, wanted_ref.shape[0]):
                target = target | (labels == wanted_ref[column : column + 1, low : low + block])
            target_ref[place * size : (place + 1) * size, low : low + block] = jnp.where(
                target, 1.0, 0.0
            ).astype(BF16)


def inputs_kernel(enc_ref, proj_ref, *refs):
    hidden_t_ref = refs[-1]
    samples = enc_ref.shape[0]
    tile = min(256, samples)
    for start in range(0, samples, tile):
        hidden = dot(enc_ref[start : start + tile, :], proj_ref[...], NN).astype(BF16)
        hidden_t_ref[:, start : start + tile] = hidden.T


def logistic(value):
    bottom = 1.0 + jnp.exp(-jnp.maximum(value, -80.0))
    guess = pl.reciprocal(bottom, approx=True)
    return guess * (2.0 - bottom * guess)


def score_kernel(group, block, count, halves, list_ref, me_ref, z_ref, hidden_t_ref, enc_ref, *refs):
    targets, payloads, refs = refs[:halves], refs[halves : halves + 2], refs[-6:]
    grads_ref, kept_ref, sent_ref, weights_ref, scale_ref, logits_ref = refs
    samples = enc_ref.shape[0]
    size = payloads[0].shape[0] - TAIL
    for core in range(2):
        rows = pl.ds(core * size, size)
        weights_ref[rows, :] = payloads[core][:size, :]
        tail = payloads[core][size:, :size].astype(F32)
        ratio = tail[0:1, :] / tail[1:2, :]
        scale_ref[rows, :] = jnp.broadcast_to(ratio, (block, size)).T
    tile = min(2 * block, samples)
    for start in range(0, samples, tile):
        logits_ref[:, start : start + tile] = dot(
            weights_ref[...], hidden_t_ref[:, start : start + tile], NN
        )
        for low in range(start, start + tile, block):
            for core in range(2):
                cluster = me_ref[0] ^ (2 * group + core)
                place = jnp.int32(-1)
                for beam_slot in range(list_ref.shape[0]):
                    place = jnp.where(list_ref[beam_slot, low // block] == cluster, beam_slot, place)
                factor = jnp.where(place >= 0, 1.0 / block, 0.0)
                first = pl.multiple_of(jnp.maximum(place, 0) * size, size)
                rows = slice(core * size, (core + 1) * size)
                half, column = divmod(low, samples // halves)
                target = targets[half][pl.ds(first, size), column : column + block].astype(F32)
                share = logistic(logits_ref[rows, low : low + block]) - target
                grads_ref[rows, low : low + block] = (scale_ref[rows, :] * factor * share).astype(BF16)
    outer = dot(grads_ref[...], enc_ref[...], NN)
    depth = size // count
    for r in range(count):
        rows = pl.ds(pl.multiple_of((z_ref[0] ^ r) * depth, depth), depth)
        kept_ref[rows, :] = outer[r * depth : (r + 1) * depth, :]
        sent_ref[rows, :] = outer[size + r * depth : size + (r + 1) * depth, :].astype(BF16)


def hidden_kernel(owners, me_ref, *refs):
    chips = owners // 2
    grads, payloads, refs = refs[:chips], refs[chips : chips + owners], refs[chips + owners :]
    out_ref, rows_ref, weights_ref = refs[-3:]
    size = payloads[0].shape[0] - TAIL
    for slot in range(owners):
        piece = payloads[slot][:size, :]
        start = pl.multiple_of((me_ref[0] ^ slot) * size, size)
        rows_ref[pl.ds(start, size), :] = piece
        weights_ref[slot * size : (slot + 1) * size, :] = piece
    samples = out_ref.shape[0]
    tile = min(256, samples)
    for low in range(0, samples, tile):
        total = jnp.zeros((tile, out_ref.shape[1]), F32)
        for group in range(chips):
            rows = weights_ref[2 * group * size : 2 * (group + 1) * size, :]
            total = total + dot(grads[group][:, low : low + tile], rows, TN)
        out_ref[low : low + tile, :] = total.astype(BF16)


def enc_kernel(grad_hidden_ref, proj_ref, after_ref, out_ref, done_ref):
    out_ref[...] = dot(grad_hidden_ref[...], proj_ref[...], NT)
    done_ref[...] = jnp.zeros_like(done_ref)


def combine_kernel(own_ref, *refs):
    *received, after_ref, kept_ref, sent_ref = refs
    cut = kept_ref.shape[0]
    for rows, out_ref in ((slice(cut, None), sent_ref), (slice(0, cut), kept_ref)):
        total = own_ref[rows, :]
        for ref in received:
            total = total + ref[rows, :].astype(F32)
        out_ref[...] = total.astype(out_ref.dtype)


def whole_kernel(z_ref, *refs):
    *parts, whole_ref, rows_ref = refs
    depth = parts[0].shape[0]
    for r, part in enumerate(parts):
        rows_ref[pl.ds(pl.multiple_of((z_ref[0] ^ r) * depth, depth), depth), :] = part[...]
    whole_ref[...] = rows_ref[...].T


def head_kernel(rows_any, whole_ref, slice_ref, rows_ref, head_ref, sem):
    copy = pltpu.make_async_copy(rows_any, rows_ref, sem)
    copy.start()
    head_ref[...] = dot(slice_ref[...], whole_ref[...], TN)
    copy.wait()


def proj_kernel(cuts, me_ref, *refs):
    *parts, rows_ref, out_hbm, outer_ref, done_ref, sems = refs
    width, size = parts[0].shape
    for distance, part in enumerate(parts):
        start = pl.multiple_of((me_ref[0] ^ distance) * size, size)
        outer_ref[:, pl.ds(start, size)] = part[...]
    height = width // cuts
    copies = []
    for cut in range(cuts):
        rows = pl.ds(cut * height, height)
        done_ref[rows, :] = dot(outer_ref[rows, :], rows_ref[...], NN)
        copy = pltpu.make_async_copy(done_ref.at[rows, :], out_hbm.at[rows, :], sems.at[cut])
        copy.start()
        copies.append(copy)
    for copy in copies:
        copy.wait()


def shards(enc, proj, head_weight, shortlist, positives, weight_num, weight_den):
    owners, planes = lax.axis_size("label"), lax.axis_size("dp")
    chips = owners // 2
    near = [g for g in range(1, chips) if g & (g - 1) == 0]
    far = [g for g in range(1, chips) if g & (g - 1) != 0]
    row_blocks = max(1, planes // 2)
    me = lax.axis_index("label").astype(jnp.int32)
    z = lax.axis_index("dp").astype(jnp.int32)
    z_low = z & (row_blocks - 1)
    blocks, beam = shortlist.shape
    samples, width = enc.shape
    block = samples // blocks
    size = head_weight.shape[0]
    labels = owners * size
    depth = size // row_blocks
    me_s, z_s = me.reshape(1), z_low.reshape(1)
    listed = shortlist.astype(jnp.int32).T

    payload = pl.pallas_call(
        payload_kernel,
        out_shape=shape((size + TAIL, width), BF16),
        in_specs=[ANY] * 3,
        out_specs=VMEM,
        scratch_shapes=[pltpu.VMEM((1, size), jnp.int32)] * 2 + [pltpu.SemaphoreType.DMA((3,))],
        compiler_params=pltpu.CompilerParams(vmem_limit_bytes=56 * MIB),
    )(weight_num.reshape(1, size), weight_den.reshape(1, size), head_weight)
    got = {0: payload}
    for g in far + near:
        got[2 * g] = swap(payload, "label", 2 * g)
    got[1] = swap(payload, "label", 1)
    halves = 2 if blocks % 2 == 0 else 1
    targets = [
        call(
            functools.partial(target_kernel, beam, block),
            [shape((beam * size, samples // halves), BF16)],
            [part],
            vmem=2,
            nbytes=8_000_000 // halves,
        )[0]
        for part in jnp.split(positives.T, halves, axis=1)
    ]
    (hidden_t,) = call(
        inputs_kernel,
        [shape((width, samples), BF16)],
        [enc, proj],
        after=targets,
        flops=2 * samples * width * width,
        nbytes=6_000_000,
    )
    grads, kept, from_core, moved, received = {}, {}, {}, {}, {}
    order = [0] + far + near
    for at, g in enumerate(order):
        after = [grads[order[at - 1]]] if at else []
        if at == 1:
            after.extend(got[2 * ahead] for ahead in order[2:])
        if at >= 3:
            after.append(moved[order[at - 2]])
        grads[g], kept[g], sent = call(
            functools.partial(score_kernel, g, block, row_blocks, halves),
            [shape((2 * size, samples), BF16), shape((size, width), F32), shape((size, width), BF16)],
            [hidden_t, enc, *targets, got[2 * g], got[2 * g + 1]],
            scalars=[listed, me_s, z_s],
            after=after,
            scratch=[
                pltpu.VMEM((2 * size, width), BF16),
                pltpu.VMEM((2 * size, block), F32),
                pltpu.VMEM((2 * size, samples), F32),
            ],
            flops=8 * samples * size * width,
            nbytes=5_000_000,
        )
        for ahead in order[1:] if at == 0 else []:
            got[2 * ahead] = gate(got[2 * ahead], grads[g])
            got[2 * ahead + 1] = swap(got[2 * ahead], "label", 1)
        from_core[g] = swap(sent, "label", 1)
        if g:
            moved[g] = (kept[g] + from_core[g].astype(F32)).astype(BF16)
            received[g] = swap(moved[g], "label", 2 * g)
    own = kept[0] + from_core[0].astype(F32)
    received = [received[g] for g in far + near]

    grad_hidden, rows = call(
        functools.partial(hidden_kernel, owners),
        [shape((samples, width), BF16), shape((labels, width), BF16)],
        [grads[g] for g in range(chips)] + [got[d] for d in range(owners)],
        scalars=[me_s],
        after=[moved[g] for g in far + near],
        scratch=[pltpu.VMEM((labels, width), BF16)],
        vmem=12,
        flops=2 * samples * width * labels,
        nbytes=5_000_000,
    )
    tile = min(256, samples)

    def grad_enc_after(value):
        return pl.pallas_call(
            enc_kernel,
            grid=(samples // tile,),
            out_shape=[shape((samples, width), F32), shape((8, 128), F32)],
            in_specs=[
                pl.BlockSpec((tile, width), lambda i: (i, 0)),
                pl.BlockSpec((width, width), lambda i: (0, 0)),
                ANY,
            ],
            out_specs=[
                pl.BlockSpec((tile, width), lambda i: (i, 0)),
                pl.BlockSpec((8, 128), lambda i: (0, 0)),
            ],
            compiler_params=pltpu.CompilerParams(vmem_limit_bytes=12 * MIB),
            cost_estimate=pl.CostEstimate(
                flops=2 * samples * width * width, bytes_accessed=6_000_000, transcendentals=0
            ),
        )(grad_hidden, proj, value)

    grad_enc, enc_done = grad_enc_after(own)
    if row_blocks > 1:
        cut = size // 2
        total, upper = call(
            combine_kernel,
            [shape((cut, width), F32), shape((cut, width), BF16)],
            [own] + received,
            after=[enc_done],
            nbytes=2_000_000,
        )
        span = row_blocks // 2
        total = total + swap(upper, "dp", span).astype(F32)
        while span > 1:
            cut = span // 2 * depth
            total = total[:cut] + swap(total[cut:].astype(BF16), "dp", span // 2).astype(F32)
            span //= 2
    else:
        total = own
        for value in received:
            total = total + value.astype(F32)
    total = total.astype(BF16)
    if planes > 1:
        other = swap(total, "dp", planes // 2)
        total = (total.astype(F32) + other.astype(F32)).astype(BF16)
    parts = {0: total}
    span = 1
    while span < row_blocks:
        for r in range(span):
            parts[r + span] = swap(parts[r], "dp", span)
        span *= 2
    proj_slice = lax.dynamic_slice_in_dim(proj, z * (width // planes), width // planes, 1)
    (whole,) = call(
        whole_kernel,
        [shape((width, size), BF16)],
        [parts[r] for r in range(row_blocks)],
        scalars=[z_s],
        scratch=[pltpu.VMEM((size, width), BF16)],
        vmem=4,
    )
    rows, grad_head = pl.pallas_call(
        head_kernel,
        out_shape=[shape((labels, width), BF16), shape((width // planes, size), F32)],
        in_specs=[ANY, VMEM, VMEM],
        out_specs=[VMEM, VMEM],
        scratch_shapes=[pltpu.SemaphoreType.DMA],
        compiler_params=pltpu.CompilerParams(vmem_limit_bytes=4 * MIB),
        cost_estimate=pl.CostEstimate(
            flops=2 * size * width * width // planes, bytes_accessed=3_000_000, transcendentals=0
        ),
    )(rows, whole, proj_slice)
    have = {0: whole}
    for g in near + far:
        have[2 * g] = gate(swap(whole, "label", 2 * g), rows)
    for distance in list(have):
        have[distance + 1] = swap(have[distance], "label", 1)
    cuts = max(1, width // 256)
    grad_proj = pl.pallas_call(
        functools.partial(proj_kernel, cuts),
        out_shape=shape((width, width), F32),
        in_specs=[SMEM] + [VMEM] * (owners + 1),
        out_specs=ANY,
        scratch_shapes=[
            pltpu.VMEM((width, labels), BF16),
            pltpu.VMEM((width, width), F32),
            pltpu.SemaphoreType.DMA((cuts,)),
        ],
        compiler_params=pltpu.CompilerParams(vmem_limit_bytes=16 * MIB),
        cost_estimate=pl.CostEstimate(
            flops=2 * labels * width * width, bytes_accessed=6_000_000, transcendentals=0
        ),
    )(me_s, *[have[distance] for distance in range(owners)], rows)
    return (grad_enc, grad_proj, grad_head.T)


def solution(mesh):
    placed = (
        P(("dp", "label"), None),
        P(),
        P("label", None),
        P(("dp", "label"), None),
        P(("dp", "label"), None),
        P("label"),
        P("label"),
    )
    return jax.shard_map(
        shards,
        mesh=mesh,
        in_specs=placed,
        out_specs=(P(("dp", "label"), None), P(), P("label", "dp")),
        check_vma=False,
    )
```
